32 devices in a mesh: shard: 4 (over z), context: 4 (over y, core), tensor: 2 (over x).
Axes of the slice: x: 2, y: 2, z: 4, core: 2. Of those that a mesh axis runs over, the one named last changes fastest.
Arguments:
- tokens: bfloat16 [4, 2048, 2048], P('shard', 'context'), may hold values from -6 to 6
- layer_input: bfloat16 [4, 2048, 256], P('shard', 'context'), may hold values from -6 to 6
- segments: int32 [4, 2048], P('shard'), may hold values from 0 to 65, as said below
- adapter_ids: int32 [4], P('shard'), may hold values from 0 to 7
- cotangent: bfloat16 [4, 2048, 2048], P('shard', 'context'), may hold values from -6 to 6
- w_query: bfloat16 [2048, 2048], P('shard', 'tensor'), may hold values from -0.125 to 0.125
- w_key: bfloat16 [2048, 512], P('shard', 'tensor'), may hold values from -0.125 to 0.125
- w_value: bfloat16 [2048, 512], P('shard', 'tensor'), may hold values from -0.125 to 0.125
- w_output: bfloat16 [2048, 2048], P('tensor', 'shard'), may hold values from -0.125 to 0.125
- w_gate: bfloat16 [2048, 8192], P('shard', 'tensor'), may hold values from -0.125 to 0.125
- w_up: bfloat16 [2048, 8192], P('shard', 'tensor'), may hold values from -0.125 to 0.125
- w_down: bfloat16 [8192, 2048], P('tensor', 'shard'), may hold values from -0.0625 to 0.0625
- laurel_left: bfloat16 [2048, 64], P('shard'), may hold values from -0.125 to 0.125
- laurel_right: bfloat16 [64, 2048], P(None, 'shard'), may hold values from -0.75 to 0.75
- input_gate: bfloat16 [2048, 256], P('shard'), may hold values from -0.125 to 0.125
- input_proj: bfloat16 [256, 2048], P(None, 'shard'), may hold values from -0.375 to 0.375
- gain_in: float32 [2048], replicated, may hold values from 0.25 to 1.75
- gain_attn: float32 [2048], replicated, may hold values from 0.25 to 1.75
- gain_laurel: float32 [2048], replicated, may hold values from 0.25 to 1.75
- gain_pre: float32 [2048], replicated, may hold values from 0.25 to 1.75
- gain_post: float32 [2048], replicated, may hold values from 0.25 to 1.75
- gain_layer: float32 [2048], replicated, may hold values from 0.25 to 1.75
- gain_query: float32 [256], replicated, may hold values from 0.25 to 1.75
- gain_key: float32 [256], replicated, may hold values from 0.25 to 1.75
- adapt_attn_in: bfloat16 [8, 2048, 48], replicated, may hold values from -0.125 to 0.125
- adapt_query_out: bfloat16 [8, 16, 2048], P(None, None, 'tensor'), may hold values from -0.59765625 to 0.59765625
- adapt_kv_out: bfloat16 [8, 2, 16, 512], P(None, None, None, 'tensor'), may hold values from -0.59765625 to 0.59765625
- adapt_out_in: bfloat16 [8, 2048, 16], P(None, 'tensor'), may hold values from -0.125 to 0.125
- adapt_out_out: bfloat16 [8, 16, 2048], replicated, may hold values from -0.59765625 to 0.59765625
- adapt_ffn_in: bfloat16 [8, 2048, 32], replicated, may hold values from -0.125 to 0.125
- adapt_gu_out: bfloat16 [8, 2, 16, 8192], P(None, None, None, 'tensor'), may hold values from -0.59765625 to 0.59765625
- adapt_down_in: bfloat16 [8, 8192, 16], P(None, 'tensor'), may hold values from -0.0625 to 0.0625
- adapt_down_out: bfloat16 [8, 16, 2048], replicated, may hold values from -0.59765625 to 0.59765625
Outputs:
- layer_output: bfloat16 [4, 2048, 2048], P('shard', 'context')
- input_grad: bfloat16 [4, 2048, 2048], P('shard', 'context')
- grad_attn_in: float32 [8, 2048, 48], replicated
- grad_query_out: float32 [8, 16, 2048], replicated
- grad_kv_out: float32 [8, 2, 16, 512], replicated
- grad_out_in: float32 [8, 2048, 16], replicated
- grad_out_out: float32 [8, 16, 2048], replicated
- grad_ffn_in: float32 [8, 2048, 32], replicated
- grad_gu_out: float32 [8, 2, 16, 8192], replicated
- grad_down_in: float32 [8, 8192, 16], replicated
- grad_down_out: float32 [8, 16, 2048], replicated
The draws below stay inside these ranges and needn't reach their ends.
Inputs may be any that keep to these rules, and one draw needn't show every extreme that they name: `segments`: segment numbers start at 0 in every sequence and never fall from one position to the next; each number marks one document; every sequence holds 66 documents.
All inputs are finite; a program needn't handle non-finite values.
Results may differ from the reference program's by a relative error of at most 0.019.
Values may be sent and summed in bfloat16 or wider, within the bound.
A program may use at most 320 MiB of HBM per device.

```python
import math
import jax
import jax.numpy as jnp
from jax import lax

D = 2048
H = 8
KV = 2
HD = 256
FF = 8192
LR = 64
PL = 256
WINDOW = 512
NA = 8
R = 16
LOC = 512
SEQ_LEN = 2048
SEQS = 4


def draw_segments(key, part):
    key = jax.random.fold_in(key, 11)
    extra_cuts = LOC // 8 - 1

    def one_row(row_key):
        row_keys = jax.random.split(row_key, 3)
        counter = jnp.arange(SEQ_LEN, dtype=jnp.int32)
        opening = jax.random.randint(row_keys[0], (), 1, LOC // 2 + 1)
        closing = SEQ_LEN - LOC + jax.random.randint(row_keys[1], (), LOC // 2, 3 * LOC // 4)
        inside = (counter >= opening) & (counter <= closing)
        usable = jnp.logical_not(inside) & (counter > 0)
        raw_score = jax.random.randint(row_keys[2], (SEQ_LEN,), 0, 1024) * SEQ_LEN + counter
        score = jnp.where(usable, raw_score, -1)
        chosen_score, chosen_place = lax.top_k(score, extra_cuts)
        picked = jnp.any(counter[:, None] == chosen_place[None, :].astype(jnp.int32), axis=1)
        cuts = picked | (counter == opening) | (counter == closing)
        return jnp.cumsum(cuts.astype(jnp.int32)).astype(jnp.int32)
    return jax.vmap(one_row)(jax.random.split(key, SEQS))


def place_ends(drawn, rng, smallest, largest):
    longest = drawn.shape.index(max(drawn.shape))
    spots = []
    for shift in (0, 1):
        where = [jax.random.randint(jax.random.fold_in(rng, axis), (), 0, length) for axis, length in enumerate(drawn.shape)]
        where[longest] = (where[longest] + shift) % drawn.shape[longest]
        spots.append(tuple(where))
    return drawn.at[spots[0]].set(smallest).at[spots[1]].set(largest)


def levels(key, extent, shards, least, top_value):
    def one(dim, parts):
        heights = jax.random.uniform(jax.random.fold_in(jax.random.fold_in(key, 6), dim), (parts,), jnp.float32, least / len(shards), top_value / len(shards))
        return jnp.repeat(jnp.exp(heights), extent[dim] // parts).reshape((-1,) + (1,) * (len(extent) - dim - 1))

    gain = one(*shards[0])
    for cut in shards[1:]:
        gain = gain * one(*cut)
    return gain


def normal_values(key, extent, deviation, limit, cuts=(), kind=jnp.bfloat16):
    entries = jax.random.normal(key, extent, jnp.float32) * deviation
    if len(cuts) > 0:
        entries = levels(key, extent, cuts, -0.22, 0.18) * entries
    return jnp.clip(entries, min=-limit, max=limit).astype(kind)


def setup_inputs(seed: int = 0) -> dict:
    keys = jax.random.split(jax.random.key(seed), 34)
    return {
        "tokens": normal_values(keys[0], (SEQS, SEQ_LEN, D), 1.0, 6.0, ((0, 4), (1, 4))),
        "layer_input": normal_values(keys[1], (SEQS, SEQ_LEN, PL), 1.0, 6.0, ((0, 4), (1, 4))),
        "segments": draw_segments(jax.random.fold_in(keys[33], 71), 0),
        "adapter_ids": place_ends(jax.random.randint(keys[3], (SEQS,), 0, NA), jax.random.fold_in(keys[3], 1), 0, NA - 1).astype(jnp.int32),
        "cotangent": normal_values(keys[4], (SEQS, SEQ_LEN, D), 1.0, 6.0, ((0, 4), (1, 4))),
        "w_query": normal_values(keys[5], (D, H * HD), D ** -0.5, 0.125, ((0, 4), (1, 2))),
        "w_key": normal_values(keys[6], (D, KV * HD), D ** -0.5, 0.125, ((0, 4), (1, 2))),
        "w_value": normal_values(keys[7], (D, KV * HD), D ** -0.5, 0.125, ((0, 4), (1, 2))),
        "w_output": normal_values(keys[8], (H * HD, D), (H * HD) ** -0.5, 0.125, ((0, 2), (1, 4))),
        "w_gate": normal_values(keys[9], (D, FF), D ** -0.5, 0.125, ((0, 4), (1, 2))),
        "w_up": normal_values(keys[10], (D, FF), D ** -0.5, 0.125, ((0, 4), (1, 2))),
        "w_down": normal_values(keys[11], (FF, D), FF ** -0.5, 0.0625, ((0, 2), (1, 4))),
        "laurel_left": normal_values(keys[12], (D, LR), D ** -0.5, 0.125, ((0, 4),)),
        "laurel_right": normal_values(keys[13], (LR, D), LR ** -0.5, 0.75, ((1, 4),)),
        "input_gate": normal_values(keys[14], (D, PL), D ** -0.5, 0.125, ((0, 4),)),
        "input_proj": normal_values(keys[15], (PL, D), PL ** -0.5, 0.375, ((1, 4),)),
        "gain_in": jnp.clip(1.0 + 0.15 * jax.random.normal(keys[16], (D,), jnp.float32), 0.25, 1.75),
        "gain_attn": jnp.clip(1.0 + 0.15 * jax.random.normal(keys[17], (D,), jnp.float32), 0.25, 1.75),
        "gain_laurel": jnp.clip(1.0 + 0.15 * jax.random.normal(keys[18], (D,), jnp.float32), 0.25, 1.75),
        "gain_pre": jnp.clip(1.0 + 0.15 * jax.random.normal(keys[19], (D,), jnp.float32), 0.25, 1.75),
        "gain_post": jnp.clip(1.0 + 0.15 * jax.random.normal(keys[20], (D,), jnp.float32), 0.25, 1.75),
        "gain_layer": jnp.clip(1.0 + 0.15 * jax.random.normal(keys[21], (D,), jnp.float32), 0.25, 1.75),
        "gain_query": jnp.clip(1.0 + 0.15 * jax.random.normal(keys[22], (HD,), jnp.float32), 0.25, 1.75),
        "gain_key": jnp.clip(1.0 + 0.15 * jax.random.normal(keys[23], (HD,), jnp.float32), 0.25, 1.75),
        "adapt_attn_in": normal_values(keys[24], (NA, D, 3 * R), D ** -0.5, 0.125),
        "adapt_query_out": normal_values(keys[25], (NA, R, H * HD), 0.1, 0.59765625, ((2, 2),)),
        "adapt_kv_out": normal_values(keys[26], (NA, 2, R, KV * HD), 0.1, 0.59765625, ((3, 2),)),
        "adapt_out_in": normal_values(keys[27], (NA, H * HD, R), (H * HD) ** -0.5, 0.125, ((1, 2),)),
        "adapt_out_out": normal_values(keys[28], (NA, R, D), 0.1, 0.59765625),
        "adapt_ffn_in": normal_values(keys[29], (NA, D, 2 * R), D ** -0.5, 0.125),
        "adapt_gu_out": normal_values(keys[30], (NA, 2, R, FF), 0.1, 0.59765625, ((3, 2),)),
        "adapt_down_in": normal_values(keys[31], (NA, FF, R), FF ** -0.5, 0.0625, ((1, 2),)),
        "adapt_down_out": normal_values(keys[32], (NA, R, D), 0.1, 0.59765625),
    }


EPSILON = 1e-06
HIGHEST = lax.Precision.HIGHEST
ROOT_HALF = 0.7071067811865476

@jax.custom_vjp
def low(v):
    return lax.optimization_barrier(v.astype(jnp.bfloat16)).astype(jnp.float32)

@jax.custom_vjp
def low_back(v):
    return v

def low_keep(v):
    return (low(v), None)

def low_pass(kept, grad):
    return (grad,)

def back_keep(v):
    return (v, None)

def back_low(kept, grad):
    return (low(grad),)
low.defvjp(low_keep, low_pass)
low_back.defvjp(back_keep, back_low)

def rms_norm(values, scaling):
    return values * lax.rsqrt(lax.optimization_barrier(jnp.mean(values * values, axis=-1, keepdims=True)) + EPSILON) * scaling

def gelu_tanh(values):
    return jax.nn.gelu(values, approximate=True)

def matmul_high(left_op, right_op):
    return jnp.dot(left_op, right_op, precision=HIGHEST, preferred_element_type=jnp.float32)

def rotate_half(values, cosine, sine_table):
    middle = values.shape[-1] // 2
    former = values[..., :middle]
    latter = values[..., middle:]
    return jnp.concatenate([former * cosine - latter * sine_table, latter * cosine + former * sine_table], axis=-1)

def doc_positions(segment_ids):
    counter = jnp.broadcast_to(jnp.arange(segment_ids.shape[-1], dtype=jnp.int32), segment_ids.shape)
    boundary = jnp.concatenate([jnp.ones(segment_ids.shape[:-1] + (1,), dtype=jnp.bool_), segment_ids[..., 1:] != segment_ids[..., :-1]], axis=-1)
    starts = lax.cummax(jnp.where(boundary, counter, 0), axis=segment_ids.ndim - 1)
    return counter - starts

def rope_tables(positions, head_size):
    frequency = jnp.exp(jnp.arange(head_size // 2, dtype=jnp.float32) * (-2.0 * math.log(10000.0) / head_size))
    angles = positions.astype(jnp.float32)[..., None] * frequency
    return (jnp.cos(angles), jnp.sin(angles))

def layer(inputs, per_layer, segment_ids, chosen, frozen, gain_set):
    attn_in, query_out, kv_out, out_in, out_out, ffn_in, gu_out, down_in, down_out = chosen
    w_query, w_key, w_value, w_output, w_gate, w_up, w_down, laurel_left, laurel_right, input_gate, input_proj = frozen
    gain_in, gain_attn, gain_laurel, gain_pre, gain_post, gain_layer, gain_query, gain_key = gain_set
    seq_len = inputs.shape[0]
    normed = rms_norm(inputs, gain_in)
    normed_r = low(normed)
    code_attn = matmul_high(normed_r, attn_in)
    query_lin = low_back(matmul_high(normed_r, w_query) + matmul_high(code_attn[:, :R], query_out))
    key_lin = low_back(matmul_high(normed_r, w_key) + matmul_high(code_attn[:, R:2 * R], kv_out[0]))
    value_lin = low_back(matmul_high(normed_r, w_value) + matmul_high(code_attn[:, 2 * R:], kv_out[1]))
    cosine, sine_table = rope_tables(doc_positions(segment_ids), HD)
    cosine = cosine[:, None, :]
    sine_table = sine_table[:, None, :]
    queries = low(rotate_half(rms_norm(query_lin.reshape(seq_len, H, HD), gain_query), cosine, sine_table))
    keys_rot = low(rotate_half(rms_norm(key_lin.reshape(seq_len, KV, HD), gain_key), cosine, sine_table))
    values_nrm = low(rms_norm(value_lin.reshape(seq_len, KV, HD), 1.0))
    queries = queries.reshape(seq_len, KV, H // KV, HD)
    score_scale = 1.0 / math.sqrt(HD)
    scores = low_back(jnp.einsum('tkgd,skd->kgts', queries, keys_rot, precision=HIGHEST) * score_scale)
    place_ids = jnp.arange(seq_len, dtype=jnp.int32)
    distance = place_ids[:, None] - place_ids[None, :]
    allowed = (segment_ids[:, None] == segment_ids[None, :]) & (distance >= 0) & (distance < WINDOW)
    scores = jnp.where(allowed, scores, -1e+30)
    row_max = lax.optimization_barrier(jnp.max(scores, axis=-1, keepdims=True))
    exponent = jnp.exp(scores - row_max)
    attn_probs = exponent / lax.optimization_barrier(jnp.sum(exponent, axis=-1, keepdims=True))
    attended = jnp.einsum('kgts,skd->tkgd', low(attn_probs), values_nrm, precision=HIGHEST).reshape(seq_len, H * HD)
    attended = low_back(low(attended))
    code_out = matmul_high(attended, out_in)
    attn_proj = low_back(matmul_high(attended, w_output) + matmul_high(code_out, out_out))
    laurel_mid = low_back(low(matmul_high(normed_r, laurel_left)))
    laurel_end = low_back(matmul_high(laurel_mid, laurel_right))
    combined = (inputs + rms_norm(attn_proj, gain_attn) + normed + rms_norm(laurel_end, gain_laurel)) * ROOT_HALF
    ffn_input = low(rms_norm(combined, gain_pre))
    code_ffn = matmul_high(ffn_input, ffn_in)
    gate_lin = low_back(matmul_high(ffn_input, w_gate) + matmul_high(code_ffn[:, :R], gu_out[0]))
    up_lin = low_back(matmul_high(ffn_input, w_up) + matmul_high(code_ffn[:, R:], gu_out[1]))
    hidden_act = low(gelu_tanh(gate_lin) * up_lin)
    code_down = matmul_high(hidden_act, down_in)
    down_proj = low_back(matmul_high(hidden_act, w_down) + matmul_high(code_down, down_out))
    after_ffn = combined + rms_norm(down_proj, gain_post)
    layer_gate = low_back(matmul_high(low(after_ffn), input_gate))
    layer_mix = low(gelu_tanh(layer_gate) * per_layer)
    layer_proj = low_back(matmul_high(layer_mix, input_proj))
    return after_ffn + rms_norm(layer_proj, gain_layer)

def reference(tokens, layer_input, segments, adapter_ids, cotangent, w_query, w_key, w_value, w_output, w_gate, w_up, w_down, laurel_left, laurel_right, input_gate, input_proj, gain_in, gain_attn, gain_laurel, gain_pre, gain_post, gain_layer, gain_query, gain_key, adapt_attn_in, adapt_query_out, adapt_kv_out, adapt_out_in, adapt_out_out, adapt_ffn_in, adapt_gu_out, adapt_down_in, adapt_down_out):
    frozen = tuple((weight.astype(jnp.float32) for weight in (w_query, w_key, w_value, w_output, w_gate, w_up, w_down, laurel_left, laurel_right, input_gate, input_proj)))
    gain_set = (gain_in, gain_attn, gain_laurel, gain_pre, gain_post, gain_layer, gain_query, gain_key)
    tables = tuple((adapter.astype(jnp.float32) for adapter in (adapt_attn_in, adapt_query_out, adapt_kv_out, adapt_out_in, adapt_out_out, adapt_ffn_in, adapt_gu_out, adapt_down_in, adapt_down_out)))

    def one_sequence(totals, step_item):
        inputs, per_layer, segment_ids, chosen_id, upstream = step_item
        chosen = tuple((adapter_table[chosen_id] for adapter_table in tables))

        def forward(inputs_in, chosen_in):
            return layer(inputs_in, per_layer, segment_ids, chosen_in, frozen, gain_set)
        output, pullback = jax.vjp(forward, inputs, chosen)
        grad_inputs, chosen_grads = pullback(upstream)
        totals = tuple((total_grad.at[chosen_id].add(grad_piece) for total_grad, grad_piece in zip(totals, chosen_grads)))
        return (totals, (output.astype(jnp.bfloat16), grad_inputs.astype(jnp.bfloat16)))
    initial = tuple((jnp.zeros(adapter_table.shape, jnp.float32) for adapter_table in tables))
    totals, (outputs, input_grads) = lax.scan(one_sequence, initial, (tokens.astype(jnp.float32), layer_input.astype(jnp.float32), segments, adapter_ids, cotangent.astype(jnp.float32)))
    return (outputs, input_grads, totals[0], totals[1], totals[2], totals[3], totals[4], totals[5], totals[6], totals[7], totals[8])
```

```python
import functools
import math

import jax
import jax.numpy as jnp
from jax import lax
from jax.experimental import pallas as pl
from jax.experimental.pallas import tpu as pltpu
from jax.sharding import PartitionSpec as P

WINDOW = 512
EPSILON = 1e-06
ROOT_HALF = 0.7071067811865476

MESH = pl.DeviceIdType.MESH


def gather_kernel(plan, count, shards, depth, *refs):
    sources, fulls, held = refs[:count], refs[count : 2 * count], refs[2 * count : 3 * count]
    load_sem, local_sem, z_recv, y_recv, near_recv, far_recv, z_send, y_send, near_send, far_send = refs[3 * count :]
    z, c = lax.axis_index("shard"), lax.axis_index("context")
    across = lax.rem(c + 2, 4)
    beside = c + 1 - 2 * lax.rem(c, 2)

    barrier = pltpu.get_barrier_semaphore()

    def greet(place):
        pl.semaphore_signal(barrier, inc=1, device_id=place, device_id_type=MESH)

    greet({"context": across})
    greet({"context": beside})

    @pl.when(z > 0)
    def _():
        greet({"shard": z - 1})

    @pl.when(z < shards - 1)
    def _():
        greet({"shard": z + 1})

    pl.semaphore_wait(barrier, 2 + lax.div(z + shards - 1, shards) + lax.div(2 * shards - 2 - z, shards))

    def region(piece, s, q):
        item, axis, row, rows, col, cols = plan[piece]
        rows_here, cols_here = sources[item].shape
        part = rows // 4
        if axis == 0:
            first = s * rows_here + row + q * part
            return fulls[item].at[pl.ds(pl.multiple_of(first, 16), part), pl.ds(col, cols)]
        return fulls[item].at[
            pl.ds(pl.multiple_of(row + q * part, 16), part),
            pl.ds(pl.multiple_of(s * cols_here + col, 128), cols),
        ]

    def own(piece, q):
        item, axis, row, rows, col, cols = plan[piece]
        part = rows // 4
        return sources[item].at[pl.ds(pl.multiple_of(row + q * part, 16), part), pl.ds(col, cols)]

    def copy(source, target, send, recv, place):
        return pltpu.make_async_remote_copy(
            src_ref=source, dst_ref=target, send_sem=send, recv_sem=recv, device_id=place, device_id_type=MESH
        )

    def up(piece, s, source, slot):
        return copy(source, region(piece, s, c), z_send.at[piece, slot], z_recv.at[piece, s], {"shard": z + 1})

    def down(piece, s, source, slot):
        return copy(source, region(piece, s, c), z_send.at[piece, slot], z_recv.at[piece, s], {"shard": z - 1})

    def y_copy(piece, s, q):
        return copy(region(piece, s, q), region(piece, s, q), y_send.at[piece, s], y_recv.at[piece, s], {"context": across})

    def near_copy(piece, s, q):
        return copy(region(piece, s, q), region(piece, s, q), near_send.at[piece, s], near_recv.at[piece, s], {"context": beside})

    def far_copy(piece, s, q):
        return copy(region(piece, s, q), region(piece, s, q), far_send.at[piece, s], far_recv.at[piece, s], {"context": beside})

    loads, stores = [], []
    for item in range(count):
        rows_here, cols_here = sources[item].shape
        axis = next(p[1] for p in plan if p[0] == item)
        if axis == 0:
            target = fulls[item].at[pl.ds(pl.multiple_of(z * rows_here, 16), rows_here), :]
        else:
            target = fulls[item].at[:, pl.ds(pl.multiple_of(z * cols_here, 128), cols_here)]
        loads.append(pltpu.make_async_copy(sources[item], held[item], load_sem.at[item]))
        stores.append(pltpu.make_async_copy(held[item], target, local_sem.at[item]))

    def begin(piece):
        @pl.when(z < shards - 1)
        def _():
            up(piece, z, own(piece, c), z).start()

        @pl.when(z > 0)
        def _():
            down(piece, z, own(piece, c), shards).start()

    def relay(piece):
        def hop(d, carry):
            @pl.when(z >= d)
            def _():
                s = z - d
                up(piece, s, region(piece, s, c), s).wait_recv()

                @pl.when(z < shards - 1)
                def _():
                    up(piece, s, region(piece, s, c), s).start()

                y_copy(piece, s, c).start()
                near_copy(piece, s, c).start()

            @pl.when(z + d <= shards - 1)
            def _():
                s = z + d
                down(piece, s, region(piece, s, c), s).wait_recv()

                @pl.when(z > 0)
                def _():
                    down(piece, s, region(piece, s, c), s).start()

                y_copy(piece, s, c).start()
                near_copy(piece, s, c).start()

            return carry

        lax.fori_loop(1, shards, hop, 0)

    def others(act):
        def one(d, carry):
            act(lax.rem(z + d, shards))
            return carry

        lax.fori_loop(1, shards, one, 0)

    def spread(piece):
        def act(s):
            y_copy(piece, s, across).wait_recv()
            far_copy(piece, s, across).start()

        others(act)

    pieces = len(plan)
    for piece in range(min(depth, pieces)):
        begin(piece)
    for item in range(count):
        loads[item].start()
    for item in range(count):
        loads[item].wait()
        stores[item].start()
    for piece in range(pieces):
        relay(piece)
        if piece + depth < pieces:
            begin(piece + depth)
        if piece >= 1:
            spread(piece - 1)
    spread(pieces - 1)
    for piece in range(pieces):

        @pl.when(z < shards - 1)
        def _():
            up(piece, z, own(piece, c), z).wait_send()

        @pl.when(z > 0)
        def _():
            down(piece, z, own(piece, c), shards).wait_send()

        def act(s, piece=piece):
            near_copy(piece, s, beside).wait_recv()
            far_copy(piece, s, lax.rem(beside + 2, 4)).wait_recv()
            y_copy(piece, s, c).wait_send()
            near_copy(piece, s, c).wait_send()
            far_copy(piece, s, across).wait_send()

            @pl.when((s < z) & (z < shards - 1))
            def _():
                up(piece, s, region(piece, s, c), s).wait_send()

            @pl.when((s > z) & (z > 0))
            def _():
                down(piece, s, region(piece, s, c), s).wait_send()

        others(act)
    for item in range(count):
        stores[item].wait()


def gather(weights, axes, plan, shards, depth, collective_id):
    count = len(weights)
    shapes = []
    for w, axis in zip(weights, axes):
        shape = list(w.shape)
        shape[axis] *= shards
        shapes.append(jax.ShapeDtypeStruct(tuple(shape), w.dtype))
    pieces = len(plan)
    table = pltpu.SemaphoreType.DMA((pieces, shards))
    return pl.pallas_call(
        functools.partial(gather_kernel, plan, count, shards, depth),
        out_shape=shapes,
        in_specs=[pl.BlockSpec(memory_space=pl.ANY)] * count,
        out_specs=[pl.BlockSpec(memory_space=pl.ANY)] * count,
        scratch_shapes=[
            *[pltpu.VMEM(w.shape, w.dtype) for w in weights],
            pltpu.SemaphoreType.DMA((count,)),
            pltpu.SemaphoreType.DMA((count,)),
            table, table, table, table,
            pltpu.SemaphoreType.DMA((pieces, shards + 1)),
            table, table, table,
        ],
        compiler_params=pltpu.CompilerParams(collective_id=collective_id, has_side_effects=True, vmem_limit_bytes=40 * 2**20),
    )(*weights)


def shifted(array, axis, by):
    count = lax.axis_size(axis)
    pairs = [(i, i + by) for i in range(count) if 0 <= i + by < count]
    return lax.ppermute(array, axis, pairs)


def swap(array):
    return lax.ppermute(array, "tensor", [(0, 1), (1, 0)])


def rms_norm(values, scaling):
    return values * lax.rsqrt(jnp.mean(values * values, axis=-1, keepdims=True) + EPSILON) * scaling


def gelu_tanh(values):
    return jax.nn.gelu(values, approximate=True)


def rotate_half(values, cosine, sine_table):
    middle = values.shape[-1] // 2
    former = values[..., :middle]
    latter = values[..., middle:]
    return jnp.concatenate(
        [former * cosine - latter * sine_table, latter * cosine + former * sine_table], axis=-1
    )


def rope_tables(positions, head_size):
    frequency = jnp.exp(
        jnp.arange(head_size // 2, dtype=jnp.float32) * (-2.0 * math.log(10000.0) / head_size)
    )
    angles = positions.astype(jnp.float32)[..., None] * frequency
    return (jnp.cos(angles), jnp.sin(angles))


def low(values):
    return values.astype(jnp.bfloat16)


def wide(values):
    return values.astype(jnp.float32)


def matmul(left_op, right_op):
    return jnp.dot(low(left_op), low(right_op), preferred_element_type=jnp.float32)


def matmul_t(left_op, right_op):
    return lax.dot_general(
        low(left_op), low(right_op), (((1,), (1,)), ((), ())), preferred_element_type=jnp.float32
    )


def outer(left_op, right_op):
    return lax.dot_general(
        low(left_op), low(right_op), (((0,), (0,)), ((), ())), preferred_element_type=jnp.float32
    )


def share(packed):
    part = lax.psum_scatter(packed, "context", scatter_dimension=1, tiled=True)
    whole = lax.all_gather(low(part), ("shard", "context", "tensor"), axis=0, tiled=False)
    shards, contexts, tensors = (lax.axis_size(a) for a in ("shard", "context", "tensor"))
    whole = whole.reshape(shards, contexts, tensors, packed.shape[0], part.shape[1])
    return whole.transpose(2, 0, 3, 1, 4).reshape(tensors, shards, packed.shape[0], packed.shape[1])


def body(
    tokens,
    layer_input,
    segments,
    adapter_ids,
    cotangent,
    w_query,
    w_key,
    w_value,
    w_output,
    w_gate,
    w_up,
    w_down,
    laurel_left,
    laurel_right,
    input_gate,
    input_proj,
    gain_in,
    gain_attn,
    gain_laurel,
    gain_pre,
    gain_post,
    gain_layer,
    gain_query,
    gain_key,
    adapt_attn_in,
    adapt_query_out,
    adapt_kv_out,
    adapt_out_in,
    adapt_out_out,
    adapt_ffn_in,
    adapt_gu_out,
    adapt_down_in,
    adapt_down_out,
):
    seq_count, count, width = tokens.shape
    assert seq_count == 1 and lax.axis_size("tensor") == 2 and lax.axis_size("context") == 4
    half = count // 2
    head_size = gain_query.shape[0]
    rank = adapt_query_out.shape[1]
    heads = adapt_query_out.shape[2] // head_size
    kv_heads = adapt_kv_out.shape[3] // head_size
    group = heads // kv_heads
    side = lax.axis_index("tensor")
    place = lax.axis_index("context")
    shards = lax.axis_size("shard")

    weights = (
        w_query, w_key, w_value, laurel_left, w_output, laurel_right,
        w_gate, w_up, input_gate, input_proj, w_down,
    )
    axes = (0, 0, 0, 0, 1, 1, 0, 0, 0, 1, 1)
    plan = [(i, axes[i], 0, weights[i].shape[0], 0, weights[i].shape[1]) for i in range(6)]
    steps = 4
    hidden_here = w_gate.shape[1]
    cut = hidden_here // steps
    for j in range(steps):
        plan += [(i, 0, 0, weights[i].shape[0], j * cut, cut) for i in (6, 7)]
        if j == steps - 1:
            plan += [(i, axes[i], 0, weights[i].shape[0], 0, weights[i].shape[1]) for i in (8, 9)]
        plan.append((10, 1, j * cut, cut, 0, weights[10].shape[1]))
    (
        full_query, full_key, full_value, full_left, full_output, full_right,
        full_gate, full_up, full_layer_gate, full_layer_proj, full_down,
    ) = gather(weights, axes, tuple(plan), shards, 2, 0)

    chosen = adapter_ids[0]

    def pick(table):
        return lax.dynamic_index_in_dim(table, chosen, 0, keepdims=False)

    pick_attn_in, pick_query_out, pick_kv_out = pick(adapt_attn_in), pick(adapt_query_out), pick(adapt_kv_out)
    pick_out_in, pick_out_out, pick_ffn_in = pick(adapt_out_in), pick(adapt_out_out), pick(adapt_ffn_in)
    pick_gu_out, pick_down_in, pick_down_out = pick(adapt_gu_out), pick(adapt_down_in), pick(adapt_down_out)

    def own_half(array):
        return lax.dynamic_slice_in_dim(array, side * half, half, 0)

    def other_half(array):
        return lax.dynamic_slice_in_dim(array, (1 - side) * half, half, 0)

    def in_order(own, other):
        return jnp.where(
            side == 0, jnp.concatenate([own, other], axis=0), jnp.concatenate([other, own], axis=0)
        )

    start_pos = place * count
    seg_all = segments[0]
    seg_query = lax.dynamic_slice_in_dim(seg_all, start_pos, count, 0)
    before = jnp.sum((seg_all[None, :] < seg_query[:, None]).astype(jnp.int32), axis=1)
    own_pos = start_pos + jnp.arange(count, dtype=jnp.int32) - before
    cosine, sine_table = rope_tables(own_pos, head_size)
    cosine = cosine[:, None, :]
    sine_table = sine_table[:, None, :]
    tokens_f = wide(tokens[0])
    normed_b = low(rms_norm(tokens_f, gain_in))
    tokens_h = wide(own_half(tokens[0]))
    normed_h, normed_back = jax.vjp(lambda v: rms_norm(v, gain_in), tokens_h)
    code_attn = matmul(normed_b, pick_attn_in)
    query_lin = matmul(normed_b, full_query) + matmul(code_attn[:, :rank], pick_query_out)
    key_lin = matmul(normed_b, full_key) + matmul(code_attn[:, rank : 2 * rank], pick_kv_out[0])
    value_lin = matmul(normed_b, full_value) + matmul(code_attn[:, 2 * rank :], pick_kv_out[1])

    def prepare(query_in, key_in, value_in):
        query_rot = rotate_half(
            rms_norm(query_in.reshape(count, heads, head_size), gain_query), cosine, sine_table
        )
        key_rot = rotate_half(
            rms_norm(key_in.reshape(count, kv_heads, head_size), gain_key), cosine, sine_table
        )
        value_nrm = rms_norm(value_in.reshape(count, kv_heads, head_size), 1.0)
        return (query_rot, key_rot, value_nrm)

    (query_rot, key_rot, value_nrm), prepare_back = jax.vjp(prepare, query_lin, key_lin, value_lin)
    query_b = low(query_rot).reshape(count, kv_heads, group, head_size)
    kv_own = low(jnp.stack([key_rot, value_nrm]))
    kv_prior = shifted(kv_own, "context", 1)
    kv_all = jnp.concatenate([kv_prior, kv_own], axis=1)
    query_pos = start_pos + jnp.arange(count, dtype=jnp.int32)
    key_pos = start_pos - count + jnp.arange(2 * count, dtype=jnp.int32)
    seg_prior = lax.dynamic_slice_in_dim(seg_all, jnp.maximum(start_pos - count, 0), count, 0)
    seg_keys = jnp.concatenate([seg_prior, seg_query], axis=0)
    distance = query_pos[:, None] - key_pos[None, :]
    window_ok = (distance >= 0) & (distance < WINDOW) & (key_pos >= 0)[None, :]
    allowed = (seg_query[:, None] == seg_keys[None, :]) & window_ok
    allowed = allowed[None, None]
    score_scale = 1.0 / math.sqrt(head_size)

    def masked_scores():
        raw_scores = (
            jnp.einsum("lkgd,mkd->kglm", query_b, kv_all[0], preferred_element_type=jnp.float32)
            * score_scale
        )
        return jnp.where(allowed, raw_scores, -1e30)

    scores = masked_scores()
    row_max = jnp.max(scores, axis=-1, keepdims=True)
    exponent = jnp.exp(scores - row_max)
    row_total = jnp.sum(exponent, axis=-1, keepdims=True)
    log_total = row_max + jnp.log(row_total)
    attn_probs = low(exponent / row_total)
    attended = jnp.einsum("kglm,mkd->lkgd", attn_probs, kv_all[1], preferred_element_type=jnp.float32)
    attended_b = low(attended.reshape(count, heads * head_size))
    code_out = matmul(attended_b, pick_out_in)
    attn_part = low(matmul(attended_b, full_output) + matmul(code_out, pick_out_out))
    attn_proj = wide(own_half(attn_part)) + wide(swap(other_half(attn_part)))
    laurel_mid = low(matmul(normed_h, full_left))
    laurel_end = matmul(laurel_mid, full_right)

    def combine(inputs_in, normed_in, attn_in, laurel_in):
        return (
            inputs_in + rms_norm(attn_in, gain_attn) + normed_in + rms_norm(laurel_in, gain_laurel)
        ) * ROOT_HALF

    combined, combine_back = jax.vjp(combine, tokens_h, normed_h, attn_proj, laurel_end)
    ffn_input, pre_ffn_back = jax.vjp(lambda v: rms_norm(v, gain_pre), combined)
    ffn_own = low(ffn_input)
    ffn_b = jnp.concatenate([ffn_own, swap(ffn_own)], axis=0)
    code_ffn = matmul(ffn_b, pick_ffn_in)
    gate_lin = matmul(ffn_b, full_gate) + matmul(code_ffn[:, :rank], pick_gu_out[0])
    up_lin = matmul(ffn_b, full_up) + matmul(code_ffn[:, rank:], pick_gu_out[1])

    def activate(gate_in, up_in):
        return gelu_tanh(gate_in) * up_in

    hidden_act, activate_back = jax.vjp(activate, gate_lin, up_lin)
    hidden_b = low(hidden_act)
    code_down = matmul(hidden_b, pick_down_in)
    down_part = low(matmul(hidden_b, full_down) + matmul(code_down, pick_down_out))
    down_proj = wide(down_part[:half]) + wide(swap(down_part[half:]))

    def after_step(combined_in, down_in):
        return combined_in + rms_norm(down_in, gain_post)

    after_ffn, after_back = jax.vjp(after_step, combined, down_proj)
    layer_gate = matmul(after_ffn, full_layer_gate)
    per_layer = wide(own_half(layer_input[0]))

    def mix_layer(gate_in):
        return gelu_tanh(gate_in) * per_layer

    layer_mix, mix_back = jax.vjp(mix_layer, layer_gate)
    layer_proj = matmul(layer_mix, full_layer_proj)

    def finish(after_in, proj_in):
        return after_in + rms_norm(proj_in, gain_layer)

    output_h, finish_back = jax.vjp(finish, after_ffn, layer_proj)
    output_own = low(output_h)
    layer_output = in_order(output_own, swap(output_own))
    grad_after, grad_lproj = finish_back(wide(own_half(cotangent[0])))
    (grad_lgate,) = mix_back(matmul_t(grad_lproj, full_layer_proj))
    grad_after = grad_after + matmul_t(grad_lgate, full_layer_gate)
    grad_comb, grad_down = after_back(grad_after)
    grad_down_own = low(grad_down)
    grad_down_b = jnp.concatenate([grad_down_own, swap(grad_down_own)], axis=0)
    code_down_back = matmul_t(grad_down_b, pick_down_out)
    term_down_out = outer(code_down, grad_down_b)
    term_down_in = outer(code_down_back, hidden_b)
    grad_hidden = matmul_t(grad_down_b, full_down) + matmul_t(code_down_back, pick_down_in)
    grad_gate, grad_up = activate_back(grad_hidden)
    grad_gate_b = low(grad_gate)
    grad_up_b = low(grad_up)
    code_ffn_back = jnp.concatenate(
        [matmul_t(grad_gate_b, pick_gu_out[0]), matmul_t(grad_up_b, pick_gu_out[1])], axis=1
    )
    term_gate_out = outer(code_ffn[:, :rank], grad_gate_b)
    term_up_out = outer(code_ffn[:, rank:], grad_up_b)
    term_ffn_in = outer(code_ffn_back, ffn_b)
    mark = jnp.where(
        (lax.broadcasted_iota(jnp.int32, (rank, 512), 1) == chosen) & (place == 0), 1.0, 0.0
    )
    early = share(
        jnp.concatenate(
            [term_gate_out, term_up_out, term_down_in, term_ffn_in[:rank], term_ffn_in[rank:], term_down_out, mark],
            axis=1,
        )
    )
    grad_ffn_part = low(
        matmul_t(grad_gate_b, full_gate)
        + matmul_t(grad_up_b, full_up)
        + matmul_t(code_ffn_back, pick_ffn_in)
    )
    grad_ffn_input = wide(grad_ffn_part[:half]) + wide(swap(grad_ffn_part[half:]))
    grad_comb = grad_comb + pre_ffn_back(grad_ffn_input)[0]
    grad_inputs, grad_normed, grad_attn, grad_laurel = combine_back(grad_comb)
    grad_laurel_mid = low(matmul_t(grad_laurel, full_right))
    grad_normed = grad_normed + matmul_t(grad_laurel_mid, full_left)
    grad_attn_own = low(grad_attn)
    grad_attn_b = in_order(grad_attn_own, swap(grad_attn_own))
    code_out_back = matmul_t(grad_attn_b, pick_out_out)
    term_out_out = outer(code_out, grad_attn_b)
    term_out_in = outer(code_out_back, attended_b)
    grad_attended = low(matmul_t(grad_attn_b, full_output) + matmul_t(code_out_back, pick_out_in))
    grad_heads = grad_attended.reshape(count, kv_heads, group, head_size)
    recomputed = jnp.exp(masked_scores() - log_total)
    grad_probs = jnp.einsum("lkgd,mkd->kglm", grad_heads, kv_all[1], preferred_element_type=jnp.float32)
    grad_scores = low(
        recomputed * (grad_probs - jnp.sum(recomputed * grad_probs, axis=-1, keepdims=True))
    )
    grad_query = (
        jnp.einsum("kglm,mkd->lkgd", grad_scores, kv_all[0], preferred_element_type=jnp.float32)
        * score_scale
    )
    grad_keys = (
        jnp.einsum("kglm,lkgd->mkd", grad_scores, query_b, preferred_element_type=jnp.float32)
        * score_scale
    )
    grad_values = jnp.einsum(
        "kglm,lkgd->mkd", low(recomputed), grad_heads, preferred_element_type=jnp.float32
    )
    grad_kv = jnp.stack([grad_keys, grad_values])
    grad_kv_later = wide(shifted(low(grad_kv[:, :count]), "context", -1))
    grad_kv_own = grad_kv[:, count:] + grad_kv_later
    grad_qlin, grad_klin, grad_vlin = prepare_back(
        (grad_query.reshape(count, heads, head_size), grad_kv_own[0], grad_kv_own[1])
    )
    grad_qlin_b = low(grad_qlin)
    grad_klin_b = low(grad_klin)
    grad_vlin_b = low(grad_vlin)
    code_attn_back = jnp.concatenate(
        [
            matmul_t(grad_qlin_b, pick_query_out),
            matmul_t(grad_klin_b, pick_kv_out[0]),
            matmul_t(grad_vlin_b, pick_kv_out[1]),
        ],
        axis=1,
    )
    term_query_out = outer(code_attn[:, :rank], grad_qlin_b)
    term_key_out = outer(code_attn[:, rank : 2 * rank], grad_klin_b)
    term_value_out = outer(code_attn[:, 2 * rank :], grad_vlin_b)
    term_attn_in = outer(code_attn_back, normed_b)
    late = share(
        jnp.concatenate(
            [
                term_out_in, term_out_out, term_query_out, term_key_out, term_value_out,
                term_attn_in[:rank], term_attn_in[rank : 2 * rank], term_attn_in[2 * rank :],
            ],
            axis=1,
        )
    )
    grad_normed_part = low(
        matmul_t(grad_qlin_b, full_query)
        + matmul_t(grad_klin_b, full_key)
        + matmul_t(grad_vlin_b, full_value)
        + matmul_t(code_attn_back, pick_attn_in)
    )
    grad_normed = grad_normed + wide(own_half(grad_normed_part)) + wide(swap(other_half(grad_normed_part)))
    grad_own = low(grad_inputs + normed_back(grad_normed)[0])
    input_grad = in_order(grad_own, swap(grad_own))

    at = 0

    def take(packed, columns):
        nonlocal at
        at += columns
        return wide(packed[..., at - columns : at])

    def joined(packed, columns):
        both = take(packed, columns)
        return jnp.concatenate([both[0], both[1]], axis=-1)

    def added(packed, columns):
        both = take(packed, columns)
        return both[0] + both[1]

    gate_out, up_out, down_in = (joined(early, hidden_here) for _ in range(3))
    ffn_in = [added(early, width) for _ in range(2)]
    down_out = added(early, width)
    adapters = adapt_attn_in.shape[0]
    marks = wide(early[0, :, 0, at : at + adapters])
    at = 0
    out_in = joined(late, heads * head_size)
    out_out = added(late, width)
    query_out = joined(late, heads * head_size)
    key_out, value_out = (joined(late, kv_heads * head_size) for _ in range(2))
    attn_in = [added(late, width) for _ in range(3)]

    def tables(terms):
        return sum(
            marks[s].reshape((adapters,) + (1,) * (terms.ndim - 1)) * terms[s][None] for s in range(shards)
        )

    def turned(terms):
        return tables(terms).transpose(0, 2, 1)

    return (
        layer_output[None],
        input_grad[None],
        turned(jnp.concatenate(attn_in, axis=1)),
        tables(query_out),
        tables(jnp.stack([key_out, value_out], axis=1)),
        turned(out_in),
        tables(out_out),
        turned(jnp.concatenate(ffn_in, axis=1)),
        tables(jnp.stack([gate_out, up_out], axis=1)),
        turned(down_in),
        tables(down_out),
    )


def solution(mesh):
    in_specs = (
        P("shard", "context", None),
        P("shard", "context", None),
        P("shard", None),
        P("shard"),
        P("shard", "context", None),
        P("shard", "tensor"),
        P("shard", "tensor"),
        P("shard", "tensor"),
        P("tensor", "shard"),
        P("shard", "tensor"),
        P("shard", "tensor"),
        P("tensor", "shard"),
        P("shard", None),
        P(None, "shard"),
        P("shard", None),
        P(None, "shard"),
        P(),
        P(),
        P(),
        P(),
        P(),
        P(),
        P(),
        P(),
        P(),
        P(None, None, "tensor"),
        P(None, None, None, "tensor"),
        P(None, "tensor", None),
        P(),
        P(),
        P(None, None, None, "tensor"),
        P(None, "tensor", None),
        P(),
    )
    out_specs = (
        P("shard", "context", None),
        P("shard", "context", None),
        P(),
        P(),
        P(),
        P(),
        P(),
        P(),
        P(),
        P(),
        P(),
    )
    return jax.shard_map(body, mesh=mesh, in_specs=in_specs, out_specs=out_specs, check_vma=False)
```

```python
import functools
import math

import jax
import jax.numpy as jnp
from jax import lax
from jax.experimental import pallas as pl
from jax.experimental.pallas import tpu as pltpu
from jax.sharding import PartitionSpec as P

WINDOW = 512
EPSILON = 1e-06
ROOT_HALF = 0.7071067811865476
GELU_SCALE = math.sqrt(2.0 / math.pi)
GELU_CUBE = 0.044715

MESH = pl.DeviceIdType.MESH


def shifted(array, axis, by):
    count = lax.axis_size(axis)
    pairs = [(i, i + by) for i in range(count) if 0 <= i + by < count]
    return lax.ppermute(array, axis, pairs)


def swap(array):
    return lax.ppermute(array, "tensor", [(0, 1), (1, 0)])


def rms_norm(values, scaling):
    return values * lax.rsqrt(jnp.mean(values * values, axis=-1, keepdims=True) + EPSILON) * scaling


def gelu_tanh(values):
    return jax.nn.gelu(values, approximate=True)


def rotate_half(values, cosine, sine_table):
    middle = values.shape[-1] // 2
    former = values[..., :middle]
    latter = values[..., middle:]
    return jnp.concatenate(
        [former * cosine - latter * sine_table, latter * cosine + former * sine_table], axis=-1
    )


def rope_tables(positions, head_size):
    frequency = jnp.exp(
        jnp.arange(head_size // 2, dtype=jnp.float32) * (-2.0 * math.log(10000.0) / head_size)
    )
    angles = positions.astype(jnp.float32)[..., None] * frequency
    return (jnp.cos(angles), jnp.sin(angles))


def low(values):
    return values.astype(jnp.bfloat16)


def wide(values):
    return values.astype(jnp.float32)


def matmul(left_op, right_op):
    return jnp.dot(low(left_op), low(right_op), preferred_element_type=jnp.float32)


def matmul_t(left_op, right_op):
    return lax.dot_general(
        low(left_op), low(right_op), (((1,), (1,)), ((), ())), preferred_element_type=jnp.float32
    )


def outer(left_op, right_op):
    return lax.dot_general(
        low(left_op), low(right_op), (((0,), (0,)), ((), ())), preferred_element_type=jnp.float32
    )


def dot(left, right):
    return lax.dot_general(left, right, (((1,), (0,)), ((), ())), preferred_element_type=jnp.float32)


def dot_t(left, right):
    return lax.dot_general(left, right, (((1,), (1,)), ((), ())), preferred_element_type=jnp.float32)


def dot_o(left, right):
    return lax.dot_general(left, right, (((0,), (0,)), ((), ())), preferred_element_type=jnp.float32)


def row_mean(values):
    return jnp.mean(values, axis=-1, keepdims=True)


def inverse_rms(values):
    return lax.rsqrt(row_mean(values * values) + EPSILON)


def rms_back(values, inverse, scaled):
    return inverse * scaled - values * (inverse * inverse * inverse * row_mean(values * scaled))


def gelu_parts(values):
    squared = values * values
    bend = jnp.tanh(GELU_SCALE * values * (1.0 + GELU_CUBE * squared))
    rise = 0.5 * (1.0 + bend)
    slope = rise + 0.5 * values * (1.0 - bend * bend) * (GELU_SCALE * (1.0 + 3.0 * GELU_CUBE * squared))
    return values * rise, slope


def ffn_back_kernel(
    grad, gate, up, codes, code_down, ffn, w_down, w_gate, w_up, down_in, down_out, gu_out, ffn_in,
    part, term_gate, term_up, term_down, term_ffn, term_out, total, back_codes, ffn_codes,
):
    step = pl.program_id(0)
    rank = down_in.shape[0]

    @pl.when(step == 0)
    def _():
        back_codes[...] = low(dot_t(grad[...], down_out[...]))
        total[...] = jnp.zeros_like(total)
        ffn_codes[...] = jnp.zeros_like(ffn_codes)
        term_out[...] = dot_o(code_down[...], grad[...])

    hidden_grad = dot_t(grad[...], w_down[...]) + dot(back_codes[...], down_in[...])
    up_now = wide(up[...])
    act, slope = gelu_parts(wide(gate[...]))
    grad_gate = low(hidden_grad * up_now * slope)
    grad_up = low(hidden_grad * act)
    hidden = low(act * up_now)
    total[...] += dot_t(grad_gate, w_gate[...]) + dot_t(grad_up, w_up[...])
    ffn_codes[0] += dot_t(grad_gate, gu_out[0])
    ffn_codes[1] += dot_t(grad_up, gu_out[1])
    term_gate[...] = dot_o(codes[:, :rank], grad_gate)
    term_up[...] = dot_o(codes[:, rank:], grad_up)
    term_down[...] = dot_o(back_codes[...], hidden)

    @pl.when(step == pl.num_programs(0) - 1)
    def _():
        first, second = low(ffn_codes[0]), low(ffn_codes[1])
        part[...] = low(total[...] + dot(first, ffn_in[:rank]) + dot(second, ffn_in[rank:]))
        term_ffn[:rank] = dot_o(first, ffn[...])
        term_ffn[rank:] = dot_o(second, ffn[...])


def ffn_back(group, grad, gate, up, codes, code_down, ffn, w_down, w_gate, w_up, down_in, down_out, gu_out, ffn_in):
    rows, width = grad.shape
    hidden = gate.shape[1]
    rank = down_in.shape[0]
    block = min(512, hidden)
    whole = lambda *shape: pl.BlockSpec(shape, lambda j: (0,) * len(shape))
    picked = lambda columns: pl.BlockSpec((rows, columns), lambda j: (group, 0))
    f32 = jnp.float32
    return pl.pallas_call(
        ffn_back_kernel,
        grid=(hidden // block,),
        in_specs=[
            whole(rows, width),
            pl.BlockSpec((rows, block), lambda j: (group, j)),
            pl.BlockSpec((rows, block), lambda j: (group, j)),
            picked(2 * rank),
            picked(rank),
            picked(width),
            pl.BlockSpec((block, width), lambda j: (j, 0)),
            pl.BlockSpec((width, block), lambda j: (0, j)),
            pl.BlockSpec((width, block), lambda j: (0, j)),
            pl.BlockSpec((rank, block), lambda j: (0, j)),
            whole(rank, width),
            pl.BlockSpec((2, rank, block), lambda j: (0, 0, j)),
            whole(2 * rank, width),
        ],
        out_specs=[
            whole(rows, width),
            pl.BlockSpec((rank, block), lambda j: (0, j)),
            pl.BlockSpec((rank, block), lambda j: (0, j)),
            pl.BlockSpec((rank, block), lambda j: (0, j)),
            whole(2 * rank, width),
            whole(rank, width),
        ],
        out_shape=[
            jax.ShapeDtypeStruct((rows, width), jnp.bfloat16),
            jax.ShapeDtypeStruct((rank, hidden), f32),
            jax.ShapeDtypeStruct((rank, hidden), f32),
            jax.ShapeDtypeStruct((rank, hidden), f32),
            jax.ShapeDtypeStruct((2 * rank, width), f32),
            jax.ShapeDtypeStruct((rank, width), f32),
        ],
        scratch_shapes=[
            pltpu.VMEM((rows, width), f32),
            pltpu.VMEM((rows, rank), jnp.bfloat16),
            pltpu.VMEM((2, rows, rank), f32),
        ],
        compiler_params=pltpu.CompilerParams(vmem_limit_bytes=48 * 2**20),
        cost_estimate=pl.CostEstimate(
            flops=6 * rows * width * hidden, bytes_accessed=6 * width * hidden, transcendentals=rows * hidden
        ),
    )(grad, gate, up, codes, code_down, ffn, w_down, w_gate, w_up, down_in, down_out, gu_out, ffn_in)


def crown_kernel(
    mine, theirs, combined, per_layer, cotangent, input_gate, input_proj, gain_post, gain_layer,
    output, grad_down, grad_after,
):
    down = wide(mine[...]) + wide(theirs[...])
    down_inverse = inverse_rms(down)
    after = combined[...] + down * down_inverse * gain_post[...]
    mixing = wide(per_layer[...])
    act, slope = gelu_parts(dot(low(after), input_gate[...]))
    proj = dot(low(act * mixing), input_proj[...])
    proj_inverse = inverse_rms(proj)
    output[...] = low(after + proj * proj_inverse * gain_layer[...])
    grad = wide(cotangent[...])
    grad_proj = rms_back(proj, proj_inverse, grad * gain_layer[...])
    grad_gate = dot_t(low(grad_proj), input_proj[...]) * mixing * slope
    grad = grad + dot_t(low(grad_gate), input_gate[...])
    grad_after[...] = grad
    grad_down[...] = low(rms_back(down, down_inverse, grad * gain_post[...]))


def comb_back_kernel(
    mine, theirs, grad_after, combined, attn_proj, laurel_mid, left, right, gain_pre, gain_attn, gain_laurel,
    grad_attn, grad_comb, grad_normed,
):
    grad = (wide(mine[...]) + wide(theirs[...])) * gain_pre[...]
    comb = combined[...]
    grad = (grad_after[...] + rms_back(comb, inverse_rms(comb), grad)) * ROOT_HALF
    grad_comb[...] = grad
    proj = attn_proj[...]
    grad_attn[...] = low(rms_back(proj, inverse_rms(proj), grad * gain_attn[...]))
    end = dot(laurel_mid[...], right[...])
    grad_end = low(rms_back(end, inverse_rms(end), grad * gain_laurel[...]))
    grad_normed[...] = grad + dot(low(dot_t(grad_end, right[...])), left[...])


def rowwise(kernel, group, rows, arrays, constants, outs):
    width = max(a.shape[1] for a, _ in arrays)

    def spec(columns, at):
        return pl.BlockSpec((rows, columns), lambda i: (at, 0))

    return pl.pallas_call(
        kernel,
        grid=(1,),
        in_specs=[spec(a.shape[1], group if own is None else own) for a, own in arrays]
        + [pl.BlockSpec(c.shape, lambda i: (0, 0)) for c in constants],
        out_specs=[spec(columns, 0) for columns, _ in outs],
        out_shape=[jax.ShapeDtypeStruct((rows, columns), kind) for columns, kind in outs],
        compiler_params=pltpu.CompilerParams(vmem_limit_bytes=48 * 2**20),
        cost_estimate=pl.CostEstimate(
            flops=40 * rows * width + 2 * rows * width * 1024, bytes_accessed=24 * rows * width, transcendentals=rows
        ),
    )(*[a for a, _ in arrays], *constants)


def mover(sources, fulls, semaphores, shards):
    z_recv, y_recv, near_recv, far_recv, z_send, y_send, near_send, far_send = semaphores
    z, c = lax.axis_index("shard"), lax.axis_index("context")
    across = lax.rem(c + 2, 4)
    beside = c + 1 - 2 * lax.rem(c, 2)

    def greet(also=()):
        barrier = pltpu.get_barrier_semaphore()

        def signal(place):
            pl.semaphore_signal(barrier, inc=1, device_id=place, device_id_type=MESH)

        signal({"context": across})
        signal({"context": beside})
        for place in also:
            signal(place)

        @pl.when(z > 0)
        def _():
            signal({"shard": z - 1})

        @pl.when(z < shards - 1)
        def _():
            signal({"shard": z + 1})

        peers = 2 + len(also) + lax.div(z + shards - 1, shards) + lax.div(2 * shards - 2 - z, shards)
        pl.semaphore_wait(barrier, peers)

    def region(piece, s, q):
        _, item, axis, row, rows, col, cols = piece
        rows_here, cols_here = sources[item].shape
        part = rows // 4
        if axis == 0:
            return fulls[item].at[
                pl.ds(pl.multiple_of(s * rows_here + row + q * part, 16), part),
                pl.ds(pl.multiple_of(col, 128), cols),
            ]
        return fulls[item].at[
            pl.ds(pl.multiple_of(row + q * part, 16), part),
            pl.ds(pl.multiple_of(s * cols_here + col, 128), cols),
        ]

    def own(piece):
        _, item, axis, row, rows, col, cols = piece
        part = rows // 4
        return sources[item].at[
            pl.ds(pl.multiple_of(row + c * part, 16), part), pl.ds(pl.multiple_of(col, 128), cols)
        ]

    def copy(source, target, send, recv, place):
        return pltpu.make_async_remote_copy(
            src_ref=source, dst_ref=target, send_sem=send, recv_sem=recv, device_id=place, device_id_type=MESH
        )

    def along(piece, s, source, sender, by):
        slot = piece[0]
        return copy(source, region(piece, s, c), z_send.at[slot, sender], z_recv.at[slot, s], {"shard": z + by})

    def passed(piece, s, by):
        return along(piece, s, region(piece, s, c), s, by)

    def y_copy(piece, s, q):
        at = region(piece, s, q)
        return copy(at, at, y_send.at[piece[0], s], y_recv.at[piece[0], s], {"context": across})

    def near_copy(piece, s, q):
        at = region(piece, s, q)
        return copy(at, at, near_send.at[piece[0], s], near_recv.at[piece[0], s], {"context": beside})

    def far_copy(piece, s, q):
        at = region(piece, s, q)
        return copy(at, at, far_send.at[piece[0], s], far_recv.at[piece[0], s], {"context": beside})

    def begin(pieces):
        @pl.when(z < shards - 1)
        def _():
            for piece in pieces:
                along(piece, z, own(piece), z, 1).start()

        @pl.when(z > 0)
        def _():
            for piece in pieces:
                along(piece, z, own(piece), shards, -1).start()

    def relay(pieces, first=1, last=None):
        def hop(d, carry):
            @pl.when(z >= d)
            def _():
                s = z - d
                for piece in pieces:
                    passed(piece, s, 1).wait_recv()

                    @pl.when(z < shards - 1)
                    def _(piece=piece):
                        passed(piece, s, 1).start()

                    y_copy(piece, s, c).start()
                    near_copy(piece, s, c).start()

            @pl.when(z + d <= shards - 1)
            def _():
                s = z + d
                for piece in pieces:
                    passed(piece, s, -1).wait_recv()

                    @pl.when(z > 0)
                    def _(piece=piece):
                        passed(piece, s, -1).start()

                    y_copy(piece, s, c).start()
                    near_copy(piece, s, c).start()

            return carry

        last = shards - 1 if last is None else last
        if first == last:
            hop(first, 0)
        else:
            lax.fori_loop(first, last + 1, hop, 0)

    def others(pieces, act):
        def one(d, carry):
            for piece in pieces:
                act(piece, lax.rem(z + d, shards))
            return carry

        lax.fori_loop(1, shards, one, 0)

    def spread(pieces):
        def act(piece, s):
            y_copy(piece, s, across).wait_recv()
            far_copy(piece, s, across).start()

        others(pieces, act)

    def finish(pieces):
        def act(piece, s):
            near_copy(piece, s, beside).wait_recv()
            far_copy(piece, s, lax.rem(beside + 2, 4)).wait_recv()

        others(pieces, act)

    def flush(pieces):
        @pl.when(z < shards - 1)
        def _():
            for piece in pieces:
                along(piece, z, own(piece), z, 1).wait_send()

        @pl.when(z > 0)
        def _():
            for piece in pieces:
                along(piece, z, own(piece), shards, -1).wait_send()

        def act(piece, s):
            y_copy(piece, s, c).wait_send()
            near_copy(piece, s, c).wait_send()
            far_copy(piece, s, across).wait_send()

            @pl.when((s < z) & (z < shards - 1))
            def _():
                passed(piece, s, 1).wait_send()

            @pl.when((s > z) & (z > 0))
            def _():
                passed(piece, s, -1).wait_send()

        others(pieces, act)

    def own_place(item, axis):
        rows_here, cols_here = sources[item].shape
        if axis == 0:
            return fulls[item].at[pl.ds(pl.multiple_of(z * rows_here, 16), rows_here), :]
        return fulls[item].at[:, pl.ds(pl.multiple_of(z * cols_here, 128), cols_here)]

    return greet, begin, relay, spread, finish, flush, own_place


def mover_semaphores(slots, shards):
    table = pltpu.SemaphoreType.DMA((slots, shards))
    return [table, table, table, table, pltpu.SemaphoreType.DMA((slots, shards + 1)), table, table, table]


def full_shapes(weights, axes, shards):
    shapes = []
    for w, axis in zip(weights, axes):
        shape = list(w.shape)
        shape[axis] *= shards
        shapes.append(jax.ShapeDtypeStruct(tuple(shape), w.dtype))
    return shapes


def gather_kernel(axes, shards, *refs):
    count = len(axes)
    sources, fulls, held = refs[:count], refs[count : 2 * count], refs[2 * count : 3 * count]
    load_sem, store_sem = refs[3 * count : 3 * count + 2]
    greet, begin, relay, spread, finish, flush, own_place = mover(
        sources, fulls, refs[3 * count + 2 :], shards
    )
    pieces = [
        [(i, i, axes[i], 0, sources[i].shape[0], 0, sources[i].shape[1])] for i in range(count)
    ]
    greet()
    for piece in pieces:
        begin(piece)
    loads = [pltpu.make_async_copy(sources[i], held[i], load_sem.at[i]) for i in range(count)]
    stores = [pltpu.make_async_copy(held[i], own_place(i, axes[i]), store_sem.at[i]) for i in range(count)]
    for load in loads:
        load.start()
    for load, store in zip(loads, stores):
        load.wait()
        store.start()
    for piece in pieces:
        relay(piece)
    for piece in pieces:
        spread(piece)
    for piece in pieces:
        finish(piece)
    for piece in pieces:
        flush(piece)
    for store in stores:
        store.wait()


def gather(weights, axes, shards):
    count = len(weights)
    return pl.pallas_call(
        functools.partial(gather_kernel, axes, shards),
        out_shape=full_shapes(weights, axes, shards),
        in_specs=[pl.BlockSpec(memory_space=pl.ANY)] * count,
        out_specs=[pl.BlockSpec(memory_space=pl.ANY)] * count,
        scratch_shapes=[pltpu.VMEM(w.shape, w.dtype) for w in weights]
        + [pltpu.SemaphoreType.DMA((count,)), pltpu.SemaphoreType.DMA((count,))]
        + mover_semaphores(count, shards),
        compiler_params=pltpu.CompilerParams(
            collective_id=0, has_side_effects=True, vmem_limit_bytes=32 * 2**20
        ),
    )(*weights)


FORE_AXES = (1, 1, 0, 1, 0, 0, 1)


def fore_kernel(
    shards, block,
    w_output, w_right, w_lgate, w_lproj, w_gate, w_up, w_down,
    attended, tokens, laurel_mid, out_in, out_out, ffn_in, gu_out, down_in, down_out,
    gain_in, gain_attn, gain_laurel, gain_pre,
    full_output, full_right, full_lgate, full_lproj, full_gate, full_up, full_down, gate_out, up_out, ffn_out,
    attn_proj, combined, code_out, code_ffn, code_down, part,
    stage_a, stage_b, stage_c, stage_d, stage_e, stage_f, stage_g, out_w, right_w, gate_w, up_w, down_w, sent, got, ffn, total, codes, hidden,
    gate_keep, up_keep,
    load_sem, store_sem, weight_sem, keep_sem, ffn_sem, swap_send, swap_recv, *semaphores,
):
    sources = (w_output, w_right, w_lgate, w_lproj, w_gate, w_up, w_down)
    fulls = (full_output, full_right, full_lgate, full_lproj, full_gate, full_up, full_down)
    side = lax.axis_index("tensor")
    partner = {"tensor": 1 - side}
    greet, begin, relay, spread, finish, flush, own_place = mover(sources, fulls, semaphores, shards)
    rank = out_in.shape[0]
    count, width = ffn.shape
    half = count // 2
    quarter = half // 2
    groups = w_gate.shape[1] // block

    def whole(i):
        return (i, i, FORE_AXES[i], 0, sources[i].shape[0], 0, sources[i].shape[1])

    first = [whole(0), whole(1)]
    small = [whole(2), whole(3)]

    def group(g):
        base = 4 + 3 * g
        return [
            (base, 4, 0, 0, sources[4].shape[0], g * block, block),
            (base + 1, 5, 0, 0, sources[5].shape[0], g * block, block),
            (base + 2, 6, 1, g * block, block, 0, sources[6].shape[1]),
        ]

    greet([partner])
    begin(first)
    begin(group(0))
    begin(small)
    begin(group(1))
    stages = (stage_a, stage_b, stage_c, stage_d, stage_e, stage_f, stage_g)
    loads = [pltpu.make_async_copy(sources[i], stages[i], load_sem.at[i]) for i in range(7)]
    stores = [pltpu.make_async_copy(stages[i], own_place(i, FORE_AXES[i]), store_sem.at[i]) for i in range(7)]
    for load in loads:
        load.start()
    for load, store in zip(loads, stores):
        load.wait()
        store.start()
    for store in stores:
        store.wait()

    relay(first)
    spread(first)
    finish(first)
    load_out = pltpu.make_async_copy(full_output, out_w, weight_sem.at[0])
    load_right = pltpu.make_async_copy(full_right, right_w, weight_sem.at[1])
    load_out.start()
    load_right.start()
    code = low(dot_t(attended[...], out_in[...]))
    code_out[...] = code
    load_out.wait()
    load_right.wait()
    mine = pl.ds(pl.multiple_of(side * half, half), half)
    theirs = pl.ds(pl.multiple_of((1 - side) * half, half), half)
    sent[...] = low(dot(attended[theirs, :], out_w[...]) + dot(code_out[theirs, :], out_out[...]))
    swap_attn = pltpu.make_async_remote_copy(
        src_ref=sent, dst_ref=got, send_sem=swap_send.at[0], recv_sem=swap_recv.at[0],
        device_id=partner, device_id_type=MESH,
    )
    swap_attn.start()
    attn_proj[...] = dot(attended[mine, :], out_w[...]) + dot(code_out[mine, :], out_out[...])

    relay(group(0))
    swap_attn.wait()
    rows = 64

    def combine(i, carry):
        at = pl.ds(pl.multiple_of(i * rows, rows), rows)
        proj = attn_proj[at, :] + wide(got[at, :])
        attn_proj[at, :] = proj
        token = wide(tokens[at, :])
        normed = token * inverse_rms(token) * gain_in[...]
        end = dot(laurel_mid[at, :], right_w[...])
        comb = (
            token + proj * inverse_rms(proj) * gain_attn[...] + normed + end * inverse_rms(end) * gain_laurel[...]
        ) * ROOT_HALF
        combined[at, :] = comb
        to = pl.multiple_of(i * rows + lax.div(i * rows, quarter) * quarter, rows)
        ffn[pl.ds(to, rows), :] = low(comb * inverse_rms(comb) * gain_pre[...])
        return carry

    lax.fori_loop(0, half // rows, combine, 0)
    swaps = []
    for k in range(2):
        swaps.append(
            pltpu.make_async_remote_copy(
                src_ref=ffn.at[pl.ds(k * half, quarter), :], dst_ref=ffn.at[pl.ds(k * half + quarter, quarter), :],
                send_sem=swap_send.at[1 + k], recv_sem=swap_recv.at[1 + k],
                device_id=partner, device_id_type=MESH,
            )
        )
        swaps[k].start()
    relay(small)
    spread(small)
    total[...] = jnp.zeros_like(total)
    codes[...] = jnp.zeros_like(codes)

    def keeps(g, slot):
        at = pl.ds(pl.multiple_of(g * block, block), block)
        return (
            pltpu.make_async_copy(gate_keep.at[slot], gate_out.at[:, at], keep_sem.at[0, slot]),
            pltpu.make_async_copy(up_keep.at[slot], up_out.at[:, at], keep_sem.at[1, slot]),
        )

    def weights(g):
        at = pl.ds(pl.multiple_of(g * block, block), block)
        return (
            pltpu.make_async_copy(full_gate.at[:, at], gate_w, weight_sem.at[2]),
            pltpu.make_async_copy(full_up.at[:, at], up_w, weight_sem.at[3]),
            pltpu.make_async_copy(full_down.at[at, :], down_w, weight_sem.at[4]),
        )

    def climb(g):
        at = pl.ds(pl.multiple_of(g * block, block), block)
        slot = lax.rem(g, 2)

        @pl.when(g >= 2)
        def _():
            for keep in keeps(g - 2, slot):
                keep.wait()

        ready = weights(g)
        ready[0].wait()
        gate = dot(ffn[...], gate_w[...]) + dot(code_ffn[:, :rank], gu_out[0, :, at])
        gate_keep[slot] = low(gate)
        act = gelu_parts(gate)[0]
        ready[1].wait()
        up = dot(ffn[...], up_w[...]) + dot(code_ffn[:, rank:], gu_out[1, :, at])
        up_keep[slot] = low(up)
        hidden[...] = low(act * up)
        for keep in keeps(g, slot):
            keep.start()

    def descend(g):
        at = pl.ds(pl.multiple_of(g * block, block), block)
        weights(g)[2].wait()
        codes[...] += dot_t(hidden[...], down_in[:, at])
        total[...] += dot(hidden[...], down_w[...])

    def round_(g, carry):
        more = g + 1 < groups

        @pl.when(more)
        def _():
            relay(group(g + 1), 1, 1)

        @pl.when(g + 2 < groups)
        def _():
            begin(group(g + 2))

        spread(group(g))

        @pl.when(g >= 1)
        def _():
            descend(g - 1)

        @pl.when(more)
        def _():
            relay(group(g + 1), 2, 2)

        finish(group(g))
        for load in weights(g):
            load.start()

        @pl.when(more)
        def _():
            relay(group(g + 1), 3)

        @pl.when(g == 0)
        def _():
            for swap_ffn in swaps:
                swap_ffn.wait()
            pltpu.make_async_copy(ffn, ffn_out, ffn_sem).start()
            code_ffn[...] = low(dot_t(ffn[...], ffn_in[...]))

        climb(g)
        return carry

    lax.fori_loop(0, groups, round_, 0)
    descend(groups - 1)
    code_down[...] = low(codes[...])
    part[...] = low(total[...] + dot(code_down[...], down_out[...]))
    finish(small)
    for g in (groups - 2, groups - 1):
        for keep in keeps(g, g % 2):
            keep.wait()
    pltpu.make_async_copy(ffn, ffn_out, ffn_sem).wait()
    flush(first)
    flush(small)

    def flush_group(g, carry):
        flush(group(g))
        return carry

    lax.fori_loop(0, groups, flush_group, 0)


def fore(
    weights, attended, tokens, laurel_mid, out_in, out_out, ffn_in, gu_out, down_in, down_out, gains, shards
):
    count = attended.shape[0]
    width = tokens.shape[1]
    hidden = weights[4].shape[1]
    half = count // 2
    rank = out_in.shape[0]
    block = min(512, hidden)
    groups = hidden // block
    bf16, f32 = jnp.bfloat16, jnp.float32
    anywhere, vmem = pl.BlockSpec(memory_space=pl.ANY), pl.BlockSpec(memory_space=pltpu.VMEM)
    shape = jax.ShapeDtypeStruct
    return pl.pallas_call(
        functools.partial(fore_kernel, shards, block),
        out_shape=full_shapes(weights, FORE_AXES, shards)
        + [
            shape((count, hidden), bf16),
            shape((count, hidden), bf16),
            shape((count, width), bf16),
            shape((half, width), f32),
            shape((half, width), f32),
            shape((count, rank), bf16),
            shape((count, 2 * rank), bf16),
            shape((count, rank), bf16),
            shape((count, width), bf16),
        ],
        in_specs=[anywhere] * 7 + [vmem] * 13,
        out_specs=[anywhere] * 10 + [vmem] * 6,
        scratch_shapes=[
            *[pltpu.VMEM(w.shape, bf16) for w in weights],
            pltpu.VMEM((weights[0].shape[0], width), bf16),
            pltpu.VMEM((weights[1].shape[0], width), bf16),
            pltpu.VMEM((width, block), bf16),
            pltpu.VMEM((width, block), bf16),
            pltpu.VMEM((block, width), bf16),
            pltpu.VMEM((half, width), bf16),
            pltpu.VMEM((half, width), bf16),
            pltpu.VMEM((count, width), bf16),
            pltpu.VMEM((count, width), f32),
            pltpu.VMEM((count, rank), f32),
            pltpu.VMEM((count, block), bf16),
            pltpu.VMEM((2, count, block), bf16),
            pltpu.VMEM((2, count, block), bf16),
            pltpu.SemaphoreType.DMA((7,)),
            pltpu.SemaphoreType.DMA((7,)),
            pltpu.SemaphoreType.DMA((5,)),
            pltpu.SemaphoreType.DMA((2, 2)),
            pltpu.SemaphoreType.DMA,
            pltpu.SemaphoreType.DMA((3,)),
            pltpu.SemaphoreType.DMA((3,)),
        ]
        + mover_semaphores(4 + 3 * groups, shards),
        compiler_params=pltpu.CompilerParams(
            collective_id=1, has_side_effects=True, vmem_limit_bytes=60 * 2**20
        ),
    )(*weights, attended, tokens, laurel_mid, out_in, out_out, ffn_in, gu_out, down_in, down_out, *gains)


def share(packed):
    part = lax.psum_scatter(packed, "context", scatter_dimension=1, tiled=True)
    whole = lax.all_gather(low(part), ("shard", "context", "tensor"), axis=0, tiled=False)
    shards, contexts, tensors = (lax.axis_size(a) for a in ("shard", "context", "tensor"))
    whole = whole.reshape(shards, contexts, tensors, packed.shape[0], part.shape[1])
    return whole.transpose(2, 0, 3, 1, 4).reshape(tensors, shards, packed.shape[0], packed.shape[1])


def body(
    tokens,
    layer_input,
    segments,
    adapter_ids,
    cotangent,
    w_query,
    w_key,
    w_value,
    w_output,
    w_gate,
    w_up,
    w_down,
    laurel_left,
    laurel_right,
    input_gate,
    input_proj,
    gain_in,
    gain_attn,
    gain_laurel,
    gain_pre,
    gain_post,
    gain_layer,
    gain_query,
    gain_key,
    adapt_attn_in,
    adapt_query_out,
    adapt_kv_out,
    adapt_out_in,
    adapt_out_out,
    adapt_ffn_in,
    adapt_gu_out,
    adapt_down_in,
    adapt_down_out,
):
    seq_count, count, width = tokens.shape
    assert seq_count == 1 and lax.axis_size("tensor") == 2 and lax.axis_size("context") == 4
    half = count // 2
    head_size = gain_query.shape[0]
    rank = adapt_query_out.shape[1]
    heads = adapt_query_out.shape[2] // head_size
    kv_heads = adapt_kv_out.shape[3] // head_size
    group = heads // kv_heads
    side = lax.axis_index("tensor")
    place = lax.axis_index("context")
    shards = lax.axis_size("shard")

    full_query, full_key, full_value, full_left = gather(
        (w_query, w_key, w_value, laurel_left.T), (0, 0, 0, 1), shards
    )
    hidden_here = w_gate.shape[1]
    chosen = adapter_ids[0]

    def pick(table):
        return lax.dynamic_index_in_dim(table, chosen, 0, keepdims=False)

    pick_attn_in, pick_query_out, pick_kv_out = pick(adapt_attn_in), pick(adapt_query_out), pick(adapt_kv_out)
    pick_out_in, pick_out_out, pick_ffn_in = pick(adapt_out_in), pick(adapt_out_out), pick(adapt_ffn_in)
    pick_gu_out, pick_down_in, pick_down_out = pick(adapt_gu_out), pick(adapt_down_in), pick(adapt_down_out)

    def own_half(array):
        return lax.dynamic_slice_in_dim(array, side * half, half, 0)

    def other_half(array):
        return lax.dynamic_slice_in_dim(array, (1 - side) * half, half, 0)

    def in_order(own, other):
        return jnp.where(
            side == 0, jnp.concatenate([own, other], axis=0), jnp.concatenate([other, own], axis=0)
        )

    start_pos = place * count
    seg_all = segments[0]
    seg_query = lax.dynamic_slice_in_dim(seg_all, start_pos, count, 0)
    before = jnp.sum((seg_all[None, :] < seg_query[:, None]).astype(jnp.int32), axis=1)
    own_pos = start_pos + jnp.arange(count, dtype=jnp.int32) - before
    cosine, sine_table = rope_tables(own_pos, head_size)
    cosine = cosine[:, None, :]
    sine_table = sine_table[:, None, :]
    tokens_f = wide(tokens[0])
    normed_b = low(rms_norm(tokens_f, gain_in))
    tokens_h = wide(own_half(tokens[0]))
    normed_h, normed_back = jax.vjp(lambda v: rms_norm(v, gain_in), tokens_h)
    code_attn = matmul(normed_b, pick_attn_in)
    query_lin = matmul(normed_b, full_query) + matmul(code_attn[:, :rank], pick_query_out)
    key_lin = matmul(normed_b, full_key) + matmul(code_attn[:, rank : 2 * rank], pick_kv_out[0])
    value_lin = matmul(normed_b, full_value) + matmul(code_attn[:, 2 * rank :], pick_kv_out[1])

    def prepare(query_in, key_in, value_in):
        query_rot = rotate_half(
            rms_norm(query_in.reshape(count, heads, head_size), gain_query), cosine, sine_table
        )
        key_rot = rotate_half(
            rms_norm(key_in.reshape(count, kv_heads, head_size), gain_key), cosine, sine_table
        )
        value_nrm = rms_norm(value_in.reshape(count, kv_heads, head_size), 1.0)
        return (query_rot, key_rot, value_nrm)

    (query_rot, key_rot, value_nrm), prepare_back = jax.vjp(prepare, query_lin, key_lin, value_lin)
    query_b = low(query_rot).reshape(count, kv_heads, group, head_size)
    kv_own = low(jnp.stack([key_rot, value_nrm]))
    kv_prior = shifted(kv_own, "context", 1)
    kv_all = jnp.concatenate([kv_prior, kv_own], axis=1)
    query_pos = start_pos + jnp.arange(count, dtype=jnp.int32)
    key_pos = start_pos - count + jnp.arange(2 * count, dtype=jnp.int32)
    seg_prior = lax.dynamic_slice_in_dim(seg_all, jnp.maximum(start_pos - count, 0), count, 0)
    seg_keys = jnp.concatenate([seg_prior, seg_query], axis=0)
    distance = query_pos[:, None] - key_pos[None, :]
    window_ok = (distance >= 0) & (distance < WINDOW) & (key_pos >= 0)[None, :]
    allowed = (seg_query[:, None] == seg_keys[None, :]) & window_ok
    allowed = allowed[None, None]
    score_scale = 1.0 / math.sqrt(head_size)

    def masked_scores():
        raw_scores = (
            jnp.einsum("lkgd,mkd->kglm", query_b, kv_all[0], preferred_element_type=jnp.float32)
            * score_scale
        )
        return jnp.where(allowed, raw_scores, -1e30)

    scores = masked_scores()
    row_max = jnp.max(scores, axis=-1, keepdims=True)
    exponent = jnp.exp(scores - row_max)
    row_total = jnp.sum(exponent, axis=-1, keepdims=True)
    log_total = row_max + jnp.log(row_total)
    attn_probs = low(exponent / row_total)
    attended = jnp.einsum("kglm,mkd->lkgd", attn_probs, kv_all[1], preferred_element_type=jnp.float32)
    attended_b = low(attended.reshape(count, heads * head_size))
    laurel_mid = low(matmul_t(normed_h, full_left))
    (
        full_output, full_right, full_layer_gate, full_layer_proj, full_gate, full_up, full_down,
        gate_b, up_b, ffn_b, attn_proj, combined, code_out, code_ffn, code_down, down_part,
    ) = fore(
        (w_output, laurel_right, input_gate, input_proj, w_gate, w_up, w_down),
        attended_b, own_half(tokens[0]), laurel_mid,
        pick_out_in.T, pick_out_out, pick_ffn_in.T, pick_gu_out, pick_down_in.T, pick_down_out,
        (gain_in[None], gain_attn[None], gain_laurel[None], gain_pre[None]), shards,
    )
    quarter = half // 2
    bf16, f32 = jnp.bfloat16, jnp.float32
    per_layer_h, cotangent_h = own_half(layer_input[0]), own_half(cotangent[0])
    crowned = []
    for g in range(2):
        theirs = swap(down_part[g * half + quarter : (g + 1) * half])
        output_g, grad_down_g, grad_after_g = rowwise(
            crown_kernel, g, quarter,
            [(down_part, 2 * g), (theirs, 0), (combined, None), (per_layer_h, None), (cotangent_h, None)],
            [full_layer_gate, full_layer_proj, gain_post[None], gain_layer[None]],
            [(width, bf16), (width, bf16), (width, f32)],
        )
        crowned.append((output_g, grad_down_g, grad_after_g, swap(grad_down_g)))
    parted = []
    for g in range(2):
        grad_down_b = jnp.concatenate([crowned[g][1], crowned[g][3]], axis=0)
        parted.append(
            ffn_back(
                g, grad_down_b, gate_b, up_b, code_ffn, code_down, ffn_b, full_down, full_gate, full_up,
                pick_down_in.T, pick_down_out, pick_gu_out, pick_ffn_in.T,
            )
        )
    term_gate_out, term_up_out, term_down_in, term_ffn_in, term_down_out = (
        parted[0][i] + parted[1][i] for i in range(1, 6)
    )
    mark = jnp.where(
        (lax.broadcasted_iota(jnp.int32, (rank, 512), 1) == chosen) & (place == 0), 1.0, 0.0
    )
    early = share(
        jnp.concatenate(
            [term_gate_out, term_up_out, term_down_in, term_ffn_in[:rank], term_ffn_in[rank:], term_down_out, mark],
            axis=1,
        )
    )
    turned_back = []
    for g in range(2):
        part = parted[g][0]
        turned_back.append(
            rowwise(
                comb_back_kernel, g, quarter,
                [
                    (part, 0), (swap(part[quarter:]), 0), (crowned[g][2], 0), (combined, None),
                    (attn_proj, None), (laurel_mid, None),
                ],
                [full_left, full_right, gain_pre[None], gain_attn[None], gain_laurel[None]],
                [(width, bf16), (width, f32), (width, f32)],
            )
        )
    grad_inputs = jnp.concatenate([turned_back[0][1], turned_back[1][1]], axis=0)
    grad_normed = jnp.concatenate([turned_back[0][2], turned_back[1][2]], axis=0)
    grad_attn_b = in_order(
        jnp.concatenate([turned_back[0][0], turned_back[1][0]], axis=0),
        jnp.concatenate([swap(turned_back[0][0]), swap(turned_back[1][0])], axis=0),
    )
    output_own = jnp.concatenate([crowned[0][0], crowned[1][0]], axis=0)
    layer_output = in_order(output_own, swap(output_own))
    code_out_back = matmul_t(grad_attn_b, pick_out_out)
    term_out_out = outer(code_out, grad_attn_b)
    term_out_in = outer(code_out_back, attended_b)
    grad_attended = low(matmul_t(grad_attn_b, full_output) + matmul_t(code_out_back, pick_out_in))
    grad_heads = grad_attended.reshape(count, kv_heads, group, head_size)
    recomputed = jnp.exp(masked_scores() - log_total)
    grad_probs = jnp.einsum("lkgd,mkd->kglm", grad_heads, kv_all[1], preferred_element_type=jnp.float32)
    grad_scores = low(
        recomputed * (grad_probs - jnp.sum(recomputed * grad_probs, axis=-1, keepdims=True))
    )
    grad_query = (
        jnp.einsum("kglm,mkd->lkgd", grad_scores, kv_all[0], preferred_element_type=jnp.float32)
        * score_scale
    )
    grad_keys = (
        jnp.einsum("kglm,lkgd->mkd", grad_scores, query_b, preferred_element_type=jnp.float32)
        * score_scale
    )
    grad_values = jnp.einsum(
        "kglm,lkgd->mkd", low(recomputed), grad_heads, preferred_element_type=jnp.float32
    )
    grad_kv = jnp.stack([grad_keys, grad_values])
    grad_kv_later = wide(shifted(low(grad_kv[:, :count]), "context", -1))
    grad_kv_own = grad_kv[:, count:] + grad_kv_later
    grad_qlin, grad_klin, grad_vlin = prepare_back(
        (grad_query.reshape(count, heads, head_size), grad_kv_own[0], grad_kv_own[1])
    )
    grad_qlin_b = low(grad_qlin)
    early, grad_qlin_b = lax.optimization_barrier((early, grad_qlin_b))
    grad_klin_b = low(grad_klin)
    grad_vlin_b = low(grad_vlin)
    code_attn_back = jnp.concatenate(
        [
            matmul_t(grad_qlin_b, pick_query_out),
            matmul_t(grad_klin_b, pick_kv_out[0]),
            matmul_t(grad_vlin_b, pick_kv_out[1]),
        ],
        axis=1,
    )
    term_query_out = outer(code_attn[:, :rank], grad_qlin_b)
    term_key_out = outer(code_attn[:, rank : 2 * rank], grad_klin_b)
    term_value_out = outer(code_attn[:, 2 * rank :], grad_vlin_b)
    term_attn_in = outer(code_attn_back, normed_b)
    late = share(
        jnp.concatenate(
            [
                term_out_in, term_out_out, term_query_out, term_key_out, term_value_out,
                term_attn_in[:rank], term_attn_in[rank : 2 * rank], term_attn_in[2 * rank :],
            ],
            axis=1,
        )
    )
    grad_normed_part = low(
        matmul_t(grad_qlin_b, full_query)
        + matmul_t(grad_klin_b, full_key)
        + matmul_t(grad_vlin_b, full_value)
        + matmul_t(code_attn_back, pick_attn_in)
    )
    grad_normed = grad_normed + wide(own_half(grad_normed_part)) + wide(swap(other_half(grad_normed_part)))
    grad_own = low(grad_inputs + normed_back(grad_normed)[0])
    input_grad = in_order(grad_own, swap(grad_own))

    at = 0

    def take(packed, columns):
        nonlocal at
        at += columns
        return wide(packed[..., at - columns : at])

    def joined(packed, columns):
        both = take(packed, columns)
        return jnp.concatenate([both[0], both[1]], axis=-1)

    def added(packed, columns):
        both = take(packed, columns)
        return both[0] + both[1]

    gate_out, up_out, down_in = (joined(early, hidden_here) for _ in range(3))
    ffn_in = [added(early, width) for _ in range(2)]
    down_out = added(early, width)
    adapters = adapt_attn_in.shape[0]
    marks = wide(early[0, :, 0, at : at + adapters])
    at = 0
    out_in = joined(late, heads * head_size)
    out_out = added(late, width)
    query_out = joined(late, heads * head_size)
    key_out, value_out = (joined(late, kv_heads * head_size) for _ in range(2))
    attn_in = [added(late, width) for _ in range(3)]

    def tables(terms):
        return sum(
            marks[s].reshape((adapters,) + (1,) * (terms.ndim - 1)) * terms[s][None] for s in range(shards)
        )

    def turned(terms):
        return tables(terms).transpose(0, 2, 1)

    return (
        layer_output[None],
        input_grad[None],
        turned(jnp.concatenate(attn_in, axis=1)),
        tables(query_out),
        tables(jnp.stack([key_out, value_out], axis=1)),
        turned(out_in),
        tables(out_out),
        turned(jnp.concatenate(ffn_in, axis=1)),
        tables(jnp.stack([gate_out, up_out], axis=1)),
        turned(down_in),
        tables(down_out),
    )


def solution(mesh):
    in_specs = (
        P("shard", "context", None),
        P("shard", "context", None),
        P("shard", None),
        P("shard"),
        P("shard", "context", None),
        P("shard", "tensor"),
        P("shard", "tensor"),
        P("shard", "tensor"),
        P("tensor", "shard"),
        P("shard", "tensor"),
        P("shard", "tensor"),
        P("tensor", "shard"),
        P("shard", None),
        P(None, "shard"),
        P("shard", None),
        P(None, "shard"),
        P(),
        P(),
        P(),
        P(),
        P(),
        P(),
        P(),
        P(),
        P(),
        P(None, None, "tensor"),
        P(None, None, None, "tensor"),
        P(None, "tensor", None),
        P(),
        P(),
        P(None, None, None, "tensor"),
        P(None, "tensor", None),
        P(),
    )
    out_specs = (
        P("shard", "context", None),
        P("shard", "context", None),
        P(),
        P(),
        P(),
        P(),
        P(),
        P(),
        P(),
        P(),
        P(),
    )
    return jax.shard_map(body, mesh=mesh, in_specs=in_specs, out_specs=out_specs, check_vma=False)
```

```python
import functools
import math

import jax
import jax.numpy as jnp
from jax import lax
from jax.experimental import pallas as pl
from jax.experimental.pallas import tpu as pltpu
from jax.sharding import PartitionSpec as P

WINDOW = 512
EPSILON = 1e-06
ROOT_HALF = 0.7071067811865476
GELU_SCALE = math.sqrt(2.0 / math.pi)
GELU_CUBE = 0.044715

MESH = pl.DeviceIdType.MESH


def shifted(array, axis, by):
    count = lax.axis_size(axis)
    pairs = [(i, i + by) for i in range(count) if 0 <= i + by < count]
    return lax.ppermute(array, axis, pairs)


def swap(array):
    return lax.ppermute(array, "tensor", [(0, 1), (1, 0)])


def rms_norm(values, scaling):
    return values * lax.rsqrt(jnp.mean(values * values, axis=-1, keepdims=True) + EPSILON) * scaling


def gelu_tanh(values):
    return jax.nn.gelu(values, approximate=True)


def rotate_half(values, cosine, sine_table):
    middle = values.shape[-1] // 2
    former = values[..., :middle]
    latter = values[..., middle:]
    return jnp.concatenate(
        [former * cosine - latter * sine_table, latter * cosine + former * sine_table], axis=-1
    )


def rope_tables(positions, head_size):
    frequency = jnp.exp(
        jnp.arange(head_size // 2, dtype=jnp.float32) * (-2.0 * math.log(10000.0) / head_size)
    )
    angles = positions.astype(jnp.float32)[..., None] * frequency
    return (jnp.cos(angles), jnp.sin(angles))


def low(values):
    return values.astype(jnp.bfloat16)


def wide(values):
    return values.astype(jnp.float32)


def matmul(left_op, right_op):
    return jnp.dot(low(left_op), low(right_op), preferred_element_type=jnp.float32)


def matmul_t(left_op, right_op):
    return lax.dot_general(
        low(left_op), low(right_op), (((1,), (1,)), ((), ())), preferred_element_type=jnp.float32
    )


def outer(left_op, right_op):
    return lax.dot_general(
        low(left_op), low(right_op), (((0,), (0,)), ((), ())), preferred_element_type=jnp.float32
    )


def dot(left, right):
    return lax.dot_general(left, right, (((1,), (0,)), ((), ())), preferred_element_type=jnp.float32)


def dot_t(left, right):
    return lax.dot_general(left, right, (((1,), (1,)), ((), ())), preferred_element_type=jnp.float32)


def dot_o(left, right):
    return lax.dot_general(left, right, (((0,), (0,)), ((), ())), preferred_element_type=jnp.float32)


def row_mean(values):
    return jnp.mean(values, axis=-1, keepdims=True)


def inverse_rms(values):
    return lax.rsqrt(row_mean(values * values) + EPSILON)


def rms_back(values, inverse, scaled):
    return inverse * scaled - values * (inverse * inverse * inverse * row_mean(values * scaled))


def gelu_parts(values):
    squared = values * values
    bend = jnp.tanh(GELU_SCALE * values * (1.0 + GELU_CUBE * squared))
    rise = 0.5 * (1.0 + bend)
    slope = rise + 0.5 * values * (1.0 - bend * bend) * (GELU_SCALE * (1.0 + 3.0 * GELU_CUBE * squared))
    return values * rise, slope


def greet_all(shards, places, ends):
    z = lax.axis_index("shard")
    barrier = pltpu.get_barrier_semaphore()

    def signal(place):
        pl.semaphore_signal(barrier, inc=1, device_id=place, device_id_type=MESH)

    for place in places:
        signal(place)
    peers = len(places)
    if ends:

        @pl.when(z > 0)
        def _():
            signal({"shard": z - 1})

        @pl.when(z < shards - 1)
        def _():
            signal({"shard": z + 1})

        peers = peers + lax.div(z + shards - 1, shards) + lax.div(2 * shards - 2 - z, shards)
    pl.semaphore_wait(barrier, peers)


def context_partners():
    c = lax.axis_index("context")
    return lax.rem(c + 2, 4), c + 1 - 2 * lax.rem(c, 2)


def sharer(pack, whole, inbox, turn_in, turn_out, piece, semaphores, shards):
    (
        pre_send, pre_recv, z_send, z_recv, x_send, x_recv, y_send, y_recv, near_send, near_recv,
        far_send, far_recv, keep_sem,
    ) = semaphores
    z, c, side = (lax.axis_index(a) for a in ("shard", "context", "tensor"))
    across, beside = context_partners()
    opposite = lax.rem(beside + 2, 4)
    columns = piece.shape[1]

    def cols(q):
        return pl.ds(pl.multiple_of(q * columns, 128), columns)

    def region(t, s, q):
        return whole.at[t, s, :, cols(q)]

    def copy(source, target, send, recv, place):
        return pltpu.make_async_remote_copy(
            src_ref=source, dst_ref=target, send_sem=send, recv_sem=recv, device_id=place, device_id_type=MESH
        )

    def halves(k):
        q = beside if k == 0 else opposite
        return copy(pack.at[:, cols(q)], inbox.at[k], pre_send.at[k], pre_recv.at[k], {"context": beside})

    def turned():
        return copy(turn_out, turn_in, pre_send.at[2], pre_recv.at[2], {"context": across})

    def z_copy(s, source, sender, by):
        return copy(source, region(side, s, c), z_send.at[sender], z_recv.at[s], {"shard": z + by})

    def passed(s, by):
        return z_copy(s, region(side, s, c), s, by)

    def x_copy(s, source, t):
        return copy(source, region(t, s, c), x_send.at[s], x_recv.at[s], {"tensor": 1 - side})

    def y_copy(t, s, source, q):
        return copy(source, region(t, s, q), y_send.at[t, s], y_recv.at[t, s], {"context": across})

    def near_copy(t, s, source, q):
        return copy(source, region(t, s, q), near_send.at[t, s], near_recv.at[t, s], {"context": beside})

    def far_copy(t, s, q):
        at = region(t, s, q)
        return copy(at, at, far_send.at[t, s], far_recv.at[t, s], {"context": beside})

    def keep():
        return pltpu.make_async_copy(piece, region(side, z, c), keep_sem)

    def start():
        for k in range(2):
            halves(k).start()

    def turn():
        for k in range(2):
            halves(k).wait_recv()
        turn_out[...] = low(pack[:, cols(across)] + inbox[1])
        turned().start()

    def settle():
        turned().wait_recv()
        piece[...] = low(pack[:, cols(c)] + inbox[0] + wide(turn_in[...]))
        keep().start()

        @pl.when(z < shards - 1)
        def _():
            z_copy(z, piece, z, 1).start()

        @pl.when(z > 0)
        def _():
            z_copy(z, piece, shards, -1).start()

        x_copy(z, piece, side).start()
        y_copy(side, z, piece, c).start()
        near_copy(side, z, piece, c).start()

    def hand_on(s):
        at = region(side, s, c)
        x_copy(s, at, side).start()
        y_copy(side, s, at, c).start()
        near_copy(side, s, at, c).start()

    def hop(d):
        @pl.when(z >= d)
        def _():
            s = z - d
            passed(s, 1).wait_recv()

            @pl.when(z < shards - 1)
            def _():
                passed(s, 1).start()

            hand_on(s)

        @pl.when(z + d <= shards - 1)
        def _():
            s = z + d
            passed(s, -1).wait_recv()

            @pl.when(z > 0)
            def _():
                passed(s, -1).start()

            hand_on(s)

    def hops(first):
        lax.fori_loop(first, shards, lambda d, carry: (hop(d), carry)[1], 0)

    def cross_over():
        def one(s, carry):
            at = region(1 - side, s, c)
            x_copy(s, at, 1 - side).wait_recv()
            y_copy(1 - side, s, at, c).start()
            near_copy(1 - side, s, at, c).start()
            return carry

        lax.fori_loop(0, shards, one, 0)

    def every(act):
        def one(s, carry):
            for t in range(2):
                act(t, s)
            return carry

        lax.fori_loop(0, shards, one, 0)

    def spread():
        def act(t, s):
            y_copy(t, s, region(t, s, across), across).wait_recv()
            far_copy(t, s, across).start()

        every(act)

    def finish():
        def act(t, s):
            near_copy(t, s, region(t, s, beside), beside).wait_recv()
            far_copy(t, s, opposite).wait_recv()
            y_copy(t, s, region(t, s, c), c).wait_send()
            near_copy(t, s, region(t, s, c), c).wait_send()
            far_copy(t, s, across).wait_send()

        every(act)

        def one(s, carry):
            x_copy(s, region(side, s, c), side).wait_send()

            @pl.when((s < z) & (z < shards - 1))
            def _():
                passed(s, 1).wait_send()

            @pl.when((s > z) & (z > 0))
            def _():
                passed(s, -1).wait_send()

            return carry

        lax.fori_loop(0, shards, one, 0)

        @pl.when(z < shards - 1)
        def _():
            z_copy(z, piece, z, 1).wait_send()

        @pl.when(z > 0)
        def _():
            z_copy(z, piece, shards, -1).wait_send()

        for k in range(2):
            halves(k).wait_send()
        turned().wait_send()
        keep().wait()

    return start, turn, settle, hop, hops, cross_over, spread, finish


def sharer_scratch(rows, columns, shards):
    part = columns // 4
    dma = pltpu.SemaphoreType.DMA
    return [
        pltpu.VMEM((2, rows, part), jnp.float32),
        pltpu.VMEM((rows, part), jnp.bfloat16),
        pltpu.VMEM((rows, part), jnp.bfloat16),
        pltpu.VMEM((rows, part), jnp.bfloat16),
        dma((3,)), dma((3,)), dma((shards + 1,)), dma((shards,)), dma((shards,)), dma((shards,)),
        dma((2, shards)), dma((2, shards)), dma((2, shards)), dma((2, shards)), dma((2, shards)), dma((2, shards)),
        dma,
    ]


def tail_kernel(
    shards,
    grad_query, grad_key, grad_value, w_query, w_key, w_value, code_attn, normed, query_out, kv_out, attn_in,
    out_in_term, out_out_term, tokens, gain_in, grad_comb, grad_normed,
    input_grad_out, whole,
    pack, mine, sent, got, result, send_sem, recv_sem, keep_sem, *shared,
):
    side = lax.axis_index("tensor")
    partner = {"tensor": 1 - side}
    across, beside = context_partners()
    count, width = normed.shape
    half = count // 2
    quarter = half // 2
    rank = query_out.shape[0]
    start, turn, settle, hop, hops, cross_over, spread, finish = sharer(
        pack, whole, shared[0], shared[1], shared[2], shared[3], shared[4:], shards
    )
    greet_all(shards, [partner, {"context": across}, {"context": beside}], True)
    parts = ((grad_query, w_query, query_out[...]), (grad_key, w_key, kv_out[0]), (grad_value, w_value, kv_out[1]))
    at = 0

    def put(term):
        nonlocal at
        pack[:, at : at + term.shape[1]] = term
        at += term.shape[1]

    put(out_in_term[...])
    put(out_out_term[...])
    backs = []
    for i, (grad, _, table) in enumerate(parts):
        put(dot_o(code_attn[:, i * rank : (i + 1) * rank], grad[...]))
        backs.append(low(dot_t(grad[...], table)))
    for back in backs:
        put(dot_o(back, normed[...]))
    start()

    def product(here):
        total = dot_t(grad_query[here, :], w_query[...])
        total += dot_t(grad_key[here, :], w_key[...]) + dot_t(grad_value[here, :], w_value[...])
        for i, (grad, _, table) in enumerate(parts):
            back = low(dot_t(grad[here, :], table))
            total += dot(back, attn_in[i * rank : (i + 1) * rank, :])
        return total

    def send(source, target, k):
        return pltpu.make_async_remote_copy(
            src_ref=source, dst_ref=target, send_sem=send_sem.at[k], recv_sem=recv_sem.at[k],
            device_id=partner, device_id_type=MESH,
        )

    def rows(k):
        return pl.ds(k * quarter, quarter)

    def rows_of(owner, k):
        return pl.ds(pl.multiple_of(owner * half + k * quarter, quarter), quarter)

    swaps = []
    for k in range(2):
        sent[rows(k), :] = low(product(rows_of(1 - side, k)))
        swaps.append(send(sent.at[rows(k), :], got.at[rows(k), :], k))
        swaps[k].start()
    turn()
    for k in range(2):
        mine[rows(k), :] = product(rows_of(side, k))
        if k == 0:
            settle()
    ends = []
    for k in range(2):
        swaps[k].wait_recv()
        here = rows(k)
        grad = (grad_normed[here, :] + mine[here, :] + wide(got[here, :])) * gain_in[...]
        token = wide(tokens[here, :])
        there = rows_of(side, k)
        result[there, :] = low(grad_comb[here, :] + rms_back(token, inverse_rms(token), grad))
        ends.append(send(result.at[there, :], result.at[there, :], 2 + k))
        ends[k].start()
        if k == 0:
            hop(1)
    hops(2)
    cross_over()
    spread()
    for end in ends:
        end.wait()
    keep = pltpu.make_async_copy(result, input_grad_out, keep_sem)
    keep.start()
    for swap_part in swaps:
        swap_part.wait_send()
    finish()
    keep.wait()


def tail(arrays, shards):
    count, width = arrays[7].shape
    rank = arrays[8].shape[0]
    half = count // 2
    columns = sum(a.shape[1] for a in arrays[:3]) + arrays[11].shape[1] + arrays[12].shape[1] + 3 * width
    bf16, f32 = jnp.bfloat16, jnp.float32
    anywhere, vmem = pl.BlockSpec(memory_space=pl.ANY), pl.BlockSpec(memory_space=pltpu.VMEM)
    return pl.pallas_call(
        functools.partial(tail_kernel, shards),
        out_shape=[
            jax.ShapeDtypeStruct((count, width), bf16),
            jax.ShapeDtypeStruct((2, shards, rank, columns), bf16),
        ],
        in_specs=[vmem] * len(arrays),
        out_specs=[anywhere] * 2,
        scratch_shapes=[
            pltpu.VMEM((rank, columns), f32),
            pltpu.VMEM((half, width), f32),
            pltpu.VMEM((half, width), bf16),
            pltpu.VMEM((half, width), bf16),
            pltpu.VMEM((count, width), bf16),
            pltpu.SemaphoreType.DMA((4,)),
            pltpu.SemaphoreType.DMA((4,)),
            pltpu.SemaphoreType.DMA,
        ]
        + sharer_scratch(rank, columns, shards),
        compiler_params=pltpu.CompilerParams(
            collective_id=3, has_side_effects=True, vmem_limit_bytes=56 * 2**20
        ),
    )(*arrays)


def aft_kernel(
    shards, block, strip,
    full_gate, full_up, full_down, gate_in, up_in,
    part, combined, per_layer, cotangent, lgate, lproj, code_ffn, code_down, ffn, down_in, down_out, gu_out, ffn_in,
    attn_proj, laurel_mid, left, right, mark, gain_post, gain_layer, gain_pre, gain_attn, gain_laurel,
    grad_attn_out, whole, output, grad_comb, grad_normed, pack,
    got, grad, grad_gate, grad_up, down_w, gate_v, up_v, gate_w, up_w, mine, sent, came, attn, back_codes, ffn_codes,
    fetch_sem, strip_sem, keep_sem, send_sem, recv_sem, *shared,
):
    side = lax.axis_index("tensor")
    partner = {"tensor": 1 - side}
    across, beside = context_partners()
    greet_all(shards, [partner, {"context": across}, {"context": beside}], True)
    start, turn, settle, hop, hops, cross_over, spread, finish = sharer(
        pack, whole, shared[0], shared[1], shared[2], shared[3], shared[4:], shards
    )
    count, width = grad.shape
    half = count // 2
    quarter = half // 2
    rank = down_in.shape[0]
    hidden = grad_gate.shape[1]
    steps = hidden // block
    strips = width // strip

    def send(source, target, k):
        return pltpu.make_async_remote_copy(
            src_ref=source, dst_ref=target, send_sem=send_sem.at[k], recv_sem=recv_sem.at[k],
            device_id=partner, device_id_type=MESH,
        )

    def rows(k):
        return pl.ds(k * quarter, quarter)

    down_swaps = [send(part.at[rows(2 + k), :], got.at[rows(k), :], k) for k in range(2)]
    grad_swaps = [send(grad.at[rows(k), :], grad.at[rows(2 + k), :], 2 + k) for k in range(2)]
    for swap_down in down_swaps:
        swap_down.start()

    def fetches(t):
        slot, j = lax.rem(t, 2), lax.rem(t, steps)
        at = pl.ds(pl.multiple_of(j * block, block), block)
        here = pl.ds(pl.multiple_of(lax.div(t, steps) * half, half), half)
        return (
            pltpu.make_async_copy(full_down.at[at, :], down_w.at[slot], fetch_sem.at[0, slot]),
            pltpu.make_async_copy(gate_in.at[here, at], gate_v.at[slot], fetch_sem.at[1, slot]),
            pltpu.make_async_copy(up_in.at[here, at], up_v.at[slot], fetch_sem.at[2, slot]),
        )

    def strip_fetches(k):
        slot = lax.rem(k, 2)
        at = pl.ds(pl.multiple_of(k * strip, strip), strip)
        return (
            pltpu.make_async_copy(full_gate.at[at, :], gate_w.at[slot], strip_sem.at[0, slot]),
            pltpu.make_async_copy(full_up.at[at, :], up_w.at[slot], strip_sem.at[1, slot]),
        )

    for fetch in fetches(0) + strip_fetches(0):
        fetch.start()
    pack[...] = jnp.zeros_like(pack)
    ffn_codes[...] = jnp.zeros_like(ffn_codes)

    for k in range(2):
        down_swaps[k].wait_recv()
        at = rows(k)
        down = wide(part[at, :]) + wide(got[at, :])
        down_inverse = inverse_rms(down)
        after = combined[at, :] + down * down_inverse * gain_post[...]
        mixing = wide(per_layer[at, :])
        act, slope = gelu_parts(dot(low(after), lgate[...]))
        proj = dot(low(act * mixing), lproj[...])
        proj_inverse = inverse_rms(proj)
        output[at, :] = low(after + proj * proj_inverse * gain_layer[...])
        top = wide(cotangent[at, :])
        grad_proj = rms_back(proj, proj_inverse, top * gain_layer[...])
        grad_mix = dot_t(low(grad_proj), lproj[...]) * mixing * slope
        top = top + dot_t(low(grad_mix), lgate[...])
        grad_comb[at, :] = top
        grad[at, :] = low(rms_back(down, down_inverse, top * gain_post[...]))
        grad_swaps[k].start()
        back_codes[at, :] = low(dot_t(grad[at, :], down_out[...]))

    def level(t, carry):
        @pl.when(t + 1 < 2 * steps)
        def _():
            for fetch in fetches(t + 1):
                fetch.start()

        @pl.when(t == steps)
        def _():
            for k in range(2):
                grad_swaps[k].wait_recv()
            back_codes[half:, :] = low(dot_t(grad[half:, :], down_out[...]))

        slot, j = lax.rem(t, 2), lax.rem(t, steps)
        at = pl.ds(pl.multiple_of(j * block, block), block)
        here = pl.ds(pl.multiple_of(lax.div(t, steps) * half, half), half)
        for fetch in fetches(t):
            fetch.wait()
        back = back_codes[here, :]
        hidden_grad = dot_t(grad[here, :], down_w[slot]) + dot(back, down_in[:, at])
        up_now = wide(up_v[slot])
        act, slope = gelu_parts(wide(gate_v[slot]))
        grad_g = low(hidden_grad * up_now * slope)
        grad_u = low(hidden_grad * act)
        grad_gate[here, at] = grad_g
        grad_up[here, at] = grad_u
        ffn_codes[0, here, :] += dot_t(grad_g, gu_out[0, :, at])
        ffn_codes[1, here, :] += dot_t(grad_u, gu_out[1, :, at])
        codes = code_ffn[here, :]

        def put(i, term):
            pack[:, pl.ds(pl.multiple_of(i * hidden + j * block, block), block)] += term

        put(0, dot_o(codes[:, :rank], grad_g))
        put(1, dot_o(codes[:, rank:], grad_u))
        put(2, dot_o(back, low(act * up_now)))
        return carry

    lax.fori_loop(0, 2 * steps, level, 0)
    base = 3 * hidden
    pack[:, base : base + width] = dot_o(low(ffn_codes[0]), ffn[...])
    pack[:, base + width : base + 2 * width] = dot_o(low(ffn_codes[1]), ffn[...])
    pack[:, base + 2 * width : base + 3 * width] = dot_o(code_down[...], grad[...])
    pack[:, base + 3 * width :] = mark[...]
    start()

    def strip_send(k):
        return send(sent.at[k], came.at[k], 4 + k)

    def cross(k, carry):
        @pl.when(k + 1 < strips)
        def _():
            for fetch in strip_fetches(k + 1):
                fetch.start()

        slot = lax.rem(k, 2)
        at = pl.ds(pl.multiple_of(k * strip, strip), strip)
        for fetch in strip_fetches(k):
            fetch.wait()
        result = (
            dot_t(grad_gate[...], gate_w[slot])
            + dot_t(grad_up[...], up_w[slot])
            + dot(low(ffn_codes[0]), ffn_in[:rank, at])
            + dot(low(ffn_codes[1]), ffn_in[rank:, at])
        )
        sent[k] = low(result[half:])
        strip_send(k).start()
        mine[:, at] = result[:half]
        for when, act in ((1, turn), (2, settle), (3, lambda: hop(1)), (4, lambda: hop(2)), (5, lambda: hops(3))):
            pl.when(k == when)(act)
        return carry

    lax.fori_loop(0, strips, cross, 0)
    cross_over()

    def add(k, carry):
        at = pl.ds(pl.multiple_of(k * strip, strip), strip)
        strip_send(k).wait_recv()
        mine[:, at] += wide(came[k])
        return carry

    lax.fori_loop(0, strips, add, 0)
    attn_swaps = []
    for k in range(2):
        at = rows(k)
        comb = combined[at, :]
        top = (grad_comb[at, :] + rms_back(comb, inverse_rms(comb), mine[at, :] * gain_pre[...])) * ROOT_HALF
        grad_comb[at, :] = top
        proj = attn_proj[at, :]
        there = pl.ds(pl.multiple_of(side * half + k * quarter, quarter), quarter)
        attn[there, :] = low(rms_back(proj, inverse_rms(proj), top * gain_attn[...]))
        attn_swaps.append(send(attn.at[there, :], attn.at[there, :], 4 + strips + k))
        attn_swaps[k].start()
        end = dot(laurel_mid[at, :], right[...])
        grad_end = low(rms_back(end, inverse_rms(end), top * gain_laurel[...]))
        grad_normed[at, :] = top + dot(low(dot_t(grad_end, right[...])), left[...])
    spread()
    for swap_attn in attn_swaps:
        swap_attn.wait()
    keep = pltpu.make_async_copy(attn, grad_attn_out, keep_sem)
    keep.start()
    for k in range(2):
        down_swaps[k].wait_send()
        grad_swaps[k].wait_send()

    def flush(k, carry):
        strip_send(k).wait_send()
        return carry

    lax.fori_loop(0, strips, flush, 0)
    finish()
    keep.wait()


def aft(weights, kept, arrays, shards):
    full_gate = weights[0]
    part, combined, per_layer = arrays[:3]
    count, width = part.shape
    hidden = full_gate.shape[1]
    half = count // 2
    rank = arrays[9].shape[0]
    block, strip = min(512, hidden), 256
    strips = width // strip
    columns = 3 * hidden + 3 * width + arrays[17].shape[1]
    bf16, f32 = jnp.bfloat16, jnp.float32
    shape = jax.ShapeDtypeStruct
    anywhere, vmem = pl.BlockSpec(memory_space=pl.ANY), pl.BlockSpec(memory_space=pltpu.VMEM)
    return pl.pallas_call(
        functools.partial(aft_kernel, shards, block, strip),
        out_shape=[
            shape((count, width), bf16),
            shape((2, shards, rank, columns), bf16),
            shape((half, width), bf16),
            shape((half, width), f32),
            shape((half, width), f32),
        ],
        in_specs=[anywhere] * 5 + [vmem] * len(arrays),
        out_specs=[anywhere] * 2 + [vmem] * 3,
        scratch_shapes=[
            pltpu.VMEM((rank, columns), f32),
            pltpu.VMEM((half, width), bf16),
            pltpu.VMEM((count, width), bf16),
            pltpu.VMEM((count, hidden), bf16),
            pltpu.VMEM((count, hidden), bf16),
            pltpu.VMEM((2, block, width), bf16),
            pltpu.VMEM((2, half, block), bf16),
            pltpu.VMEM((2, half, block), bf16),
            pltpu.VMEM((2, strip, hidden), bf16),
            pltpu.VMEM((2, strip, hidden), bf16),
            pltpu.VMEM((half, width), f32),
            pltpu.VMEM((strips, half, strip), bf16),
            pltpu.VMEM((strips, half, strip), bf16),
            pltpu.VMEM((count, width), bf16),
            pltpu.VMEM((count, rank), bf16),
            pltpu.VMEM((2, count, rank), f32),
            pltpu.SemaphoreType.DMA((3, 2)),
            pltpu.SemaphoreType.DMA((2, 2)),
            pltpu.SemaphoreType.DMA,
            pltpu.SemaphoreType.DMA((6 + strips,)),
            pltpu.SemaphoreType.DMA((6 + strips,)),
        ]
        + sharer_scratch(rank, columns, shards),
        compiler_params=pltpu.CompilerParams(
            collective_id=2, has_side_effects=True, vmem_limit_bytes=60 * 2**20
        ),
        cost_estimate=pl.CostEstimate(
            flops=6 * count * width * hidden, bytes_accessed=8 * width * hidden, transcendentals=count * hidden
        ),
    )(*weights, *kept, *arrays)


def mover(sources, fulls, semaphores, shards):
    z_recv, y_recv, near_recv, far_recv, z_send, y_send, near_send, far_send = semaphores
    z, c = lax.axis_index("shard"), lax.axis_index("context")
    across = lax.rem(c + 2, 4)
    beside = c + 1 - 2 * lax.rem(c, 2)

    def greet(also=()):
        barrier = pltpu.get_barrier_semaphore()

        def signal(place):
            pl.semaphore_signal(barrier, inc=1, device_id=place, device_id_type=MESH)

        signal({"context": across})
        signal({"context": beside})
        for place in also:
            signal(place)

        @pl.when(z > 0)
        def _():
            signal({"shard": z - 1})

        @pl.when(z < shards - 1)
        def _():
            signal({"shard": z + 1})

        peers = 2 + len(also) + lax.div(z + shards - 1, shards) + lax.div(2 * shards - 2 - z, shards)
        pl.semaphore_wait(barrier, peers)

    def region(piece, s, q):
        _, item, axis, row, rows, col, cols = piece
        rows_here, cols_here = sources[item].shape
        part = rows // 4
        if axis == 0:
            return fulls[item].at[
                pl.ds(pl.multiple_of(s * rows_here + row + q * part, 16), part),
                pl.ds(pl.multiple_of(col, 128), cols),
            ]
        return fulls[item].at[
            pl.ds(pl.multiple_of(row + q * part, 16), part),
            pl.ds(pl.multiple_of(s * cols_here + col, 128), cols),
        ]

    def own(piece):
        _, item, axis, row, rows, col, cols = piece
        part = rows // 4
        return sources[item].at[
            pl.ds(pl.multiple_of(row + c * part, 16), part), pl.ds(pl.multiple_of(col, 128), cols)
        ]

    def copy(source, target, send, recv, place):
        return pltpu.make_async_remote_copy(
            src_ref=source, dst_ref=target, send_sem=send, recv_sem=recv, device_id=place, device_id_type=MESH
        )

    def along(piece, s, source, sender, by):
        slot = piece[0]
        return copy(source, region(piece, s, c), z_send.at[slot, sender], z_recv.at[slot, s], {"shard": z + by})

    def passed(piece, s, by):
        return along(piece, s, region(piece, s, c), s, by)

    def y_copy(piece, s, q):
        at = region(piece, s, q)
        return copy(at, at, y_send.at[piece[0], s], y_recv.at[piece[0], s], {"context": across})

    def near_copy(piece, s, q):
        at = region(piece, s, q)
        return copy(at, at, near_send.at[piece[0], s], near_recv.at[piece[0], s], {"context": beside})

    def far_copy(piece, s, q):
        at = region(piece, s, q)
        return copy(at, at, far_send.at[piece[0], s], far_recv.at[piece[0], s], {"context": beside})

    def begin(pieces):
        @pl.when(z < shards - 1)
        def _():
            for piece in pieces:
                along(piece, z, own(piece), z, 1).start()

        @pl.when(z > 0)
        def _():
            for piece in pieces:
                along(piece, z, own(piece), shards, -1).start()

    def relay(pieces, first=1, last=None):
        def hop(d, carry):
            @pl.when(z >= d)
            def _():
                s = z - d
                for piece in pieces:
                    passed(piece, s, 1).wait_recv()

                    @pl.when(z < shards - 1)
                    def _(piece=piece):
                        passed(piece, s, 1).start()

                    y_copy(piece, s, c).start()
                    near_copy(piece, s, c).start()

            @pl.when(z + d <= shards - 1)
            def _():
                s = z + d
                for piece in pieces:
                    passed(piece, s, -1).wait_recv()

                    @pl.when(z > 0)
                    def _(piece=piece):
                        passed(piece, s, -1).start()

                    y_copy(piece, s, c).start()
                    near_copy(piece, s, c).start()

            return carry

        last = shards - 1 if last is None else last
        if first == last:
            hop(first, 0)
        else:
            lax.fori_loop(first, last + 1, hop, 0)

    def others(pieces, act):
        def one(d, carry):
            for piece in pieces:
                act(piece, lax.rem(z + d, shards))
            return carry

        lax.fori_loop(1, shards, one, 0)

    def spread(pieces):
        def act(piece, s):
            y_copy(piece, s, across).wait_recv()
            far_copy(piece, s, across).start()

        others(pieces, act)

    def finish(pieces):
        def act(piece, s):
            near_copy(piece, s, beside).wait_recv()
            far_copy(piece, s, lax.rem(beside + 2, 4)).wait_recv()

        others(pieces, act)

    def flush(pieces):
        @pl.when(z < shards - 1)
        def _():
            for piece in pieces:
                along(piece, z, own(piece), z, 1).wait_send()

        @pl.when(z > 0)
        def _():
            for piece in pieces:
                along(piece, z, own(piece), shards, -1).wait_send()

        def act(piece, s):
            y_copy(piece, s, c).wait_send()
            near_copy(piece, s, c).wait_send()
            far_copy(piece, s, across).wait_send()

            @pl.when((s < z) & (z < shards - 1))
            def _():
                passed(piece, s, 1).wait_send()

            @pl.when((s > z) & (z > 0))
            def _():
                passed(piece, s, -1).wait_send()

        others(pieces, act)

    def own_place(item, axis):
        rows_here, cols_here = sources[item].shape
        if axis == 0:
            return fulls[item].at[pl.ds(pl.multiple_of(z * rows_here, 16), rows_here), :]
        return fulls[item].at[:, pl.ds(pl.multiple_of(z * cols_here, 128), cols_here)]

    return greet, begin, relay, spread, finish, flush, own_place


def mover_semaphores(slots, shards):
    table = pltpu.SemaphoreType.DMA((slots, shards))
    return [table, table, table, table, pltpu.SemaphoreType.DMA((slots, shards + 1)), table, table, table]


def full_shapes(weights, axes, shards):
    shapes = []
    for w, axis in zip(weights, axes):
        shape = list(w.shape)
        shape[axis] *= shards
        shapes.append(jax.ShapeDtypeStruct(tuple(shape), w.dtype))
    return shapes


def gather_kernel(axes, shards, *refs):
    count = len(axes)
    sources, fulls, held = refs[:count], refs[count : 2 * count], refs[2 * count : 3 * count]
    load_sem, store_sem = refs[3 * count : 3 * count + 2]
    greet, begin, relay, spread, finish, flush, own_place = mover(
        sources, fulls, refs[3 * count + 2 :], shards
    )
    pieces = [
        [(i, i, axes[i], 0, sources[i].shape[0], 0, sources[i].shape[1])] for i in range(count)
    ]
    greet()
    for piece in pieces:
        begin(piece)
    loads = [pltpu.make_async_copy(sources[i], held[i], load_sem.at[i]) for i in range(count)]
    stores = [pltpu.make_async_copy(held[i], own_place(i, axes[i]), store_sem.at[i]) for i in range(count)]
    for load in loads:
        load.start()
    for load, store in zip(loads, stores):
        load.wait()
        store.start()
    for piece in pieces:
        relay(piece)
    for piece in pieces:
        spread(piece)
    for piece in pieces:
        finish(piece)
    for piece in pieces:
        flush(piece)
    for store in stores:
        store.wait()


def gather(weights, axes, shards):
    count = len(weights)
    return pl.pallas_call(
        functools.partial(gather_kernel, axes, shards),
        out_shape=full_shapes(weights, axes, shards),
        in_specs=[pl.BlockSpec(memory_space=pl.ANY)] * count,
        out_specs=[pl.BlockSpec(memory_space=pl.ANY)] * count,
        scratch_shapes=[pltpu.VMEM(w.shape, w.dtype) for w in weights]
        + [pltpu.SemaphoreType.DMA((count,)), pltpu.SemaphoreType.DMA((count,))]
        + mover_semaphores(count, shards),
        compiler_params=pltpu.CompilerParams(
            collective_id=0, has_side_effects=True, vmem_limit_bytes=32 * 2**20
        ),
    )(*weights)


FORE_AXES = (1, 1, 0, 1, 0, 0, 1)


def fore_kernel(
    shards, block,
    w_output, w_right, w_lgate, w_lproj, w_gate, w_up, w_down,
    attended, tokens, laurel_mid, out_in, out_out, ffn_in, gu_out, down_in, down_out,
    gain_in, gain_attn, gain_laurel, gain_pre,
    full_output, full_right, full_lgate, full_lproj, full_gate, full_up, full_down, gate_out, up_out, ffn_out,
    attn_proj, combined, code_out, code_ffn, code_down, part,
    stage_a, stage_b, stage_c, stage_d, stage_e, stage_f, stage_g, out_w, right_w, gate_w, up_w, down_w, sent, got, ffn, total, codes, hidden,
    gate_keep, up_keep,
    load_sem, store_sem, weight_sem, keep_sem, ffn_sem, swap_send, swap_recv, *semaphores,
):
    sources = (w_output, w_right, w_lgate, w_lproj, w_gate, w_up, w_down)
    fulls = (full_output, full_right, full_lgate, full_lproj, full_gate, full_up, full_down)
    side = lax.axis_index("tensor")
    partner = {"tensor": 1 - side}
    greet, begin, relay, spread, finish, flush, own_place = mover(sources, fulls, semaphores, shards)
    rank = out_in.shape[0]
    count, width = ffn.shape
    half = count // 2
    quarter = half // 2
    groups = w_gate.shape[1] // block

    def whole(i):
        return (i, i, FORE_AXES[i], 0, sources[i].shape[0], 0, sources[i].shape[1])

    first = [whole(0), whole(1)]
    small = [whole(2), whole(3)]

    def group(g):
        base = 4 + 3 * g
        return [
            (base, 4, 0, 0, sources[4].shape[0], g * block, block),
            (base + 1, 5, 0, 0, sources[5].shape[0], g * block, block),
            (base + 2, 6, 1, g * block, block, 0, sources[6].shape[1]),
        ]

    greet([partner])
    begin(first)
    begin(group(0))
    begin(small)
    begin(group(1))
    stages = (stage_a, stage_b, stage_c, stage_d, stage_e, stage_f, stage_g)
    loads = [pltpu.make_async_copy(sources[i], stages[i], load_sem.at[i]) for i in range(7)]
    stores = [pltpu.make_async_copy(stages[i], own_place(i, FORE_AXES[i]), store_sem.at[i]) for i in range(7)]
    for load in loads:
        load.start()
    for load, store in zip(loads, stores):
        load.wait()
        store.start()
    for store in stores:
        store.wait()

    relay(first)
    spread(first)
    finish(first)
    load_out = pltpu.make_async_copy(full_output, out_w, weight_sem.at[0])
    load_right = pltpu.make_async_copy(full_right, right_w, weight_sem.at[1])
    load_out.start()
    load_right.start()
    code = low(dot_t(attended[...], out_in[...]))
    code_out[...] = code
    load_out.wait()
    load_right.wait()
    mine = pl.ds(pl.multiple_of(side * half, half), half)
    theirs = pl.ds(pl.multiple_of((1 - side) * half, half), half)
    sent[...] = low(dot(attended[theirs, :], out_w[...]) + dot(code_out[theirs, :], out_out[...]))
    swap_attn = pltpu.make_async_remote_copy(
        src_ref=sent, dst_ref=got, send_sem=swap_send.at[0], recv_sem=swap_recv.at[0],
        device_id=partner, device_id_type=MESH,
    )
    swap_attn.start()
    attn_proj[...] = dot(attended[mine, :], out_w[...]) + dot(code_out[mine, :], out_out[...])

    relay(group(0))
    swap_attn.wait()
    rows = 64

    def combine(i, carry):
        at = pl.ds(pl.multiple_of(i * rows, rows), rows)
        proj = attn_proj[at, :] + wide(got[at, :])
        attn_proj[at, :] = proj
        token = wide(tokens[at, :])
        normed = token * inverse_rms(token) * gain_in[...]
        end = dot(laurel_mid[at, :], right_w[...])
        comb = (
            token + proj * inverse_rms(proj) * gain_attn[...] + normed + end * inverse_rms(end) * gain_laurel[...]
        ) * ROOT_HALF
        combined[at, :] = comb
        ffn[at, :] = low(comb * inverse_rms(comb) * gain_pre[...])
        return carry

    lax.fori_loop(0, half // rows, combine, 0)
    swaps = []
    for k in range(2):
        swaps.append(
            pltpu.make_async_remote_copy(
                src_ref=ffn.at[pl.ds(k * quarter, quarter), :], dst_ref=ffn.at[pl.ds(half + k * quarter, quarter), :],
                send_sem=swap_send.at[1 + k], recv_sem=swap_recv.at[1 + k],
                device_id=partner, device_id_type=MESH,
            )
        )
        swaps[k].start()
    relay(small)
    spread(small)
    total[...] = jnp.zeros_like(total)
    codes[...] = jnp.zeros_like(codes)

    def keeps(g, slot):
        at = pl.ds(pl.multiple_of(g * block, block), block)
        return (
            pltpu.make_async_copy(gate_keep.at[slot], gate_out.at[:, at], keep_sem.at[0, slot]),
            pltpu.make_async_copy(up_keep.at[slot], up_out.at[:, at], keep_sem.at[1, slot]),
        )

    def weights(g):
        at = pl.ds(pl.multiple_of(g * block, block), block)
        return (
            pltpu.make_async_copy(full_gate.at[:, at], gate_w, weight_sem.at[2]),
            pltpu.make_async_copy(full_up.at[:, at], up_w, weight_sem.at[3]),
            pltpu.make_async_copy(full_down.at[at, :], down_w, weight_sem.at[4]),
        )

    def climb(g):
        at = pl.ds(pl.multiple_of(g * block, block), block)
        slot = lax.rem(g, 2)

        @pl.when(g >= 2)
        def _():
            for keep in keeps(g - 2, slot):
                keep.wait()

        ready = weights(g)
        ready[0].wait()
        gate = dot(ffn[...], gate_w[...]) + dot(code_ffn[:, :rank], gu_out[0, :, at])
        gate_keep[slot] = low(gate)
        act = gelu_parts(gate)[0]
        ready[1].wait()
        up = dot(ffn[...], up_w[...]) + dot(code_ffn[:, rank:], gu_out[1, :, at])
        up_keep[slot] = low(up)
        hidden[...] = low(act * up)
        for keep in keeps(g, slot):
            keep.start()

    def descend(g):
        at = pl.ds(pl.multiple_of(g * block, block), block)
        weights(g)[2].wait()
        codes[...] += dot_t(hidden[...], down_in[:, at])
        total[...] += dot(hidden[...], down_w[...])

    def round_(g, carry):
        more = g + 1 < groups

        @pl.when(more)
        def _():
            relay(group(g + 1), 1, 1)

        @pl.when(g + 2 < groups)
        def _():
            begin(group(g + 2))

        spread(group(g))

        @pl.when(g >= 1)
        def _():
            descend(g - 1)

        @pl.when(more)
        def _():
            relay(group(g + 1), 2, 2)

        finish(group(g))
        for load in weights(g):
            load.start()

        @pl.when(more)
        def _():
            relay(group(g + 1), 3)

        @pl.when(g == 0)
        def _():
            for swap_ffn in swaps:
                swap_ffn.wait()
            pltpu.make_async_copy(ffn, ffn_out, ffn_sem).start()
            code_ffn[...] = low(dot_t(ffn[...], ffn_in[...]))

        climb(g)
        return carry

    lax.fori_loop(0, groups, round_, 0)
    descend(groups - 1)
    code_down[...] = low(codes[...])
    part[...] = low(total[...] + dot(code_down[...], down_out[...]))
    finish(small)
    for g in (groups - 2, groups - 1):
        for keep in keeps(g, g % 2):
            keep.wait()
    pltpu.make_async_copy(ffn, ffn_out, ffn_sem).wait()
    flush(first)
    flush(small)

    def flush_group(g, carry):
        flush(group(g))
        return carry

    lax.fori_loop(0, groups, flush_group, 0)


def fore(
    weights, attended, tokens, laurel_mid, out_in, out_out, ffn_in, gu_out, down_in, down_out, gains, shards
):
    count = attended.shape[0]
    width = tokens.shape[1]
    hidden = weights[4].shape[1]
    half = count // 2
    rank = out_in.shape[0]
    block = min(512, hidden)
    groups = hidden // block
    bf16, f32 = jnp.bfloat16, jnp.float32
    anywhere, vmem = pl.BlockSpec(memory_space=pl.ANY), pl.BlockSpec(memory_space=pltpu.VMEM)
    shape = jax.ShapeDtypeStruct
    return pl.pallas_call(
        functools.partial(fore_kernel, shards, block),
        out_shape=full_shapes(weights, FORE_AXES, shards)
        + [
            shape((count, hidden), bf16),
            shape((count, hidden), bf16),
            shape((count, width), bf16),
            shape((half, width), f32),
            shape((half, width), f32),
            shape((count, rank), bf16),
            shape((count, 2 * rank), bf16),
            shape((count, rank), bf16),
            shape((count, width), bf16),
        ],
        in_specs=[anywhere] * 7 + [vmem] * 13,
        out_specs=[anywhere] * 10 + [vmem] * 6,
        scratch_shapes=[
            *[pltpu.VMEM(w.shape, bf16) for w in weights],
            pltpu.VMEM((weights[0].shape[0], width), bf16),
            pltpu.VMEM((weights[1].shape[0], width), bf16),
            pltpu.VMEM((width, block), bf16),
            pltpu.VMEM((width, block), bf16),
            pltpu.VMEM((block, width), bf16),
            pltpu.VMEM((half, width), bf16),
            pltpu.VMEM((half, width), bf16),
            pltpu.VMEM((count, width), bf16),
            pltpu.VMEM((count, width), f32),
            pltpu.VMEM((count, rank), f32),
            pltpu.VMEM((count, block), bf16),
            pltpu.VMEM((2, count, block), bf16),
            pltpu.VMEM((2, count, block), bf16),
            pltpu.SemaphoreType.DMA((7,)),
            pltpu.SemaphoreType.DMA((7,)),
            pltpu.SemaphoreType.DMA((5,)),
            pltpu.SemaphoreType.DMA((2, 2)),
            pltpu.SemaphoreType.DMA,
            pltpu.SemaphoreType.DMA((3,)),
            pltpu.SemaphoreType.DMA((3,)),
        ]
        + mover_semaphores(4 + 3 * groups, shards),
        compiler_params=pltpu.CompilerParams(
            collective_id=1, has_side_effects=True, vmem_limit_bytes=60 * 2**20
        ),
    )(*weights, attended, tokens, laurel_mid, out_in, out_out, ffn_in, gu_out, down_in, down_out, *gains)


def body(
    tokens,
    layer_input,
    segments,
    adapter_ids,
    cotangent,
    w_query,
    w_key,
    w_value,
    w_output,
    w_gate,
    w_up,
    w_down,
    laurel_left,
    laurel_right,
    input_gate,
    input_proj,
    gain_in,
    gain_attn,
    gain_laurel,
    gain_pre,
    gain_post,
    gain_layer,
    gain_query,
    gain_key,
    adapt_attn_in,
    adapt_query_out,
    adapt_kv_out,
    adapt_out_in,
    adapt_out_out,
    adapt_ffn_in,
    adapt_gu_out,
    adapt_down_in,
    adapt_down_out,
):
    seq_count, count, width = tokens.shape
    assert seq_count == 1 and lax.axis_size("tensor") == 2 and lax.axis_size("context") == 4
    half = count // 2
    head_size = gain_query.shape[0]
    rank = adapt_query_out.shape[1]
    heads = adapt_query_out.shape[2] // head_size
    kv_heads = adapt_kv_out.shape[3] // head_size
    group = heads // kv_heads
    side = lax.axis_index("tensor")
    place = lax.axis_index("context")
    shards = lax.axis_size("shard")

    full_query, full_key, full_value, full_left = gather(
        (w_query, w_key, w_value, laurel_left.T), (0, 0, 0, 1), shards
    )
    hidden_here = w_gate.shape[1]
    chosen = adapter_ids[0]

    def pick(table):
        return lax.dynamic_index_in_dim(table, chosen, 0, keepdims=False)

    pick_attn_in, pick_query_out, pick_kv_out = pick(adapt_attn_in), pick(adapt_query_out), pick(adapt_kv_out)
    pick_out_in, pick_out_out, pick_ffn_in = pick(adapt_out_in), pick(adapt_out_out), pick(adapt_ffn_in)
    pick_gu_out, pick_down_in, pick_down_out = pick(adapt_gu_out), pick(adapt_down_in), pick(adapt_down_out)

    def own_half(array):
        return lax.dynamic_slice_in_dim(array, side * half, half, 0)

    def other_half(array):
        return lax.dynamic_slice_in_dim(array, (1 - side) * half, half, 0)

    def in_order(own, other):
        return jnp.where(
            side == 0, jnp.concatenate([own, other], axis=0), jnp.concatenate([other, own], axis=0)
        )

    start_pos = place * count
    seg_all = segments[0]
    seg_query = lax.dynamic_slice_in_dim(seg_all, start_pos, count, 0)
    before = jnp.sum((seg_all[None, :] < seg_query[:, None]).astype(jnp.int32), axis=1)
    own_pos = start_pos + jnp.arange(count, dtype=jnp.int32) - before
    cosine, sine_table = rope_tables(own_pos, head_size)
    cosine = cosine[:, None, :]
    sine_table = sine_table[:, None, :]
    tokens_f = wide(tokens[0])
    normed_b = low(rms_norm(tokens_f, gain_in))
    tokens_h = wide(own_half(tokens[0]))
    normed_h = rms_norm(tokens_h, gain_in)
    code_attn = matmul(normed_b, pick_attn_in)
    query_lin = matmul(normed_b, full_query) + matmul(code_attn[:, :rank], pick_query_out)
    key_lin = matmul(normed_b, full_key) + matmul(code_attn[:, rank : 2 * rank], pick_kv_out[0])
    value_lin = matmul(normed_b, full_value) + matmul(code_attn[:, 2 * rank :], pick_kv_out[1])

    def prepare(query_in, key_in, value_in):
        query_rot = rotate_half(
            rms_norm(query_in.reshape(count, heads, head_size), gain_query), cosine, sine_table
        )
        key_rot = rotate_half(
            rms_norm(key_in.reshape(count, kv_heads, head_size), gain_key), cosine, sine_table
        )
        value_nrm = rms_norm(value_in.reshape(count, kv_heads, head_size), 1.0)
        return (query_rot, key_rot, value_nrm)

    (query_rot, key_rot, value_nrm), prepare_back = jax.vjp(prepare, query_lin, key_lin, value_lin)
    query_b = low(query_rot).reshape(count, kv_heads, group, head_size)
    kv_own = low(jnp.stack([key_rot, value_nrm]))
    kv_prior = shifted(kv_own, "context", 1)
    kv_all = jnp.concatenate([kv_prior, kv_own], axis=1)
    query_pos = start_pos + jnp.arange(count, dtype=jnp.int32)
    key_pos = start_pos - count + jnp.arange(2 * count, dtype=jnp.int32)
    seg_prior = lax.dynamic_slice_in_dim(seg_all, jnp.maximum(start_pos - count, 0), count, 0)
    seg_keys = jnp.concatenate([seg_prior, seg_query], axis=0)
    distance = query_pos[:, None] - key_pos[None, :]
    window_ok = (distance >= 0) & (distance < WINDOW) & (key_pos >= 0)[None, :]
    allowed = (seg_query[:, None] == seg_keys[None, :]) & window_ok
    allowed = allowed[None, None]
    score_scale = 1.0 / math.sqrt(head_size)

    def masked_scores():
        raw_scores = (
            jnp.einsum("lkgd,mkd->kglm", query_b, kv_all[0], preferred_element_type=jnp.float32)
            * score_scale
        )
        return jnp.where(allowed, raw_scores, -1e30)

    scores = masked_scores()
    row_max = jnp.max(scores, axis=-1, keepdims=True)
    exponent = jnp.exp(scores - row_max)
    row_total = jnp.sum(exponent, axis=-1, keepdims=True)
    log_total = row_max + jnp.log(row_total)
    attn_probs = low(exponent / row_total)
    attended = jnp.einsum("kglm,mkd->lkgd", attn_probs, kv_all[1], preferred_element_type=jnp.float32)
    attended_b = low(attended.reshape(count, heads * head_size))
    laurel_mid = low(matmul_t(normed_h, full_left))
    (
        full_output, full_right, full_layer_gate, full_layer_proj, full_gate, full_up, full_down,
        gate_b, up_b, ffn_b, attn_proj, combined, code_out, code_ffn, code_down, down_part,
    ) = fore(
        (w_output, laurel_right, input_gate, input_proj, w_gate, w_up, w_down),
        attended_b, own_half(tokens[0]), laurel_mid,
        pick_out_in.T, pick_out_out, pick_ffn_in.T, pick_gu_out, pick_down_in.T, pick_down_out,
        (gain_in[None], gain_attn[None], gain_laurel[None], gain_pre[None]), shards,
    )
    mark = jnp.where(
        (lax.broadcasted_iota(jnp.int32, (rank, 512), 1) == chosen) & (place == 0), 1.0, 0.0
    )
    grad_attn_b, early, output_own, grad_inputs, grad_normed = aft(
        (full_gate, full_up, full_down), (gate_b, up_b),
        (
            down_part, combined, own_half(layer_input[0]), own_half(cotangent[0]), full_layer_gate, full_layer_proj,
            code_ffn, code_down, ffn_b, pick_down_in.T, pick_down_out, pick_gu_out, pick_ffn_in.T,
            attn_proj, laurel_mid, full_left, full_right, mark,
            gain_post[None], gain_layer[None], gain_pre[None], gain_attn[None], gain_laurel[None],
        ),
        shards,
    )
    layer_output = in_order(output_own, swap(output_own))
    code_out_back = matmul_t(grad_attn_b, pick_out_out)
    term_out_out = outer(code_out, grad_attn_b)
    term_out_in = outer(code_out_back, attended_b)
    grad_attended = low(matmul_t(grad_attn_b, full_output) + matmul_t(code_out_back, pick_out_in))
    grad_heads = grad_attended.reshape(count, kv_heads, group, head_size)
    recomputed = jnp.exp(masked_scores() - log_total)
    grad_probs = jnp.einsum("lkgd,mkd->kglm", grad_heads, kv_all[1], preferred_element_type=jnp.float32)
    grad_scores = low(
        recomputed * (grad_probs - jnp.sum(recomputed * grad_probs, axis=-1, keepdims=True))
    )
    grad_query = (
        jnp.einsum("kglm,mkd->lkgd", grad_scores, kv_all[0], preferred_element_type=jnp.float32)
        * score_scale
    )
    grad_keys = (
        jnp.einsum("kglm,lkgd->mkd", grad_scores, query_b, preferred_element_type=jnp.float32)
        * score_scale
    )
    grad_values = jnp.einsum(
        "kglm,lkgd->mkd", low(recomputed), grad_heads, preferred_element_type=jnp.float32
    )
    grad_kv = jnp.stack([grad_keys, grad_values])
    grad_kv_later = wide(shifted(low(grad_kv[:, :count]), "context", -1))
    grad_kv_own = grad_kv[:, count:] + grad_kv_later
    grad_qlin, grad_klin, grad_vlin = prepare_back(
        (grad_query.reshape(count, heads, head_size), grad_kv_own[0], grad_kv_own[1])
    )
    grad_qlin_b = low(grad_qlin)
    grad_klin_b = low(grad_klin)
    grad_vlin_b = low(grad_vlin)
    input_grad, late = tail(
        (
            grad_qlin_b, grad_klin_b, grad_vlin_b, full_query, full_key, full_value, low(code_attn), normed_b,
            pick_query_out, pick_kv_out, pick_attn_in.T, term_out_in, term_out_out,
            own_half(tokens[0]), gain_in[None], grad_inputs, grad_normed,
        ),
        shards,
    )

    at = 0

    def take(packed, columns):
        nonlocal at
        at += columns
        return wide(packed[..., at - columns : at])

    def joined(packed, columns):
        both = take(packed, columns)
        return jnp.concatenate([both[0], both[1]], axis=-1)

    def added(packed, columns):
        both = take(packed, columns)
        return both[0] + both[1]

    gate_out, up_out, down_in = (joined(early, hidden_here) for _ in range(3))
    ffn_in = [added(early, width) for _ in range(2)]
    down_out = added(early, width)
    adapters = adapt_attn_in.shape[0]
    marks = wide(early[0, :, 0, at : at + adapters])
    at = 0
    out_in = joined(late, heads * head_size)
    out_out = added(late, width)
    query_out = joined(late, heads * head_size)
    key_out, value_out = (joined(late, kv_heads * head_size) for _ in range(2))
    attn_in = [added(late, width) for _ in range(3)]

    def tables(terms):
        return sum(
            marks[s].reshape((adapters,) + (1,) * (terms.ndim - 1)) * terms[s][None] for s in range(shards)
        )

    def turned(terms):
        return tables(terms).transpose(0, 2, 1)

    return (
        layer_output[None],
        input_grad[None],
        turned(jnp.concatenate(attn_in, axis=1)),
        tables(query_out),
        tables(jnp.stack([key_out, value_out], axis=1)),
        turned(out_in),
        tables(out_out),
        turned(jnp.concatenate(ffn_in, axis=1)),
        tables(jnp.stack([gate_out, up_out], axis=1)),
        turned(down_in),
        tables(down_out),
    )


def solution(mesh):
    in_specs = (
        P("shard", "context", None),
        P("shard", "context", None),
        P("shard", None),
        P("shard"),
        P("shard", "context", None),
        P("shard", "tensor"),
        P("shard", "tensor"),
        P("shard", "tensor"),
        P("tensor", "shard"),
        P("shard", "tensor"),
        P("shard", "tensor"),
        P("tensor", "shard"),
        P("shard", None),
        P(None, "shard"),
        P("shard", None),
        P(None, "shard"),
        P(),
        P(),
        P(),
        P(),
        P(),
        P(),
        P(),
        P(),
        P(),
        P(None, None, "tensor"),
        P(None, None, None, "tensor"),
        P(None, "tensor", None),
        P(),
        P(),
        P(None, None, None, "tensor"),
        P(None, "tensor", None),
        P(),
    )
    out_specs = (
        P("shard", "context", None),
        P("shard", "context", None),
        P(),
        P(),
        P(),
        P(),
        P(),
        P(),
        P(),
        P(),
        P(),
    )
    return jax.shard_map(body, mesh=mesh, in_specs=in_specs, out_specs=out_specs, check_vma=False)
```

```python
import functools
import math

import jax
import jax.numpy as jnp
from jax import lax
from jax.experimental import pallas as pl
from jax.experimental.pallas import tpu as pltpu
from jax.sharding import PartitionSpec as P

WINDOW = 512
EPSILON = 1e-06
ROOT_HALF = 0.7071067811865476
GELU_SCALE = math.sqrt(2.0 / math.pi)
GELU_CUBE = 0.044715

MESH = pl.DeviceIdType.MESH


def shifted(array, axis, by):
    count = lax.axis_size(axis)
    pairs = [(i, i + by) for i in range(count) if 0 <= i + by < count]
    return lax.ppermute(array, axis, pairs)


def swap(array):
    return lax.ppermute(array, "tensor", [(0, 1), (1, 0)])


def rope_tables(positions, head_size):
    frequency = jnp.exp(
        jnp.arange(head_size // 2, dtype=jnp.float32) * (-2.0 * math.log(10000.0) / head_size)
    )
    angles = positions.astype(jnp.float32)[..., None] * frequency
    return (jnp.cos(angles), jnp.sin(angles))


def low(values):
    return values.astype(jnp.bfloat16)


def wide(values):
    return values.astype(jnp.float32)


def dot(left, right):
    return lax.dot_general(left, right, (((1,), (0,)), ((), ())), preferred_element_type=jnp.float32)


def dot_t(left, right):
    return lax.dot_general(left, right, (((1,), (1,)), ((), ())), preferred_element_type=jnp.float32)


def dot_o(left, right):
    return lax.dot_general(left, right, (((0,), (0,)), ((), ())), preferred_element_type=jnp.float32)


def row_mean(values):
    return jnp.mean(values, axis=-1, keepdims=True)


def inverse_rms(values):
    return lax.rsqrt(row_mean(values * values) + EPSILON)


def rms_back(values, inverse, scaled):
    return inverse * scaled - values * (inverse * inverse * inverse * row_mean(values * scaled))


def gelu_parts(values):
    squared = values * values
    bend = jnp.tanh(GELU_SCALE * values * (1.0 + GELU_CUBE * squared))
    rise = 0.5 * (1.0 + bend)
    slope = rise + 0.5 * values * (1.0 - bend * bend) * (GELU_SCALE * (1.0 + 3.0 * GELU_CUBE * squared))
    return values * rise, slope


def greet_all(shards, places, ends):
    z = lax.axis_index("shard")
    barrier = pltpu.get_barrier_semaphore()

    def signal(place):
        pl.semaphore_signal(barrier, inc=1, device_id=place, device_id_type=MESH)

    for place in places:
        signal(place)
    peers = len(places)
    if ends:

        @pl.when(z > 0)
        def _():
            signal({"shard": z - 1})

        @pl.when(z < shards - 1)
        def _():
            signal({"shard": z + 1})

        peers = peers + lax.div(z + shards - 1, shards) + lax.div(2 * shards - 2 - z, shards)
    pl.semaphore_wait(barrier, peers)


def context_partners():
    c = lax.axis_index("context")
    return lax.rem(c + 2, 4), c + 1 - 2 * lax.rem(c, 2)


def sharer(pack, whole, inbox, turn_in, turn_out, piece, semaphores, shards):
    (
        pre_send, pre_recv, z_send, z_recv, x_send, x_recv, y_send, y_recv, near_send, near_recv,
        far_send, far_recv, keep_sem,
    ) = semaphores
    z, c, side = (lax.axis_index(a) for a in ("shard", "context", "tensor"))
    across, beside = context_partners()
    opposite = lax.rem(beside + 2, 4)
    columns = piece.shape[1]

    def cols(q):
        return pl.ds(pl.multiple_of(q * columns, 128), columns)

    def region(t, s, q):
        return whole.at[t, s, :, cols(q)]

    def copy(source, target, send, recv, place):
        return pltpu.make_async_remote_copy(
            src_ref=source, dst_ref=target, send_sem=send, recv_sem=recv, device_id=place, device_id_type=MESH
        )

    def halves(k):
        q = beside if k == 0 else opposite
        return copy(pack.at[:, cols(q)], inbox.at[k], pre_send.at[k], pre_recv.at[k], {"context": beside})

    def turned():
        return copy(turn_out, turn_in, pre_send.at[2], pre_recv.at[2], {"context": across})

    def z_copy(s, source, sender, by):
        return copy(source, region(side, s, c), z_send.at[sender], z_recv.at[s], {"shard": z + by})

    def passed(s, by):
        return z_copy(s, region(side, s, c), s, by)

    def x_copy(s, source, t):
        return copy(source, region(t, s, c), x_send.at[s], x_recv.at[s], {"tensor": 1 - side})

    def y_copy(t, s, source, q):
        return copy(source, region(t, s, q), y_send.at[t, s], y_recv.at[t, s], {"context": across})

    def near_copy(t, s, source, q):
        return copy(source, region(t, s, q), near_send.at[t, s], near_recv.at[t, s], {"context": beside})

    def far_copy(t, s, q):
        at = region(t, s, q)
        return copy(at, at, far_send.at[t, s], far_recv.at[t, s], {"context": beside})

    def keep():
        return pltpu.make_async_copy(piece, region(side, z, c), keep_sem)

    def start():
        for k in range(2):
            halves(k).start()

    def turn():
        for k in range(2):
            halves(k).wait_recv()
        turn_out[...] = low(pack[:, cols(across)] + inbox[1])
        turned().start()

    def settle():
        turned().wait_recv()
        piece[...] = low(pack[:, cols(c)] + inbox[0] + wide(turn_in[...]))
        keep().start()

        @pl.when(z < shards - 1)
        def _():
            z_copy(z, piece, z, 1).start()

        @pl.when(z > 0)
        def _():
            z_copy(z, piece, shards, -1).start()

        x_copy(z, piece, side).start()
        y_copy(side, z, piece, c).start()
        near_copy(side, z, piece, c).start()

    def hand_on(s):
        at = region(side, s, c)
        x_copy(s, at, side).start()
        y_copy(side, s, at, c).start()
        near_copy(side, s, at, c).start()

    def hop(d):
        @pl.when(z >= d)
        def _():
            s = z - d
            passed(s, 1).wait_recv()

            @pl.when(z < shards - 1)
            def _():
                passed(s, 1).start()

            hand_on(s)

        @pl.when(z + d <= shards - 1)
        def _():
            s = z + d
            passed(s, -1).wait_recv()

            @pl.when(z > 0)
            def _():
                passed(s, -1).start()

            hand_on(s)

    def hops(first):
        lax.fori_loop(first, shards, lambda d, carry: (hop(d), carry)[1], 0)

    def cross_over():
        def one(s, carry):
            at = region(1 - side, s, c)
            x_copy(s, at, 1 - side).wait_recv()
            y_copy(1 - side, s, at, c).start()
            near_copy(1 - side, s, at, c).start()
            return carry

        lax.fori_loop(0, shards, one, 0)

    def every(act):
        def one(s, carry):
            for t in range(2):
                act(t, s)
            return carry

        lax.fori_loop(0, shards, one, 0)

    def spread():
        def act(t, s):
            y_copy(t, s, region(t, s, across), across).wait_recv()
            far_copy(t, s, across).start()

        every(act)

    def finish():
        def act(t, s):
            near_copy(t, s, region(t, s, beside), beside).wait_recv()
            far_copy(t, s, opposite).wait_recv()
            y_copy(t, s, region(t, s, c), c).wait_send()
            near_copy(t, s, region(t, s, c), c).wait_send()
            far_copy(t, s, across).wait_send()

        every(act)

        def one(s, carry):
            x_copy(s, region(side, s, c), side).wait_send()

            @pl.when((s < z) & (z < shards - 1))
            def _():
                passed(s, 1).wait_send()

            @pl.when((s > z) & (z > 0))
            def _():
                passed(s, -1).wait_send()

            return carry

        lax.fori_loop(0, shards, one, 0)

        @pl.when(z < shards - 1)
        def _():
            z_copy(z, piece, z, 1).wait_send()

        @pl.when(z > 0)
        def _():
            z_copy(z, piece, shards, -1).wait_send()

        for k in range(2):
            halves(k).wait_send()
        turned().wait_send()
        keep().wait()

    return start, turn, settle, hop, hops, cross_over, spread, finish


def sharer_scratch(rows, columns, shards):
    part = columns // 4
    dma = pltpu.SemaphoreType.DMA
    return [
        pltpu.VMEM((2, rows, part), jnp.float32),
        pltpu.VMEM((rows, part), jnp.bfloat16),
        pltpu.VMEM((rows, part), jnp.bfloat16),
        pltpu.VMEM((rows, part), jnp.bfloat16),
        dma((3,)), dma((3,)), dma((shards + 1,)), dma((shards,)), dma((shards,)), dma((shards,)),
        dma((2, shards)), dma((2, shards)), dma((2, shards)), dma((2, shards)), dma((2, shards)), dma((2, shards)),
        dma,
    ]


def tail_kernel(
    shards,
    grad_query, w_query, w_key, w_value, code_attn, normed, query_out, kv_out, attn_in,
    out_in_term, out_out_term, tokens, gain_in, grad_comb, grad_normed,
    own_kv, came_kv, lin_kv, cosine, sine, gain_key,
    input_grad_out, whole,
    pack, mine, sent, got, result, grad_key, grad_value, send_sem, recv_sem, keep_sem, *shared,
):
    side = lax.axis_index("tensor")
    partner = {"tensor": 1 - side}
    across, beside = context_partners()
    count, width = normed.shape
    half = count // 2
    quarter = half // 2
    rank = query_out.shape[0]
    start, turn, settle, hop, hops, cross_over, spread, finish = sharer(
        pack, whole, shared[0], shared[1], shared[2], shared[3], shared[4:], shards
    )
    greet_all(shards, [partner, {"context": across}, {"context": beside}], True)
    keys = grad_key.shape[1]
    values = lin_kv[:, :keys]
    turned = unrotate(own_kv[0] + wide(came_kv[0]), cosine[...], sine[...]) * gain_key[...]
    grad_key[...] = low(rms_back(values, inverse_rms(values), turned))
    values = lin_kv[:, keys:]
    grad_value[...] = low(rms_back(values, inverse_rms(values), own_kv[1] + wide(came_kv[1])))
    parts = ((grad_query, w_query, query_out[...]), (grad_key, w_key, kv_out[0]), (grad_value, w_value, kv_out[1]))
    at = 0

    def put(term):
        nonlocal at
        pack[:, at : at + term.shape[1]] = term
        at += term.shape[1]

    put(out_in_term[...])
    put(out_out_term[...])
    backs = []
    for i, (grad, _, table) in enumerate(parts):
        put(dot_o(code_attn[:, i * rank : (i + 1) * rank], grad[...]))
        backs.append(low(dot_t(grad[...], table)))
    for back in backs:
        put(dot_o(back, normed[...]))
    start()

    def product(here):
        total = dot_t(grad_query[here, :], w_query[...])
        total += dot_t(grad_key[here, :], w_key[...]) + dot_t(grad_value[here, :], w_value[...])
        for i, (grad, _, table) in enumerate(parts):
            back = low(dot_t(grad[here, :], table))
            total += dot(back, attn_in[i * rank : (i + 1) * rank, :])
        return total

    def send(source, target, k):
        return pltpu.make_async_remote_copy(
            src_ref=source, dst_ref=target, send_sem=send_sem.at[k], recv_sem=recv_sem.at[k],
            device_id=partner, device_id_type=MESH,
        )

    def rows(k):
        return pl.ds(k * quarter, quarter)

    def rows_of(owner, k):
        return pl.ds(pl.multiple_of(owner * half + k * quarter, quarter), quarter)

    swaps = []
    for k in range(2):
        sent[rows(k), :] = low(product(rows_of(1 - side, k)))
        swaps.append(send(sent.at[rows(k), :], got.at[rows(k), :], k))
        swaps[k].start()
    turn()
    for k in range(2):
        mine[rows(k), :] = product(rows_of(side, k))
        if k == 0:
            settle()
    hop(1)
    ends = []
    for k in range(2):
        swaps[k].wait_recv()
        here = rows(k)
        grad = (grad_normed[here, :] + mine[here, :] + wide(got[here, :])) * gain_in[...]
        token = wide(tokens[here, :])
        there = rows_of(side, k)
        result[there, :] = low(grad_comb[here, :] + rms_back(token, inverse_rms(token), grad))
        ends.append(send(result.at[there, :], result.at[there, :], 2 + k))
        ends[k].start()
        if k == 0:
            hops(2)
    cross_over()
    spread()
    for end in ends:
        end.wait()
    keep = pltpu.make_async_copy(result, input_grad_out, keep_sem)
    keep.start()
    for swap_part in swaps:
        swap_part.wait_send()
    finish()
    keep.wait()


def tail(arrays, shards):
    count, width = arrays[5].shape
    rank = arrays[6].shape[0]
    half = count // 2
    queries, keys = arrays[0].shape[1], arrays[2].shape[1]
    columns = 2 * queries + 2 * keys + 4 * width
    bf16, f32 = jnp.bfloat16, jnp.float32
    anywhere, vmem = pl.BlockSpec(memory_space=pl.ANY), pl.BlockSpec(memory_space=pltpu.VMEM)
    return pl.pallas_call(
        functools.partial(tail_kernel, shards),
        out_shape=[
            jax.ShapeDtypeStruct((count, width), bf16),
            jax.ShapeDtypeStruct((2, shards, rank, columns), bf16),
        ],
        in_specs=[vmem] * len(arrays),
        out_specs=[anywhere] * 2,
        scratch_shapes=[
            pltpu.VMEM((rank, columns), f32),
            pltpu.VMEM((half, width), f32),
            pltpu.VMEM((half, width), bf16),
            pltpu.VMEM((half, width), bf16),
            pltpu.VMEM((count, width), bf16),
            pltpu.VMEM((count, keys), bf16),
            pltpu.VMEM((count, keys), bf16),
            pltpu.SemaphoreType.DMA((4,)),
            pltpu.SemaphoreType.DMA((4,)),
            pltpu.SemaphoreType.DMA,
        ]
        + sharer_scratch(rank, columns, shards),
        compiler_params=pltpu.CompilerParams(
            collective_id=3, has_side_effects=True, vmem_limit_bytes=60 * 2**20
        ),
    )(*arrays)


def allowed_bias(seg_rows, seg_cols, keys):
    count = seg_rows.shape[0]
    shape = (count, keys)
    distance = lax.broadcasted_iota(jnp.int32, shape, 0) + (keys - count) - lax.broadcasted_iota(jnp.int32, shape, 1)
    seen = (seg_rows[...] == seg_cols[...]) & (distance >= 0) & (distance < WINDOW)
    return jnp.where(seen, 0.0, -1e30)


def attend_kernel(scale, query, prior, own, seg_rows, seg_cols, attended, log_total, bias):
    count = query.shape[0]

    @pl.when(pl.program_id(0) == 0)
    def _():
        bias[...] = allowed_bias(seg_rows, seg_cols, 2 * count)

    early = dot_t(query[...], prior[0]) * scale + bias[:, :count]
    later = dot_t(query[...], own[0]) * scale + bias[:, count:]
    top = jnp.maximum(jnp.max(early, axis=-1, keepdims=True), jnp.max(later, axis=-1, keepdims=True))
    early, later = jnp.exp(early - top), jnp.exp(later - top)
    total = jnp.sum(early, axis=-1, keepdims=True) + jnp.sum(later, axis=-1, keepdims=True)
    log_total[...] = top + jnp.log(total)
    attended[...] = low(dot(low(early / total), prior[1]) + dot(low(later / total), own[1]))


def attend(query, prior, own, seg_rows, seg_cols, head, scale):
    count, inner = query.shape
    heads = inner // head
    return pl.pallas_call(
        functools.partial(attend_kernel, scale),
        grid=(heads,),
        in_specs=[
            pl.BlockSpec((count, head), lambda h: (0, h)),
            pl.BlockSpec((2, count, head), lambda h: (0, 0, 0)),
            pl.BlockSpec((2, count, head), lambda h: (0, 0, 0)),
            pl.BlockSpec((count, 1), lambda h: (0, 0)),
            pl.BlockSpec((1, 2 * count), lambda h: (0, 0)),
        ],
        out_specs=[
            pl.BlockSpec((count, head), lambda h: (0, h)),
            pl.BlockSpec((None, count, 1), lambda h: (h, 0, 0)),
        ],
        out_shape=[
            jax.ShapeDtypeStruct((count, inner), jnp.bfloat16),
            jax.ShapeDtypeStruct((heads, count, 1), jnp.float32),
        ],
        scratch_shapes=[pltpu.VMEM((count, 2 * count), jnp.float32)],
        compiler_params=pltpu.CompilerParams(vmem_limit_bytes=56 * 2**20),
    )(query, prior, own, seg_rows, seg_cols)


def unrotate(grad, cosine, sine):
    middle = grad.shape[1] // 2
    former, latter = grad[:, :middle], grad[:, middle:]
    return jnp.concatenate([former * cosine + latter * sine, latter * cosine - former * sine], axis=1)


def attend_back_kernel(
    scale, grad, w_out, out_in, out_out, code_out, attended, query, prior, own, log_total, seg_rows, seg_cols, lin,
    cosine, sine, gain_query,
    grad_query, sent_kv, own_kv, term_in, term_out, bias, back, grad_k, grad_v,
):
    count = query.shape[0]
    head = pl.program_id(0)

    @pl.when(head == 0)
    def _():
        bias[...] = allowed_bias(seg_rows, seg_cols, 2 * count)
        back[...] = low(dot_t(grad[...], out_out[...]))
        term_out[...] = dot_o(code_out[...], grad[...])
        grad_k[...] = jnp.zeros_like(grad_k)
        grad_v[...] = jnp.zeros_like(grad_v)

    top = low(dot_t(grad[...], w_out[...]) + dot(back[...], out_in[...]))
    term_in[...] = dot_o(back[...], attended[...])
    probs, slopes, mean = [], [], 0.0
    for i, kv in enumerate((prior, own)):
        score = dot_t(query[...], kv[0]) * scale + bias[:, i * count : (i + 1) * count]
        probs.append(jnp.exp(score - log_total[...]))
        slopes.append(dot_t(top, kv[1]))
        mean += jnp.sum(probs[i] * slopes[i], axis=-1, keepdims=True)
    turned = 0.0
    for i, kv in enumerate((prior, own)):
        grad_score = low(probs[i] * (slopes[i] - mean))
        turned += dot(grad_score, kv[0])
        grad_k[i] += dot_o(grad_score, query[...]) * scale
        grad_v[i] += dot_o(low(probs[i]), top)
    values = lin[...]
    turned = unrotate(turned * scale, cosine[...], sine[...]) * gain_query[...]
    grad_query[...] = low(rms_back(values, inverse_rms(values), turned))

    @pl.when(head == pl.num_programs(0) - 1)
    def _():
        sent_kv[0] = low(grad_k[0])
        sent_kv[1] = low(grad_v[0])
        own_kv[0] = grad_k[1]
        own_kv[1] = grad_v[1]


def attend_back(
    grad, w_out, out_in, out_out, code_out, attended, query, prior, own, log_total, seg_rows, seg_cols, lin,
    cosine, sine, gain_query, scale,
):
    count, inner = query.shape
    width = grad.shape[1]
    head = gain_query.shape[1]
    rank = out_in.shape[0]
    bf16, f32 = jnp.bfloat16, jnp.float32
    whole = lambda *shape: pl.BlockSpec(shape, lambda h: (0,) * len(shape))
    column = lambda rows: pl.BlockSpec((rows, head), lambda h: (0, h))
    return pl.pallas_call(
        functools.partial(attend_back_kernel, scale),
        grid=(inner // head,),
        in_specs=[
            whole(count, width),
            pl.BlockSpec((head, width), lambda h: (h, 0)),
            column(rank),
            whole(rank, width),
            whole(count, rank),
            column(count),
            column(count),
            whole(2, count, head),
            whole(2, count, head),
            pl.BlockSpec((None, count, 1), lambda h: (h, 0, 0)),
            whole(count, 1),
            whole(1, 2 * count),
            column(count),
            whole(count, head // 2),
            whole(count, head // 2),
            whole(1, head),
        ],
        out_specs=[column(count), whole(2, count, head), whole(2, count, head), column(rank), whole(rank, width)],
        out_shape=[
            jax.ShapeDtypeStruct((count, inner), bf16),
            jax.ShapeDtypeStruct((2, count, head), bf16),
            jax.ShapeDtypeStruct((2, count, head), f32),
            jax.ShapeDtypeStruct((rank, inner), f32),
            jax.ShapeDtypeStruct((rank, width), f32),
        ],
        scratch_shapes=[
            pltpu.VMEM((count, 2 * count), f32),
            pltpu.VMEM((count, rank), bf16),
            pltpu.VMEM((2, count, head), f32),
            pltpu.VMEM((2, count, head), f32),
        ],
        compiler_params=pltpu.CompilerParams(vmem_limit_bytes=56 * 2**20),
    )(
        grad, w_out, out_in, out_out, code_out, attended, query, prior, own, log_total, seg_rows, seg_cols, lin,
        cosine, sine, gain_query,
    )


def tables_kernel(
    queries, keys, early, late, output_own, output_other,
    output, out_attn, out_query, out_kv, out_out_in, out_out_out, out_ffn, out_gu, out_down_in, out_down_out,
    marks, drawn, laid, mark_sem, drawn_sem, laid_sem, output_sem,
):
    side = lax.axis_index("tensor")
    shards, rank = early.shape[1], early.shape[2]
    half, width = output_own.shape
    puts = []
    for i, (rows, owner) in enumerate(((output_own, side), (output_other, 1 - side))):
        there = output.at[pl.ds(pl.multiple_of(owner * half, half), half), :]
        puts.append(pltpu.make_async_copy(rows, there, output_sem.at[i]))
        puts[i].start()
    adapters, hidden = out_gu.shape[0], out_gu.shape[3] // 2
    wide_at = early.shape[3] - 512
    get_marks = pltpu.make_async_copy(early.at[0, :, :, pl.ds(wide_at, 128)], marks, mark_sem)
    get_marks.start()
    span = drawn.shape[4]
    def both(source, at, columns, table, inner):
        found = []
        for first in range(0, columns, span):
            size = min(span, columns - first)
            found.append(
                (source, at + first, size, [table(t * inner + first, size) for t in range(2)])
            )
        return found

    def gu_table(i):
        return lambda at, size: out_gu.at[:, i, :, pl.ds(at, size)]

    def kv_table(i):
        return lambda at, size: out_kv.at[:, i, :, pl.ds(at, size)]

    def plain(out, row=0):
        return lambda at, size: out.at[:, pl.ds(row, rank), pl.ds(at, size)]

    def single(source, at, out, row=0):
        return [
            (source, at + first, span, [plain(out, row)(first, span)]) for first in range(0, width, span)
        ]

    early_units = both(early, 0, hidden, gu_table(0), hidden) + both(early, hidden, hidden, gu_table(1), hidden)
    early_units += both(early, 2 * hidden, hidden, plain(out_down_in), hidden)
    early_units += single(early, 3 * hidden, out_ffn) + single(early, 3 * hidden + width, out_ffn, rank)
    early_units += single(early, 3 * hidden + 2 * width, out_down_out)
    late_units = both(late, 0, queries, plain(out_out_in), queries) + single(late, queries, out_out_out)
    late_units += both(late, queries + width, queries, plain(out_query), queries)
    late_units += both(late, 2 * queries + width, keys, kv_table(0), keys)
    late_units += both(late, 2 * queries + width + keys, keys, kv_table(1), keys)
    for i in range(3):
        late_units += single(late, 2 * queries + (1 + i) * width + 2 * keys, out_attn, i * rank)
    units = early_units + late_units

    def draw(u):
        source, at, size, _ = units[u]
        return pltpu.make_async_copy(
            source.at[:, :, :, pl.ds(at, size)], drawn.at[u % 2, :, :, :, pl.ds(0, size)], drawn_sem.at[u % 2]
        )

    def lays(u):
        _, _, size, targets = units[u]
        return [
            pltpu.make_async_copy(laid.at[u % 2, t, :, :, pl.ds(0, size)], target, laid_sem.at[u % 2, t])
            for t, target in enumerate(targets)
        ]

    def lay_out(u, last):
        if u + 1 < last:
            draw(u + 1).start()
        draw(u).wait()
        if u >= 2:
            for lay in lays(u - 2):
                lay.wait()
        _, _, size, targets = units[u]
        lanes = min(256, size)
        slot = u % 2

        def one(i, carry):
            at = pl.ds(pl.multiple_of(i * lanes, lanes), lanes)
            for t in range(len(targets)):
                terms = []
                for q in range(shards):
                    term = wide(drawn[slot, t, q, :, at])
                    if len(targets) == 1:
                        term += wide(drawn[slot, 1, q, :, at])
                    terms.append(term)
                for k in range(adapters):
                    total = terms[0] * wide(marks[0])[:, k : k + 1]
                    for q in range(1, shards):
                        total += terms[q] * wide(marks[q])[:, k : k + 1]
                    laid[slot, t, k, :, at] = total
            return carry

        lax.fori_loop(0, size // lanes, one, 0)
        for lay in lays(u):
            lay.start()

    draw(0).start()
    get_marks.wait()
    for u in range(len(units)):
        lay_out(u, len(units))
    for u in (len(units) - 2, len(units) - 1):
        for lay in lays(u):
            lay.wait()
    for put in puts:
        put.wait()


def tables(early, late, output_own, output_other, queries, keys, adapters, hidden):
    half, width = output_own.shape
    shards, rank = early.shape[1], early.shape[2]
    span = 2048
    bf16, f32 = jnp.bfloat16, jnp.float32
    anywhere, vmem = pl.BlockSpec(memory_space=pl.ANY), pl.BlockSpec(memory_space=pltpu.VMEM)
    return pl.pallas_call(
        functools.partial(tables_kernel, queries, keys),
        out_shape=[jax.ShapeDtypeStruct((2 * half, width), bf16)]
        + [
            jax.ShapeDtypeStruct((adapters,) + rest, f32)
            for rest in (
                (3 * rank, width), (rank, 2 * queries), (2, rank, 2 * keys), (rank, 2 * queries), (rank, width),
                (2 * rank, width), (2, rank, 2 * hidden), (rank, 2 * hidden), (rank, width),
            )
        ],
        in_specs=[anywhere] * 2 + [vmem] * 2,
        out_specs=[anywhere] * 10,
        scratch_shapes=[
            pltpu.VMEM((shards, rank, 128), bf16),
            pltpu.VMEM((2, 2, shards, rank, span), bf16),
            pltpu.VMEM((2, 2, adapters, rank, span), f32),
            pltpu.SemaphoreType.DMA,
            pltpu.SemaphoreType.DMA((2,)),
            pltpu.SemaphoreType.DMA((2, 2)),
            pltpu.SemaphoreType.DMA((2,)),
        ],
        compiler_params=pltpu.CompilerParams(vmem_limit_bytes=60 * 2**20),
    )(early, late, output_own, output_other)


def aft_kernel(
    shards, block, strip,
    full_gate, full_up, full_down, gate_in, up_in,
    part, combined, per_layer, cotangent, lgate, lproj, code_ffn, code_down, ffn, down_in, down_out, gu_out, ffn_in,
    attn_proj, laurel_mid, left, right, mark, gain_post, gain_layer, gain_pre, gain_attn, gain_laurel,
    grad_attn_out, whole, output, grad_comb, grad_normed, pack,
    got, grad, grad_gate, grad_up, down_w, gate_v, up_v, gate_w, up_w, mine, sent, came, attn, back_codes, ffn_codes,
    fetch_sem, strip_sem, keep_sem, send_sem, recv_sem, *shared,
):
    side = lax.axis_index("tensor")
    partner = {"tensor": 1 - side}
    across, beside = context_partners()
    greet_all(shards, [partner, {"context": across}, {"context": beside}], True)
    start, turn, settle, hop, hops, cross_over, spread, finish = sharer(
        pack, whole, shared[0], shared[1], shared[2], shared[3], shared[4:], shards
    )
    count, width = grad.shape
    half = count // 2
    quarter = half // 2
    rank = down_in.shape[0]
    hidden = grad_gate.shape[1]
    steps = hidden // block
    strips = width // strip

    def send(source, target, k):
        return pltpu.make_async_remote_copy(
            src_ref=source, dst_ref=target, send_sem=send_sem.at[k], recv_sem=recv_sem.at[k],
            device_id=partner, device_id_type=MESH,
        )

    def rows(k):
        return pl.ds(k * quarter, quarter)

    down_swaps = [send(part.at[rows(2 + k), :], got.at[rows(k), :], k) for k in range(2)]
    grad_swaps = [send(grad.at[rows(k), :], grad.at[rows(2 + k), :], 2 + k) for k in range(2)]
    for swap_down in down_swaps:
        swap_down.start()

    def fetches(t):
        slot, j = lax.rem(t, 2), lax.rem(t, steps)
        at = pl.ds(pl.multiple_of(j * block, block), block)
        here = pl.ds(pl.multiple_of(lax.div(t, steps) * half, half), half)
        return (
            pltpu.make_async_copy(full_down.at[at, :], down_w.at[slot], fetch_sem.at[0, slot]),
            pltpu.make_async_copy(gate_in.at[here, at], gate_v.at[slot], fetch_sem.at[1, slot]),
            pltpu.make_async_copy(up_in.at[here, at], up_v.at[slot], fetch_sem.at[2, slot]),
        )

    def strip_fetches(k):
        slot = lax.rem(k, 2)
        at = pl.ds(pl.multiple_of(k * strip, strip), strip)
        return (
            pltpu.make_async_copy(full_gate.at[at, :], gate_w.at[slot], strip_sem.at[0, slot]),
            pltpu.make_async_copy(full_up.at[at, :], up_w.at[slot], strip_sem.at[1, slot]),
        )

    for fetch in fetches(0) + strip_fetches(0):
        fetch.start()
    pack[...] = jnp.zeros_like(pack)
    ffn_codes[...] = jnp.zeros_like(ffn_codes)

    for k in range(2):
        down_swaps[k].wait_recv()
        at = rows(k)
        down = wide(part[at, :]) + wide(got[at, :])
        down_inverse = inverse_rms(down)
        after = combined[at, :] + down * down_inverse * gain_post[...]
        mixing = wide(per_layer[at, :])
        act, slope = gelu_parts(dot(low(after), lgate[...]))
        proj = dot(low(act * mixing), lproj[...])
        proj_inverse = inverse_rms(proj)
        output[at, :] = low(after + proj * proj_inverse * gain_layer[...])
        top = wide(cotangent[at, :])
        grad_proj = rms_back(proj, proj_inverse, top * gain_layer[...])
        grad_mix = dot_t(low(grad_proj), lproj[...]) * mixing * slope
        top = top + dot_t(low(grad_mix), lgate[...])
        grad_comb[at, :] = top
        grad[at, :] = low(rms_back(down, down_inverse, top * gain_post[...]))
        grad_swaps[k].start()
        back_codes[at, :] = low(dot_t(grad[at, :], down_out[...]))

    def level(t, carry):
        @pl.when(t + 1 < 2 * steps)
        def _():
            for fetch in fetches(t + 1):
                fetch.start()

        @pl.when(t == steps)
        def _():
            for k in range(2):
                grad_swaps[k].wait_recv()
            back_codes[half:, :] = low(dot_t(grad[half:, :], down_out[...]))

        slot, j = lax.rem(t, 2), lax.rem(t, steps)
        at = pl.ds(pl.multiple_of(j * block, block), block)
        here = pl.ds(pl.multiple_of(lax.div(t, steps) * half, half), half)
        for fetch in fetches(t):
            fetch.wait()
        back = back_codes[here, :]
        hidden_grad = dot_t(grad[here, :], down_w[slot]) + dot(back, down_in[:, at])
        up_now = wide(up_v[slot])
        act, slope = gelu_parts(wide(gate_v[slot]))
        grad_g = low(hidden_grad * up_now * slope)
        grad_u = low(hidden_grad * act)
        grad_gate[here, at] = grad_g
        grad_up[here, at] = grad_u
        ffn_codes[0, here, :] += dot_t(grad_g, gu_out[0, :, at])
        ffn_codes[1, here, :] += dot_t(grad_u, gu_out[1, :, at])
        codes = code_ffn[here, :]

        def put(i, term):
            pack[:, pl.ds(pl.multiple_of(i * hidden + j * block, block), block)] += term

        put(0, dot_o(codes[:, :rank], grad_g))
        put(1, dot_o(codes[:, rank:], grad_u))
        put(2, dot_o(back, low(act * up_now)))
        return carry

    lax.fori_loop(0, 2 * steps, level, 0)
    base = 3 * hidden
    pack[:, base : base + width] = dot_o(low(ffn_codes[0]), ffn[...])
    pack[:, base + width : base + 2 * width] = dot_o(low(ffn_codes[1]), ffn[...])
    pack[:, base + 2 * width : base + 3 * width] = dot_o(code_down[...], grad[...])
    pack[:, base + 3 * width :] = mark[...]
    start()

    def strip_send(k):
        return send(sent.at[k], came.at[k], 4 + k)

    def cross(k, carry):
        @pl.when(k + 1 < strips)
        def _():
            for fetch in strip_fetches(k + 1):
                fetch.start()

        slot = lax.rem(k, 2)
        at = pl.ds(pl.multiple_of(k * strip, strip), strip)
        for fetch in strip_fetches(k):
            fetch.wait()
        result = (
            dot_t(grad_gate[...], gate_w[slot])
            + dot_t(grad_up[...], up_w[slot])
            + dot(low(ffn_codes[0]), ffn_in[:rank, at])
            + dot(low(ffn_codes[1]), ffn_in[rank:, at])
        )
        sent[k] = low(result[half:])
        strip_send(k).start()
        mine[:, at] = result[:half]
        for when, act in ((1, turn), (2, settle), (3, lambda: hop(1)), (4, lambda: hop(2)), (5, lambda: hops(3))):
            pl.when(k == when)(act)
        return carry

    lax.fori_loop(0, strips, cross, 0)
    cross_over()

    def add(k, carry):
        at = pl.ds(pl.multiple_of(k * strip, strip), strip)
        strip_send(k).wait_recv()
        mine[:, at] += wide(came[k])
        return carry

    lax.fori_loop(0, strips, add, 0)
    attn_swaps = []
    for k in range(2):
        at = rows(k)
        comb = combined[at, :]
        top = (grad_comb[at, :] + rms_back(comb, inverse_rms(comb), mine[at, :] * gain_pre[...])) * ROOT_HALF
        grad_comb[at, :] = top
        proj = attn_proj[at, :]
        there = pl.ds(pl.multiple_of(side * half + k * quarter, quarter), quarter)
        attn[there, :] = low(rms_back(proj, inverse_rms(proj), top * gain_attn[...]))
        attn_swaps.append(send(attn.at[there, :], attn.at[there, :], 4 + strips + k))
        attn_swaps[k].start()
        end = dot(laurel_mid[at, :], right[...])
        grad_end = low(rms_back(end, inverse_rms(end), top * gain_laurel[...]))
        grad_normed[at, :] = top + dot(low(dot_t(grad_end, right[...])), left[...])
    spread()
    for swap_attn in attn_swaps:
        swap_attn.wait()
    keep = pltpu.make_async_copy(attn, grad_attn_out, keep_sem)
    keep.start()
    for k in range(2):
        down_swaps[k].wait_send()
        grad_swaps[k].wait_send()

    def flush(k, carry):
        strip_send(k).wait_send()
        return carry

    lax.fori_loop(0, strips, flush, 0)
    finish()
    keep.wait()


def aft(weights, kept, arrays, shards):
    full_gate = weights[0]
    part, combined, per_layer = arrays[:3]
    count, width = part.shape
    hidden = full_gate.shape[1]
    half = count // 2
    rank = arrays[9].shape[0]
    block, strip = min(512, hidden), 256
    strips = width // strip
    columns = 3 * hidden + 3 * width + arrays[17].shape[1]
    bf16, f32 = jnp.bfloat16, jnp.float32
    shape = jax.ShapeDtypeStruct
    anywhere, vmem = pl.BlockSpec(memory_space=pl.ANY), pl.BlockSpec(memory_space=pltpu.VMEM)
    return pl.pallas_call(
        functools.partial(aft_kernel, shards, block, strip),
        out_shape=[
            shape((count, width), bf16),
            shape((2, shards, rank, columns), bf16),
            shape((half, width), bf16),
            shape((half, width), f32),
            shape((half, width), f32),
        ],
        in_specs=[anywhere] * 5 + [vmem] * len(arrays),
        out_specs=[anywhere] * 2 + [vmem] * 3,
        scratch_shapes=[
            pltpu.VMEM((rank, columns), f32),
            pltpu.VMEM((half, width), bf16),
            pltpu.VMEM((count, width), bf16),
            pltpu.VMEM((count, hidden), bf16),
            pltpu.VMEM((count, hidden), bf16),
            pltpu.VMEM((2, block, width), bf16),
            pltpu.VMEM((2, half, block), bf16),
            pltpu.VMEM((2, half, block), bf16),
            pltpu.VMEM((2, strip, hidden), bf16),
            pltpu.VMEM((2, strip, hidden), bf16),
            pltpu.VMEM((half, width), f32),
            pltpu.VMEM((strips, half, strip), bf16),
            pltpu.VMEM((strips, half, strip), bf16),
            pltpu.VMEM((count, width), bf16),
            pltpu.VMEM((count, rank), bf16),
            pltpu.VMEM((2, count, rank), f32),
            pltpu.SemaphoreType.DMA((3, 2)),
            pltpu.SemaphoreType.DMA((2, 2)),
            pltpu.SemaphoreType.DMA,
            pltpu.SemaphoreType.DMA((6 + strips,)),
            pltpu.SemaphoreType.DMA((6 + strips,)),
        ]
        + sharer_scratch(rank, columns, shards),
        compiler_params=pltpu.CompilerParams(
            collective_id=2, has_side_effects=True, vmem_limit_bytes=60 * 2**20
        ),
        cost_estimate=pl.CostEstimate(
            flops=6 * count * width * hidden, bytes_accessed=8 * width * hidden, transcendentals=count * hidden
        ),
    )(*weights, *kept, *arrays)


def mover(sources, fulls, semaphores, shards):
    z_recv, y_recv, near_recv, far_recv, z_send, y_send, near_send, far_send = semaphores
    z, c = lax.axis_index("shard"), lax.axis_index("context")
    across = lax.rem(c + 2, 4)
    beside = c + 1 - 2 * lax.rem(c, 2)

    def greet(also=()):
        barrier = pltpu.get_barrier_semaphore()

        def signal(place):
            pl.semaphore_signal(barrier, inc=1, device_id=place, device_id_type=MESH)

        signal({"context": across})
        signal({"context": beside})
        for place in also:
            signal(place)

        @pl.when(z > 0)
        def _():
            signal({"shard": z - 1})

        @pl.when(z < shards - 1)
        def _():
            signal({"shard": z + 1})

        peers = 2 + len(also) + lax.div(z + shards - 1, shards) + lax.div(2 * shards - 2 - z, shards)
        pl.semaphore_wait(barrier, peers)

    def region(piece, s, q):
        _, item, axis, row, rows, col, cols = piece
        rows_here, cols_here = sources[item].shape
        part = rows // 4
        if axis == 0:
            return fulls[item].at[
                pl.ds(pl.multiple_of(s * rows_here + row + q * part, 16), part),
                pl.ds(pl.multiple_of(col, 128), cols),
            ]
        return fulls[item].at[
            pl.ds(pl.multiple_of(row + q * part, 16), part),
            pl.ds(pl.multiple_of(s * cols_here + col, 128), cols),
        ]

    def own(piece):
        _, item, axis, row, rows, col, cols = piece
        part = rows // 4
        return sources[item].at[
            pl.ds(pl.multiple_of(row + c * part, 16), part), pl.ds(pl.multiple_of(col, 128), cols)
        ]

    def copy(source, target, send, recv, place):
        return pltpu.make_async_remote_copy(
            src_ref=source, dst_ref=target, send_sem=send, recv_sem=recv, device_id=place, device_id_type=MESH
        )

    def along(piece, s, source, sender, by):
        slot = piece[0]
        return copy(source, region(piece, s, c), z_send.at[slot, sender], z_recv.at[slot, s], {"shard": z + by})

    def passed(piece, s, by):
        return along(piece, s, region(piece, s, c), s, by)

    def y_copy(piece, s, q):
        at = region(piece, s, q)
        return copy(at, at, y_send.at[piece[0], s], y_recv.at[piece[0], s], {"context": across})

    def near_copy(piece, s, q):
        at = region(piece, s, q)
        return copy(at, at, near_send.at[piece[0], s], near_recv.at[piece[0], s], {"context": beside})

    def far_copy(piece, s, q):
        at = region(piece, s, q)
        return copy(at, at, far_send.at[piece[0], s], far_recv.at[piece[0], s], {"context": beside})

    def begin(pieces):
        @pl.when(z < shards - 1)
        def _():
            for piece in pieces:
                along(piece, z, own(piece), z, 1).start()

        @pl.when(z > 0)
        def _():
            for piece in pieces:
                along(piece, z, own(piece), shards, -1).start()

    def relay(pieces, first=1, last=None):
        def hop(d, carry):
            @pl.when(z >= d)
            def _():
                s = z - d
                for piece in pieces:
                    passed(piece, s, 1).wait_recv()

                    @pl.when(z < shards - 1)
                    def _(piece=piece):
                        passed(piece, s, 1).start()

                    y_copy(piece, s, c).start()
                    near_copy(piece, s, c).start()

            @pl.when(z + d <= shards - 1)
            def _():
                s = z + d
                for piece in pieces:
                    passed(piece, s, -1).wait_recv()

                    @pl.when(z > 0)
                    def _(piece=piece):
                        passed(piece, s, -1).start()

                    y_copy(piece, s, c).start()
                    near_copy(piece, s, c).start()

            return carry

        last = shards - 1 if last is None else last
        if first == last:
            hop(first, 0)
        else:
            lax.fori_loop(first, last + 1, hop, 0)

    def others(pieces, act):
        def one(d, carry):
            for piece in pieces:
                act(piece, lax.rem(z + d, shards))
            return carry

        lax.fori_loop(1, shards, one, 0)

    def spread(pieces):
        def act(piece, s):
            y_copy(piece, s, across).wait_recv()
            far_copy(piece, s, across).start()

        others(pieces, act)

    def finish(pieces):
        def act(piece, s):
            near_copy(piece, s, beside).wait_recv()
            far_copy(piece, s, lax.rem(beside + 2, 4)).wait_recv()

        others(pieces, act)

    def flush(pieces):
        @pl.when(z < shards - 1)
        def _():
            for piece in pieces:
                along(piece, z, own(piece), z, 1).wait_send()

        @pl.when(z > 0)
        def _():
            for piece in pieces:
                along(piece, z, own(piece), shards, -1).wait_send()

        def act(piece, s):
            y_copy(piece, s, c).wait_send()
            near_copy(piece, s, c).wait_send()
            far_copy(piece, s, across).wait_send()

            @pl.when((s < z) & (z < shards - 1))
            def _():
                passed(piece, s, 1).wait_send()

            @pl.when((s > z) & (z > 0))
            def _():
                passed(piece, s, -1).wait_send()

        others(pieces, act)

    def own_place(item, axis):
        rows_here, cols_here = sources[item].shape
        if axis == 0:
            return fulls[item].at[pl.ds(pl.multiple_of(z * rows_here, 16), rows_here), :]
        return fulls[item].at[:, pl.ds(pl.multiple_of(z * cols_here, 128), cols_here)]

    return greet, begin, relay, spread, finish, flush, own_place


def mover_semaphores(slots, shards):
    table = pltpu.SemaphoreType.DMA((slots, shards))
    return [table, table, table, table, pltpu.SemaphoreType.DMA((slots, shards + 1)), table, table, table]


def full_shapes(weights, axes, shards):
    shapes = []
    for w, axis in zip(weights, axes):
        shape = list(w.shape)
        shape[axis] *= shards
        shapes.append(jax.ShapeDtypeStruct(tuple(shape), w.dtype))
    return shapes


def pick_kernel(chosen, *refs):
    count = len(refs) // 2
    for source, target in zip(refs[:count], refs[count:]):
        if len(source.shape) > len(target.shape):
            target[...] = source[0]
        else:
            target[...] = source[...]


def pick_rows(chosen, side, tables, arrays):
    in_specs, out_specs, shapes = [], [], []
    for t in tables:
        rest = t.shape[1:]
        in_specs.append(pl.BlockSpec((1,) + rest, lambda i, at, n=len(rest): (at[0],) + (0,) * n))
        out_specs.append(pl.BlockSpec(rest, lambda i, at, n=len(rest): (0,) * n))
        shapes.append(jax.ShapeDtypeStruct(rest, t.dtype))
    for a in arrays:
        part = (a.shape[0] // 2, a.shape[1])
        in_specs.append(pl.BlockSpec(part, lambda i, at: (at[1], 0)))
        out_specs.append(pl.BlockSpec(part, lambda i, at: (0, 0)))
        shapes.append(jax.ShapeDtypeStruct(part, a.dtype))
    return pl.pallas_call(
        pick_kernel,
        grid_spec=pltpu.PrefetchScalarGridSpec(
            num_scalar_prefetch=1, grid=(1,), in_specs=in_specs, out_specs=out_specs
        ),
        out_shape=shapes,
        compiler_params=pltpu.CompilerParams(vmem_limit_bytes=61 * 2**20),
    )(jnp.stack([chosen, side]), *tables, *arrays)


FRONT_AXES = (0, 0, 0, 1)


def front_kernel(
    shards, w_query, w_key, w_value, w_left, tokens, attn_in, query_out, kv_out, cosine, sine, gain_in, gain_query, gain_key,
    full_query, full_key, full_value, full_left,
    normed, code_attn, lin, lin_kv, query_rot, kv_rot,
    held_query, held_key, held_value, held_left, query_w, key_w, value_w, load_sem, store_sem, weight_sem, *semaphores,
):
    sources, fulls = (w_query, w_key, w_value, w_left), (full_query, full_key, full_value, full_left)
    held = (held_query, held_key, held_value, held_left)
    greet, begin, relay, spread, finish, flush, own_place = mover(sources, fulls, semaphores, shards)
    pieces = [
        [(i, i, FRONT_AXES[i], 0, sources[i].shape[0], 0, sources[i].shape[1])] for i in range(4)
    ]
    greet()
    for piece in pieces:
        begin(piece)
    loads = [pltpu.make_async_copy(sources[i], held[i], load_sem.at[i]) for i in range(4)]
    stores = [pltpu.make_async_copy(held[i], own_place(i, FRONT_AXES[i]), store_sem.at[i]) for i in range(4)]
    for load in loads:
        load.start()
    for load, store in zip(loads, stores):
        load.wait()
        store.start()
    count = tokens.shape[0]
    rows = 64

    def norm(i, carry):
        at = pl.ds(pl.multiple_of(i * rows, rows), rows)
        token = wide(tokens[at, :])
        normed[at, :] = low(token * inverse_rms(token) * gain_in[...])
        return carry

    for k, piece in enumerate(pieces):
        relay(piece)
        if k == 0:
            lax.fori_loop(0, count // rows, norm, 0)
            code_attn[...] = low(dot_t(normed[...], attn_in[...]))
    for piece in pieces:
        spread(piece)
    for piece in pieces:
        finish(piece)
    for store in stores:
        store.wait()
    bring = [
        pltpu.make_async_copy(full, w, weight_sem.at[i])
        for i, (full, w) in enumerate(zip(fulls[:3], (query_w, key_w, value_w)))
    ]
    for copy in bring:
        copy.start()
    head = gain_query.shape[1]
    middle = head // 2
    rank = query_out.shape[0]
    queries, keys = query_w.shape[1], key_w.shape[1]

    def rotate(values, target, at):
        former, latter = values[:, :middle], values[:, middle:]
        target[:, at : at + middle] = low(former * cosine[...] - latter * sine[...])
        target[:, at + middle : at + head] = low(latter * cosine[...] + former * sine[...])

    bring[0].wait()
    for h in range(queries // head):
        at = slice(h * head, (h + 1) * head)
        values = dot(normed[...], query_w[:, at]) + dot(code_attn[:, :rank], query_out[:, at])
        lin[:, at] = values
        rotate(values * inverse_rms(values) * gain_query[...], query_rot, h * head)
    bring[1].wait()
    bring[2].wait()
    for h in range(keys // head):
        at = slice(h * head, (h + 1) * head)
        values = dot(normed[...], key_w[:, at]) + dot(code_attn[:, rank : 2 * rank], kv_out[0, :, at])
        lin_kv[:, at] = values
        rotate(values * inverse_rms(values) * gain_key[...], kv_rot.at[0], h * head)
        values = dot(normed[...], value_w[:, at]) + dot(code_attn[:, 2 * rank :], kv_out[1, :, at])
        lin_kv[:, keys + h * head : keys + (h + 1) * head] = values
        kv_rot[1, :, at] = low(values * inverse_rms(values))
    for piece in pieces:
        flush(piece)


def front(weights, arrays, shards):
    count, width = arrays[0].shape
    queries, keys = weights[0].shape[1], weights[1].shape[1]
    rank = arrays[2].shape[0]
    bf16, f32 = jnp.bfloat16, jnp.float32
    shape = jax.ShapeDtypeStruct
    anywhere, vmem = pl.BlockSpec(memory_space=pl.ANY), pl.BlockSpec(memory_space=pltpu.VMEM)
    return pl.pallas_call(
        functools.partial(front_kernel, shards),
        out_shape=full_shapes(weights, FRONT_AXES, shards)
        + [
            shape((count, width), bf16),
            shape((count, 3 * rank), bf16),
            shape((count, queries), f32),
            shape((count, 2 * keys), f32),
            shape((count, queries), bf16),
            shape((2, count, keys), bf16),
        ],
        in_specs=[anywhere] * 4 + [vmem] * len(arrays),
        out_specs=[anywhere] * 4 + [vmem] * 6,
        scratch_shapes=[pltpu.VMEM(w.shape, w.dtype) for w in weights]
        + [pltpu.VMEM((width, n), bf16) for n in (queries, keys, keys)]
        + [pltpu.SemaphoreType.DMA((4,)), pltpu.SemaphoreType.DMA((4,)), pltpu.SemaphoreType.DMA((3,))]
        + mover_semaphores(4, shards),
        compiler_params=pltpu.CompilerParams(
            collective_id=0, has_side_effects=True, vmem_limit_bytes=60 * 2**20
        ),
    )(*weights, *arrays)


FORE_AXES = (1, 1, 0, 1, 0, 0, 1)


def fore_kernel(
    shards, block,
    w_output, w_right, w_lgate, w_lproj, w_gate, w_up, w_down,
    attended, tokens, left, out_in, out_out, ffn_in, gu_out, down_in, down_out,
    gain_in, gain_attn, gain_laurel, gain_pre,
    full_output, full_right, full_lgate, full_lproj, full_gate, full_up, full_down, gate_out, up_out, ffn_out,
    attn_proj, combined, laurel_mid, code_out, code_ffn, code_down, part,
    stage_a, stage_b, stage_c, stage_d, stage_e, stage_f, stage_g, out_w, right_w, gate_w, up_w, down_w, sent, got, ffn, total, codes, hidden,
    gate_keep, up_keep,
    load_sem, store_sem, weight_sem, keep_sem, ffn_sem, swap_send, swap_recv, *semaphores,
):
    sources = (w_output, w_right, w_lgate, w_lproj, w_gate, w_up, w_down)
    fulls = (full_output, full_right, full_lgate, full_lproj, full_gate, full_up, full_down)
    side = lax.axis_index("tensor")
    partner = {"tensor": 1 - side}
    greet, begin, relay, spread, finish, flush, own_place = mover(sources, fulls, semaphores, shards)
    rank = out_in.shape[0]
    count, width = ffn.shape
    half = count // 2
    quarter = half // 2
    groups = w_gate.shape[1] // block

    def whole(i):
        return (i, i, FORE_AXES[i], 0, sources[i].shape[0], 0, sources[i].shape[1])

    first = [whole(0), whole(1)]
    small = [whole(2), whole(3)]

    def group(g):
        base = 4 + 3 * g
        return [
            (base, 4, 0, 0, sources[4].shape[0], g * block, block),
            (base + 1, 5, 0, 0, sources[5].shape[0], g * block, block),
            (base + 2, 6, 1, g * block, block, 0, sources[6].shape[1]),
        ]

    greet([partner])
    begin(first)
    begin(group(0))
    begin(small)
    begin(group(1))
    stages = (stage_a, stage_b, stage_c, stage_d, stage_e, stage_f, stage_g)
    loads = [pltpu.make_async_copy(sources[i], stages[i], load_sem.at[i]) for i in range(7)]
    stores = [pltpu.make_async_copy(stages[i], own_place(i, FORE_AXES[i]), store_sem.at[i]) for i in range(7)]
    for load in loads:
        load.start()
    for load, store in zip(loads, stores):
        load.wait()
        store.start()
    for store in stores:
        store.wait()

    relay(first)
    spread(first)
    finish(first)
    load_out = pltpu.make_async_copy(full_output, out_w, weight_sem.at[0])
    load_right = pltpu.make_async_copy(full_right, right_w, weight_sem.at[1])
    load_out.start()
    load_right.start()
    code = low(dot_t(attended[...], out_in[...]))
    code_out[...] = code
    load_out.wait()
    load_right.wait()
    mine = pl.ds(pl.multiple_of(side * half, half), half)
    theirs = pl.ds(pl.multiple_of((1 - side) * half, half), half)
    sent[...] = low(dot(attended[theirs, :], out_w[...]) + dot(code_out[theirs, :], out_out[...]))
    swap_attn = pltpu.make_async_remote_copy(
        src_ref=sent, dst_ref=got, send_sem=swap_send.at[0], recv_sem=swap_recv.at[0],
        device_id=partner, device_id_type=MESH,
    )
    swap_attn.start()
    attn_proj[...] = dot(attended[mine, :], out_w[...]) + dot(code_out[mine, :], out_out[...])

    relay(group(0))
    swap_attn.wait()
    rows = 64

    def combine(i, carry):
        at = pl.ds(pl.multiple_of(i * rows, rows), rows)
        proj = attn_proj[at, :] + wide(got[at, :])
        attn_proj[at, :] = proj
        token = wide(tokens[at, :])
        normed = token * inverse_rms(token) * gain_in[...]
        mid = low(dot_t(low(normed), left[...]))
        laurel_mid[at, :] = mid
        end = dot(mid, right_w[...])
        comb = (
            token + proj * inverse_rms(proj) * gain_attn[...] + normed + end * inverse_rms(end) * gain_laurel[...]
        ) * ROOT_HALF
        combined[at, :] = comb
        ffn[at, :] = low(comb * inverse_rms(comb) * gain_pre[...])
        return carry

    lax.fori_loop(0, half // rows, combine, 0)
    swaps = []
    for k in range(2):
        swaps.append(
            pltpu.make_async_remote_copy(
                src_ref=ffn.at[pl.ds(k * quarter, quarter), :], dst_ref=ffn.at[pl.ds(half + k * quarter, quarter), :],
                send_sem=swap_send.at[1 + k], recv_sem=swap_recv.at[1 + k],
                device_id=partner, device_id_type=MESH,
            )
        )
        swaps[k].start()
    relay(small)
    spread(small)
    total[...] = jnp.zeros_like(total)
    codes[...] = jnp.zeros_like(codes)

    def keeps(g, slot):
        at = pl.ds(pl.multiple_of(g * block, block), block)
        return (
            pltpu.make_async_copy(gate_keep.at[slot], gate_out.at[:, at], keep_sem.at[0, slot]),
            pltpu.make_async_copy(up_keep.at[slot], up_out.at[:, at], keep_sem.at[1, slot]),
        )

    def weights(g):
        at = pl.ds(pl.multiple_of(g * block, block), block)
        return (
            pltpu.make_async_copy(full_gate.at[:, at], gate_w, weight_sem.at[2]),
            pltpu.make_async_copy(full_up.at[:, at], up_w, weight_sem.at[3]),
            pltpu.make_async_copy(full_down.at[at, :], down_w, weight_sem.at[4]),
        )

    def climb(g):
        at = pl.ds(pl.multiple_of(g * block, block), block)
        slot = lax.rem(g, 2)

        @pl.when(g >= 2)
        def _():
            for keep in keeps(g - 2, slot):
                keep.wait()

        ready = weights(g)
        ready[0].wait()
        gate = dot(ffn[...], gate_w[...]) + dot(code_ffn[:, :rank], gu_out[0, :, at])
        gate_keep[slot] = low(gate)
        act = gelu_parts(gate)[0]
        ready[1].wait()
        up = dot(ffn[...], up_w[...]) + dot(code_ffn[:, rank:], gu_out[1, :, at])
        up_keep[slot] = low(up)
        hidden[...] = low(act * up)
        for keep in keeps(g, slot):
            keep.start()

    def descend(g):
        at = pl.ds(pl.multiple_of(g * block, block), block)
        weights(g)[2].wait()
        codes[...] += dot_t(hidden[...], down_in[:, at])
        total[...] += dot(hidden[...], down_w[...])

    def round_(g, carry):
        more = g + 1 < groups

        @pl.when(more)
        def _():
            relay(group(g + 1), 1, 1)

        @pl.when(g + 2 < groups)
        def _():
            begin(group(g + 2))

        spread(group(g))

        @pl.when(g >= 1)
        def _():
            descend(g - 1)

        @pl.when(more)
        def _():
            relay(group(g + 1), 2, 2)

        finish(group(g))
        for load in weights(g):
            load.start()

        @pl.when(more)
        def _():
            relay(group(g + 1), 3)

        @pl.when(g == 0)
        def _():
            for swap_ffn in swaps:
                swap_ffn.wait()
            pltpu.make_async_copy(ffn, ffn_out, ffn_sem).start()
            code_ffn[...] = low(dot_t(ffn[...], ffn_in[...]))

        climb(g)
        return carry

    lax.fori_loop(0, groups, round_, 0)
    descend(groups - 1)
    code_down[...] = low(codes[...])
    part[...] = low(total[...] + dot(code_down[...], down_out[...]))
    finish(small)
    for g in (groups - 2, groups - 1):
        for keep in keeps(g, g % 2):
            keep.wait()
    pltpu.make_async_copy(ffn, ffn_out, ffn_sem).wait()
    flush(first)
    flush(small)

    def flush_group(g, carry):
        flush(group(g))
        return carry

    lax.fori_loop(0, groups, flush_group, 0)


def fore(
    weights, attended, tokens, left, out_in, out_out, ffn_in, gu_out, down_in, down_out, gains, shards
):
    count = attended.shape[0]
    width = tokens.shape[1]
    hidden = weights[4].shape[1]
    half = count // 2
    rank = out_in.shape[0]
    block = min(512, hidden)
    groups = hidden // block
    bf16, f32 = jnp.bfloat16, jnp.float32
    anywhere, vmem = pl.BlockSpec(memory_space=pl.ANY), pl.BlockSpec(memory_space=pltpu.VMEM)
    shape = jax.ShapeDtypeStruct
    return pl.pallas_call(
        functools.partial(fore_kernel, shards, block),
        out_shape=full_shapes(weights, FORE_AXES, shards)
        + [
            shape((count, hidden), bf16),
            shape((count, hidden), bf16),
            shape((count, width), bf16),
            shape((half, width), f32),
            shape((half, width), f32),
            shape((half, left.shape[0]), bf16),
            shape((count, rank), bf16),
            shape((count, 2 * rank), bf16),
            shape((count, rank), bf16),
            shape((count, width), bf16),
        ],
        in_specs=[anywhere] * 7 + [vmem] * 13,
        out_specs=[anywhere] * 10 + [vmem] * 7,
        scratch_shapes=[
            *[pltpu.VMEM(w.shape, bf16) for w in weights],
            pltpu.VMEM((weights[0].shape[0], width), bf16),
            pltpu.VMEM((weights[1].shape[0], width), bf16),
            pltpu.VMEM((width, block), bf16),
            pltpu.VMEM((width, block), bf16),
            pltpu.VMEM((block, width), bf16),
            pltpu.VMEM((half, width), bf16),
            pltpu.VMEM((half, width), bf16),
            pltpu.VMEM((count, width), bf16),
            pltpu.VMEM((count, width), f32),
            pltpu.VMEM((count, rank), f32),
            pltpu.VMEM((count, block), bf16),
            pltpu.VMEM((2, count, block), bf16),
            pltpu.VMEM((2, count, block), bf16),
            pltpu.SemaphoreType.DMA((7,)),
            pltpu.SemaphoreType.DMA((7,)),
            pltpu.SemaphoreType.DMA((5,)),
            pltpu.SemaphoreType.DMA((2, 2)),
            pltpu.SemaphoreType.DMA,
            pltpu.SemaphoreType.DMA((3,)),
            pltpu.SemaphoreType.DMA((3,)),
        ]
        + mover_semaphores(4 + 3 * groups, shards),
        compiler_params=pltpu.CompilerParams(
            collective_id=1, has_side_effects=True, vmem_limit_bytes=60 * 2**20
        ),
    )(*weights, attended, tokens, left, out_in, out_out, ffn_in, gu_out, down_in, down_out, *gains)


def body(
    tokens,
    layer_input,
    segments,
    adapter_ids,
    cotangent,
    w_query,
    w_key,
    w_value,
    w_output,
    w_gate,
    w_up,
    w_down,
    laurel_left,
    laurel_right,
    input_gate,
    input_proj,
    gain_in,
    gain_attn,
    gain_laurel,
    gain_pre,
    gain_post,
    gain_layer,
    gain_query,
    gain_key,
    adapt_attn_in,
    adapt_query_out,
    adapt_kv_out,
    adapt_out_in,
    adapt_out_out,
    adapt_ffn_in,
    adapt_gu_out,
    adapt_down_in,
    adapt_down_out,
):
    seq_count, count, width = tokens.shape
    assert seq_count == 1 and lax.axis_size("tensor") == 2 and lax.axis_size("context") == 4
    half = count // 2
    head_size = gain_query.shape[0]
    rank = adapt_query_out.shape[1]
    heads = adapt_query_out.shape[2] // head_size
    kv_heads = adapt_kv_out.shape[3] // head_size
    assert kv_heads == 1
    side = lax.axis_index("tensor")
    place = lax.axis_index("context")
    shards = lax.axis_size("shard")

    hidden_here = w_gate.shape[1]
    chosen = adapter_ids[0]

    def turned(table):
        return table.transpose(0, 2, 1)

    (
        pick_attn_in, pick_query_out, pick_kv_out, pick_out_in, pick_out_out, pick_ffn_in, pick_gu_out,
        pick_down_in, pick_down_out, tokens_own, per_layer_own, cotangent_own,
    ) = pick_rows(
        chosen, side,
        [
            turned(adapt_attn_in), adapt_query_out, adapt_kv_out, turned(adapt_out_in), adapt_out_out,
            turned(adapt_ffn_in), adapt_gu_out, turned(adapt_down_in), adapt_down_out,
        ],
        [tokens[0], layer_input[0], cotangent[0]],
    )

    start_pos = place * count
    seg_all = segments[0]
    seg_query = lax.dynamic_slice_in_dim(seg_all, start_pos, count, 0)
    before = jnp.sum((seg_all[None, :] < seg_query[:, None]).astype(jnp.int32), axis=1)
    own_pos = start_pos + jnp.arange(count, dtype=jnp.int32) - before
    cosine, sine_table = rope_tables(own_pos, head_size)
    (
        full_query, full_key, full_value, full_left, normed_b, code_attn, lin, lin_kv, query_rot, kv_own,
    ) = front(
        (w_query, w_key, w_value, laurel_left.T),
        (
            tokens[0], pick_attn_in, pick_query_out, pick_kv_out, cosine, sine_table,
            gain_in[None], gain_query[None], gain_key[None],
        ),
        shards,
    )
    kv_prior = shifted(kv_own, "context", 1)
    seg_prior = lax.dynamic_slice_in_dim(seg_all, jnp.maximum(start_pos - count, 0), count, 0)
    seg_cols = jnp.concatenate([jnp.where(place > 0, seg_prior, -1), seg_query])[None, :]
    seg_rows = seg_query[:, None]
    score_scale = 1.0 / math.sqrt(head_size)
    attended_b, log_total = attend(query_rot, kv_prior, kv_own, seg_rows, seg_cols, head_size, score_scale)
    (
        full_output, full_right, full_layer_gate, full_layer_proj, full_gate, full_up, full_down,
        gate_b, up_b, ffn_b, attn_proj, combined, laurel_mid, code_out, code_ffn, code_down, down_part,
    ) = fore(
        (w_output, laurel_right, input_gate, input_proj, w_gate, w_up, w_down),
        attended_b, tokens_own, full_left,
        pick_out_in, pick_out_out, pick_ffn_in, pick_gu_out, pick_down_in, pick_down_out,
        (gain_in[None], gain_attn[None], gain_laurel[None], gain_pre[None]), shards,
    )
    mark = jnp.where(
        (lax.broadcasted_iota(jnp.int32, (rank, 512), 1) == chosen) & (place == 0), 1.0, 0.0
    )
    grad_attn_b, early, output_own, grad_inputs, grad_normed = aft(
        (full_gate, full_up, full_down), (gate_b, up_b),
        (
            down_part, combined, per_layer_own, cotangent_own, full_layer_gate, full_layer_proj,
            code_ffn, code_down, ffn_b, pick_down_in, pick_down_out, pick_gu_out, pick_ffn_in,
            attn_proj, laurel_mid, full_left, full_right, mark,
            gain_post[None], gain_layer[None], gain_pre[None], gain_attn[None], gain_laurel[None],
        ),
        shards,
    )
    output_other = swap(output_own)
    grad_query, sent_kv, own_kv, term_out_in, term_out_out = attend_back(
        grad_attn_b, full_output, pick_out_in, pick_out_out, code_out, attended_b, query_rot, kv_prior, kv_own,
        log_total, seg_rows, seg_cols, lin, cosine, sine_table, gain_query[None], score_scale,
    )
    input_grad, late = tail(
        (
            grad_query, full_query, full_key, full_value, code_attn, normed_b,
            pick_query_out, pick_kv_out, pick_attn_in, term_out_in, term_out_out,
            tokens_own, gain_in[None], grad_inputs, grad_normed,
            own_kv, shifted(sent_kv, "context", -1), lin_kv, cosine, sine_table, gain_key[None],
        ),
        shards,
    )
    (
        layer_output, table_attn_in, table_query_out, table_kv_out, table_out_in, table_out_out, table_ffn_in,
        table_gu_out, table_down_in, table_down_out,
    ) = tables(
        early, late, output_own, output_other, heads * head_size, kv_heads * head_size, adapt_attn_in.shape[0], hidden_here
    )
    return (
        layer_output[None], input_grad[None], turned(table_attn_in), table_query_out, table_kv_out,
        turned(table_out_in), table_out_out, turned(table_ffn_in), table_gu_out, turned(table_down_in), table_down_out,
    )


def solution(mesh):
    in_specs = (
        P("shard", "context", None),
        P("shard", "context", None),
        P("shard", None),
        P("shard"),
        P("shard", "context", None),
        P("shard", "tensor"),
        P("shard", "tensor"),
        P("shard", "tensor"),
        P("tensor", "shard"),
        P("shard", "tensor"),
        P("shard", "tensor"),
        P("tensor", "shard"),
        P("shard", None),
        P(None, "shard"),
        P("shard", None),
        P(None, "shard"),
        P(),
        P(),
        P(),
        P(),
        P(),
        P(),
        P(),
        P(),
        P(),
        P(None, None, "tensor"),
        P(None, None, None, "tensor"),
        P(None, "tensor", None),
        P(),
        P(),
        P(None, None, None, "tensor"),
        P(None, "tensor", None),
        P(),
    )
    out_specs = (
        P("shard", "context", None),
        P("shard", "context", None),
        P(),
        P(),
        P(),
        P(),
        P(),
        P(),
        P(),
        P(),
        P(),
    )
    return jax.shard_map(body, mesh=mesh, in_specs=in_specs, out_specs=out_specs, check_vma=False)
```

```python
import functools
import math

import jax
import jax.numpy as jnp
from jax import lax
from jax.experimental import pallas as pl
from jax.experimental.pallas import tpu as pltpu
from jax.sharding import PartitionSpec as P

WINDOW = 512
EPSILON = 1e-06
ROOT_HALF = 0.7071067811865476
GELU_SCALE = math.sqrt(2.0 / math.pi)
GELU_CUBE = 0.044715

MESH = pl.DeviceIdType.MESH


def shifted(array, axis, by):
    count = lax.axis_size(axis)
    pairs = [(i, i + by) for i in range(count) if 0 <= i + by < count]
    return lax.ppermute(array, axis, pairs)


def swap(array):
    return lax.ppermute(array, "tensor", [(0, 1), (1, 0)])


def rope_tables(positions, head_size):
    frequency = jnp.exp(
        jnp.arange(head_size // 2, dtype=jnp.float32) * (-2.0 * math.log(10000.0) / head_size)
    )
    angles = positions.astype(jnp.float32)[..., None] * frequency
    return (jnp.cos(angles), jnp.sin(angles))


def low(values):
    return values.astype(jnp.bfloat16)


def wide(values):
    return values.astype(jnp.float32)


def dot(left, right):
    return lax.dot_general(left, right, (((1,), (0,)), ((), ())), preferred_element_type=jnp.float32)


def dot_t(left, right):
    return lax.dot_general(left, right, (((1,), (1,)), ((), ())), preferred_element_type=jnp.float32)


def dot_o(left, right):
    return lax.dot_general(left, right, (((0,), (0,)), ((), ())), preferred_element_type=jnp.float32)


def row_mean(values):
    return jnp.mean(values, axis=-1, keepdims=True)


def inverse_rms(values):
    return lax.rsqrt(row_mean(values * values) + EPSILON)


def rms_back(values, inverse, scaled):
    return inverse * scaled - values * (inverse * inverse * inverse * row_mean(values * scaled))


def gelu_parts(values):
    squared = values * values
    bend = jnp.tanh(GELU_SCALE * values * (1.0 + GELU_CUBE * squared))
    rise = 0.5 * (1.0 + bend)
    slope = rise + 0.5 * values * (1.0 - bend * bend) * (GELU_SCALE * (1.0 + 3.0 * GELU_CUBE * squared))
    return values * rise, slope


def greet_all(shards, places, ends):
    z = lax.axis_index("shard")
    barrier = pltpu.get_barrier_semaphore()

    def signal(place):
        pl.semaphore_signal(barrier, inc=1, device_id=place, device_id_type=MESH)

    for place in places:
        signal(place)
    peers = len(places)
    if ends:

        @pl.when(z > 0)
        def _():
            signal({"shard": z - 1})

        @pl.when(z < shards - 1)
        def _():
            signal({"shard": z + 1})

        peers = peers + lax.div(z + shards - 1, shards) + lax.div(2 * shards - 2 - z, shards)
    pl.semaphore_wait(barrier, peers)


def context_partners():
    c = lax.axis_index("context")
    return lax.rem(c + 2, 4), c + 1 - 2 * lax.rem(c, 2)


def sharer(pack, whole, inbox, turn_in, turn_out, piece, semaphores, shards):
    (
        pre_send, pre_recv, z_send, z_recv, x_send, x_recv, y_send, y_recv, near_send, near_recv,
        far_send, far_recv, keep_sem,
    ) = semaphores
    z, c, side = (lax.axis_index(a) for a in ("shard", "context", "tensor"))
    across, beside = context_partners()
    opposite = lax.rem(beside + 2, 4)
    columns = piece.shape[1]

    def cols(q):
        return pl.ds(pl.multiple_of(q * columns, 128), columns)

    def region(t, s, q):
        return whole.at[t, s, :, cols(q)]

    def copy(source, target, send, recv, place):
        return pltpu.make_async_remote_copy(
            src_ref=source, dst_ref=target, send_sem=send, recv_sem=recv, device_id=place, device_id_type=MESH
        )

    def halves(k):
        q = beside if k == 0 else opposite
        return copy(pack.at[:, cols(q)], inbox.at[k], pre_send.at[k], pre_recv.at[k], {"context": beside})

    def turned():
        return copy(turn_out, turn_in, pre_send.at[2], pre_recv.at[2], {"context": across})

    def z_copy(t, s, source, sender, by):
        return copy(source, region(t, s, c), z_send.at[t, sender], z_recv.at[t, s], {"shard": z + by})

    def passed(t, s, by):
        return z_copy(t, s, region(t, s, c), s, by)

    def x_copy(source, t):
        return copy(source, region(t, z, c), x_send, x_recv, {"tensor": 1 - side})

    def y_copy(t, s, source, q):
        return copy(source, region(t, s, q), y_send.at[t, s], y_recv.at[t, s], {"context": across})

    def near_copy(t, s, source, q):
        return copy(source, region(t, s, q), near_send.at[t, s], near_recv.at[t, s], {"context": beside})

    def far_copy(t, s, q):
        at = region(t, s, q)
        return copy(at, at, far_send.at[t, s], far_recv.at[t, s], {"context": beside})

    def keep():
        return pltpu.make_async_copy(piece, region(side, z, c), keep_sem)

    def start():
        for k in range(2):
            halves(k).start()

    def turn():
        for k in range(2):
            halves(k).wait_recv()
        turn_out[...] = low(pack[:, cols(across)] + inbox[1])
        turned().start()

    def settle():
        turned().wait_recv()
        piece[...] = low(pack[:, cols(c)] + inbox[0] + wide(turn_in[...]))
        keep().start()
        x_copy(piece, side).start()
        set_out(side, piece)

    def set_out(t, source):
        @pl.when(z < shards - 1)
        def _():
            z_copy(t, z, source, z, 1).start()

        @pl.when(z > 0)
        def _():
            z_copy(t, z, source, shards, -1).start()

        y_copy(t, z, source, c).start()
        near_copy(t, z, source, c).start()

    def cross_over():
        at = region(1 - side, z, c)
        x_copy(at, 1 - side).wait_recv()
        set_out(1 - side, at)

    def hop(d):
        def one(t, s, by, last):
            passed(t, s, by).wait_recv()

            @pl.when(z != last)
            def _():
                passed(t, s, by).start()

            at = region(t, s, c)
            y_copy(t, s, at, c).start()
            near_copy(t, s, at, c).start()

        @pl.when(z >= d)
        def _():
            for t in (side, 1 - side):
                one(t, z - d, 1, shards - 1)

        @pl.when(z + d <= shards - 1)
        def _():
            for t in (side, 1 - side):
                one(t, z + d, -1, 0)

    def hops(first):
        lax.fori_loop(first, shards, lambda d, carry: (hop(d), carry)[1], 0)

    def every(act):
        def one(s, carry):
            for t in range(2):
                act(t, s)
            return carry

        lax.fori_loop(0, shards, one, 0)

    def spread():
        def act(t, s):
            y_copy(t, s, region(t, s, across), across).wait_recv()
            far_copy(t, s, across).start()

        every(act)

    def finish():
        def act(t, s):
            near_copy(t, s, region(t, s, beside), beside).wait_recv()
            far_copy(t, s, opposite).wait_recv()
            y_copy(t, s, region(t, s, c), c).wait_send()
            near_copy(t, s, region(t, s, c), c).wait_send()
            far_copy(t, s, across).wait_send()

        every(act)

        def sent(t, s):
            @pl.when((s <= z) & (z < shards - 1))
            def _():
                passed(t, s, 1).wait_send()

            @pl.when((s > z) & (z > 0))
            def _():
                passed(t, s, -1).wait_send()

        every(sent)

        @pl.when(z > 0)
        def _():
            for t in range(2):
                z_copy(t, z, piece, shards, -1).wait_send()

        x_copy(piece, side).wait_send()

        for k in range(2):
            halves(k).wait_send()
        turned().wait_send()
        keep().wait()

    return start, turn, settle, hop, hops, cross_over, spread, finish


def sharer_scratch(rows, columns, shards):
    part = columns // 4
    dma = pltpu.SemaphoreType.DMA
    return [
        pltpu.VMEM((2, rows, part), jnp.float32),
        pltpu.VMEM((rows, part), jnp.bfloat16),
        pltpu.VMEM((rows, part), jnp.bfloat16),
        pltpu.VMEM((rows, part), jnp.bfloat16),
        dma((3,)), dma((3,)), dma((2, shards + 1)), dma((2, shards)), dma, dma,
        dma((2, shards)), dma((2, shards)), dma((2, shards)), dma((2, shards)), dma((2, shards)), dma((2, shards)),
        dma,
    ]


def tail_kernel(
    shards,
    grad_query, w_query, w_key, w_value, code_attn, normed, query_out, kv_out, attn_in,
    out_in_term, out_out_term, tokens, gain_in, grad_comb, grad_normed,
    own_kv, came_kv, lin_kv, cosine, sine, gain_key,
    input_grad_out, whole,
    pack, mine, sent, got, result, grad_key, grad_value, send_sem, recv_sem, keep_sem, *shared,
):
    side = lax.axis_index("tensor")
    partner = {"tensor": 1 - side}
    across, beside = context_partners()
    count, width = normed.shape
    half = count // 2
    quarter = half // 2
    rank = query_out.shape[0]
    start, turn, settle, hop, hops, cross_over, spread, finish = sharer(
        pack, whole, shared[0], shared[1], shared[2], shared[3], shared[4:], shards
    )
    greet_all(shards, [partner, {"context": across}, {"context": beside}], True)
    keys = grad_key.shape[1]
    values = lin_kv[:, :keys]
    turned = unrotate(own_kv[0] + wide(came_kv[0]), cosine[...], sine[...]) * gain_key[...]
    grad_key[...] = low(rms_back(values, inverse_rms(values), turned))
    values = lin_kv[:, keys:]
    grad_value[...] = low(rms_back(values, inverse_rms(values), own_kv[1] + wide(came_kv[1])))
    parts = ((grad_query, w_query, query_out[...]), (grad_key, w_key, kv_out[0]), (grad_value, w_value, kv_out[1]))
    at = 0

    def put(term):
        nonlocal at
        pack[:, at : at + term.shape[1]] = term
        at += term.shape[1]

    put(out_in_term[...])
    put(out_out_term[...])
    backs = []
    for i, (grad, _, table) in enumerate(parts):
        put(dot_o(code_attn[:, i * rank : (i + 1) * rank], grad[...]))
        backs.append(low(dot_t(grad[...], table)))
    for back in backs:
        put(dot_o(back, normed[...]))
    start()

    def product(here):
        total = dot_t(grad_query[here, :], w_query[...])
        total += dot_t(grad_key[here, :], w_key[...]) + dot_t(grad_value[here, :], w_value[...])
        for i, (grad, _, table) in enumerate(parts):
            back = low(dot_t(grad[here, :], table))
            total += dot(back, attn_in[i * rank : (i + 1) * rank, :])
        return total

    def send(source, target, k):
        return pltpu.make_async_remote_copy(
            src_ref=source, dst_ref=target, send_sem=send_sem.at[k], recv_sem=recv_sem.at[k],
            device_id=partner, device_id_type=MESH,
        )

    def rows(k):
        return pl.ds(k * quarter, quarter)

    def rows_of(owner, k):
        return pl.ds(pl.multiple_of(owner * half + k * quarter, quarter), quarter)

    swaps = []
    for k in range(2):
        sent[rows(k), :] = low(product(rows_of(1 - side, k)))
        swaps.append(send(sent.at[rows(k), :], got.at[rows(k), :], k))
        swaps[k].start()
    turn()
    for k in range(2):
        mine[rows(k), :] = product(rows_of(side, k))
        if k == 0:
            settle()
    cross_over()
    ends = []
    for k in range(2):
        swaps[k].wait_recv()
        here = rows(k)
        grad = (grad_normed[here, :] + mine[here, :] + wide(got[here, :])) * gain_in[...]
        token = wide(tokens[here, :])
        there = rows_of(side, k)
        result[there, :] = low(grad_comb[here, :] + rms_back(token, inverse_rms(token), grad))
        ends.append(send(result.at[there, :], result.at[there, :], 2 + k))
        ends[k].start()
        if k == 0:
            hop(1)
    hops(2)
    spread()
    for end in ends:
        end.wait()
    keep = pltpu.make_async_copy(result, input_grad_out, keep_sem)
    keep.start()
    for swap_part in swaps:
        swap_part.wait_send()
    finish()
    keep.wait()


def tail(arrays, shards):
    count, width = arrays[5].shape
    rank = arrays[6].shape[0]
    half = count // 2
    queries, keys = arrays[0].shape[1], arrays[2].shape[1]
    columns = 2 * queries + 2 * keys + 4 * width
    bf16, f32 = jnp.bfloat16, jnp.float32
    anywhere, vmem = pl.BlockSpec(memory_space=pl.ANY), pl.BlockSpec(memory_space=pltpu.VMEM)
    return pl.pallas_call(
        functools.partial(tail_kernel, shards),
        out_shape=[
            jax.ShapeDtypeStruct((count, width), bf16),
            jax.ShapeDtypeStruct((2, shards, rank, columns), bf16),
        ],
        in_specs=[vmem] * len(arrays),
        out_specs=[anywhere] * 2,
        scratch_shapes=[
            pltpu.VMEM((rank, columns), f32),
            pltpu.VMEM((half, width), f32),
            pltpu.VMEM((half, width), bf16),
            pltpu.VMEM((half, width), bf16),
            pltpu.VMEM((count, width), bf16),
            pltpu.VMEM((count, keys), bf16),
            pltpu.VMEM((count, keys), bf16),
            pltpu.SemaphoreType.DMA((4,)),
            pltpu.SemaphoreType.DMA((4,)),
            pltpu.SemaphoreType.DMA,
        ]
        + sharer_scratch(rank, columns, shards),
        compiler_params=pltpu.CompilerParams(
            collective_id=3, has_side_effects=True, vmem_limit_bytes=60 * 2**20
        ),
    )(*arrays)


def allowed_bias(seg_rows, seg_cols, keys):
    count = seg_rows.shape[0]
    shape = (count, keys)
    distance = lax.broadcasted_iota(jnp.int32, shape, 0) + (keys - count) - lax.broadcasted_iota(jnp.int32, shape, 1)
    seen = (seg_rows[...] == seg_cols[...]) & (distance >= 0) & (distance < WINDOW)
    return jnp.where(seen, 0.0, -1e30)


def unrotate(grad, cosine, sine):
    middle = grad.shape[1] // 2
    former, latter = grad[:, :middle], grad[:, middle:]
    return jnp.concatenate([former * cosine + latter * sine, latter * cosine - former * sine], axis=1)


def attend_back_kernel(
    scale, grad, w_out, out_in, out_out, code_out, attended, query, prior, own, log_total, seg_rows, seg_cols, lin,
    cosine, sine, gain_query,
    grad_query, sent_kv, own_kv, term_in, term_out, bias, back, grad_k, grad_v,
):
    count = query.shape[0]
    head = pl.program_id(0)

    @pl.when(head == 0)
    def _():
        bias[...] = allowed_bias(seg_rows, seg_cols, 2 * count)
        back[...] = low(dot_t(grad[...], out_out[...]))
        term_out[...] = dot_o(code_out[...], grad[...])
        grad_k[...] = jnp.zeros_like(grad_k)
        grad_v[...] = jnp.zeros_like(grad_v)

    top = low(dot_t(grad[...], w_out[...]) + dot(back[...], out_in[...]))
    term_in[...] = dot_o(back[...], attended[...])
    probs, slopes, mean = [], [], 0.0
    for i, kv in enumerate((prior, own)):
        score = dot_t(query[...], kv[0]) * scale + bias[:, i * count : (i + 1) * count]
        probs.append(jnp.exp(score - log_total[...]))
        slopes.append(dot_t(top, kv[1]))
        mean += jnp.sum(probs[i] * slopes[i], axis=-1, keepdims=True)
    turned = 0.0
    for i, kv in enumerate((prior, own)):
        grad_score = low(probs[i] * (slopes[i] - mean))
        turned += dot(grad_score, kv[0])
        grad_k[i] += dot_o(grad_score, query[...]) * scale
        grad_v[i] += dot_o(low(probs[i]), top)
    values = lin[...]
    turned = unrotate(turned * scale, cosine[...], sine[...]) * gain_query[...]
    grad_query[...] = low(rms_back(values, inverse_rms(values), turned))

    @pl.when(head == pl.num_programs(0) - 1)
    def _():
        sent_kv[0] = low(grad_k[0])
        sent_kv[1] = low(grad_v[0])
        own_kv[0] = grad_k[1]
        own_kv[1] = grad_v[1]


def attend_back(
    grad, w_out, out_in, out_out, code_out, attended, query, prior, own, log_total, seg_rows, seg_cols, lin,
    cosine, sine, gain_query, scale,
):
    count, inner = query.shape
    width = grad.shape[1]
    head = gain_query.shape[1]
    rank = out_in.shape[0]
    bf16, f32 = jnp.bfloat16, jnp.float32
    whole = lambda *shape: pl.BlockSpec(shape, lambda h: (0,) * len(shape))
    column = lambda rows: pl.BlockSpec((rows, head), lambda h: (0, h))
    return pl.pallas_call(
        functools.partial(attend_back_kernel, scale),
        grid=(inner // head,),
        in_specs=[
            whole(count, width),
            pl.BlockSpec((head, width), lambda h: (h, 0)),
            column(rank),
            whole(rank, width),
            whole(count, rank),
            column(count),
            column(count),
            whole(2, count, head),
            whole(2, count, head),
            pl.BlockSpec((None, count, 1), lambda h: (h, 0, 0)),
            whole(count, 1),
            whole(1, 2 * count),
            column(count),
            whole(count, head // 2),
            whole(count, head // 2),
            whole(1, head),
        ],
        out_specs=[column(count), whole(2, count, head), whole(2, count, head), column(rank), whole(rank, width)],
        out_shape=[
            jax.ShapeDtypeStruct((count, inner), bf16),
            jax.ShapeDtypeStruct((2, count, head), bf16),
            jax.ShapeDtypeStruct((2, count, head), f32),
            jax.ShapeDtypeStruct((rank, inner), f32),
            jax.ShapeDtypeStruct((rank, width), f32),
        ],
        scratch_shapes=[
            pltpu.VMEM((count, 2 * count), f32),
            pltpu.VMEM((count, rank), bf16),
            pltpu.VMEM((2, count, head), f32),
            pltpu.VMEM((2, count, head), f32),
        ],
        compiler_params=pltpu.CompilerParams(vmem_limit_bytes=56 * 2**20),
    )(
        grad, w_out, out_in, out_out, code_out, attended, query, prior, own, log_total, seg_rows, seg_cols, lin,
        cosine, sine, gain_query,
    )


def tables_kernel(
    queries, keys, early, late, output_own, output_other,
    output, out_attn, out_query, out_kv, out_out_in, out_out_out, out_ffn, out_gu, out_down_in, out_down_out,
    marks, drawn, laid, spots, placing, mark_sem, drawn_sem, laid_sem, output_sem,
):
    side = lax.axis_index("tensor")
    shards, rank = early.shape[1], early.shape[2]
    half, width = output_own.shape
    puts = []
    for i, (rows, owner) in enumerate(((output_own, side), (output_other, 1 - side))):
        there = output.at[pl.ds(pl.multiple_of(owner * half, half), half), :]
        puts.append(pltpu.make_async_copy(rows, there, output_sem.at[i]))
        puts[i].start()
    adapters, hidden = out_gu.shape[0], out_gu.shape[3] // 2
    wide_at = early.shape[3] - 512
    get_marks = pltpu.make_async_copy(early.at[0, :, :, pl.ds(wide_at, 128)], marks, mark_sem)
    get_marks.start()
    span = drawn.shape[4]
    def both(source, at, columns, table, inner):
        found = []
        for first in range(0, columns, span):
            size = min(span, columns - first)
            found.append(
                (source, at + first, size, [table(t * inner + first, size) for t in range(2)])
            )
        return found

    def gu_table(i):
        return lambda at, size: out_gu.at[:, i, :, pl.ds(at, size)]

    def kv_table(i):
        return lambda at, size: out_kv.at[:, i, :, pl.ds(at, size)]

    def plain(out, row=0):
        return lambda at, size: out.at[:, pl.ds(row, rank), pl.ds(at, size)]

    def single(source, at, out, row=0):
        return [
            (source, at + first, span, [plain(out, row)(first, span)]) for first in range(0, width, span)
        ]

    early_units = both(early, 0, hidden, gu_table(0), hidden) + both(early, hidden, hidden, gu_table(1), hidden)
    early_units += both(early, 2 * hidden, hidden, plain(out_down_in), hidden)
    early_units += single(early, 3 * hidden, out_ffn) + single(early, 3 * hidden + width, out_ffn, rank)
    early_units += single(early, 3 * hidden + 2 * width, out_down_out)
    late_units = both(late, 0, queries, plain(out_out_in), queries) + single(late, queries, out_out_out)
    late_units += both(late, queries + width, queries, plain(out_query), queries)
    late_units += both(late, 2 * queries + width, keys, kv_table(0), keys)
    late_units += both(late, 2 * queries + width + keys, keys, kv_table(1), keys)
    for i in range(3):
        late_units += single(late, 2 * queries + (1 + i) * width + 2 * keys, out_attn, i * rank)
    units = early_units + late_units

    def draw(u):
        source, at, size, _ = units[u]
        return pltpu.make_async_copy(
            source.at[:, :, :, pl.ds(at, size)], drawn.at[u % 2, :, :, :, pl.ds(0, size)], drawn_sem.at[u % 2]
        )

    def lays(u):
        _, _, size, targets = units[u]
        return [
            pltpu.make_async_copy(laid.at[u % 2, t, :, :, pl.ds(0, size)], target, laid_sem.at[u % 2, t])
            for t, target in enumerate(targets)
        ]

    def lay_out(u, last):
        if u + 1 < last:
            draw(u + 1).start()
        draw(u).wait()
        if u >= 2:
            for lay in lays(u - 2):
                lay.wait()
        _, _, size, targets = units[u]
        slot = u % 2
        for t in range(len(targets)):
            terms = drawn[slot, t, :, :, :size].reshape(shards * rank, size)
            total = dot(placing[...], terms)
            if len(targets) == 1:
                total += dot(placing[...], drawn[slot, 1, :, :, :size].reshape(shards * rank, size))
            laid[slot, t, :, :, :size] = total.reshape(adapters, rank, size)
        for lay in lays(u):
            lay.start()

    draw(0).start()
    get_marks.wait()
    same = lax.broadcasted_iota(jnp.int32, (rank, rank), 0) == lax.broadcasted_iota(jnp.int32, (rank, rank), 1)
    same = same.astype(jnp.float32)
    for q in range(shards):
        mark = wide(marks[q])
        for k in range(adapters):
            spots[k * rank : (k + 1) * rank, q * rank : (q + 1) * rank] = same * mark[:, k : k + 1]
    placing[...] = low(spots[...])
    for u in range(len(units)):
        lay_out(u, len(units))
    for u in (len(units) - 2, len(units) - 1):
        for lay in lays(u):
            lay.wait()
    for put in puts:
        put.wait()


def tables(early, late, output_own, output_other, queries, keys, adapters, hidden):
    half, width = output_own.shape
    shards, rank = early.shape[1], early.shape[2]
    span = 2048
    bf16, f32 = jnp.bfloat16, jnp.float32
    anywhere, vmem = pl.BlockSpec(memory_space=pl.ANY), pl.BlockSpec(memory_space=pltpu.VMEM)
    return pl.pallas_call(
        functools.partial(tables_kernel, queries, keys),
        out_shape=[jax.ShapeDtypeStruct((2 * half, width), bf16)]
        + [
            jax.ShapeDtypeStruct((adapters,) + rest, f32)
            for rest in (
                (3 * rank, width), (rank, 2 * queries), (2, rank, 2 * keys), (rank, 2 * queries), (rank, width),
                (2 * rank, width), (2, rank, 2 * hidden), (rank, 2 * hidden), (rank, width),
            )
        ],
        in_specs=[anywhere] * 2 + [vmem] * 2,
        out_specs=[anywhere] * 10,
        scratch_shapes=[
            pltpu.VMEM((shards, rank, 128), bf16),
            pltpu.VMEM((2, 2, shards, rank, span), bf16),
            pltpu.VMEM((2, 2, adapters, rank, span), f32),
            pltpu.VMEM((adapters * rank, shards * rank), f32),
            pltpu.VMEM((adapters * rank, shards * rank), bf16),
            pltpu.SemaphoreType.DMA,
            pltpu.SemaphoreType.DMA((2,)),
            pltpu.SemaphoreType.DMA((2, 2)),
            pltpu.SemaphoreType.DMA((2,)),
        ],
        compiler_params=pltpu.CompilerParams(vmem_limit_bytes=60 * 2**20),
    )(early, late, output_own, output_other)


def aft_kernel(
    shards, block, strip,
    full_gate, full_up, full_down, gate_in, up_in,
    part, combined, per_layer, cotangent, lgate, lproj, code_ffn, code_down, ffn, down_in, down_out, gu_out, ffn_in,
    attn_proj, laurel_mid, left, right, mark, gain_post, gain_layer, gain_pre, gain_attn, gain_laurel,
    grad_attn_out, whole, output, grad_comb, grad_normed, pack,
    got, grad, grad_gate, grad_up, down_w, gate_v, up_v, gate_w, up_w, mine, sent, came, attn, back_codes, ffn_codes,
    fetch_sem, strip_sem, keep_sem, send_sem, recv_sem, *shared,
):
    side = lax.axis_index("tensor")
    partner = {"tensor": 1 - side}
    across, beside = context_partners()
    greet_all(shards, [partner, {"context": across}, {"context": beside}], True)
    start, turn, settle, hop, hops, cross_over, spread, finish = sharer(
        pack, whole, shared[0], shared[1], shared[2], shared[3], shared[4:], shards
    )
    count, width = grad.shape
    half = count // 2
    quarter = half // 2
    rank = down_in.shape[0]
    hidden = grad_gate.shape[1]
    steps = hidden // block
    strips = width // strip

    def send(source, target, k):
        return pltpu.make_async_remote_copy(
            src_ref=source, dst_ref=target, send_sem=send_sem.at[k], recv_sem=recv_sem.at[k],
            device_id=partner, device_id_type=MESH,
        )

    def rows(k):
        return pl.ds(k * quarter, quarter)

    down_swaps = [send(part.at[rows(2 + k), :], got.at[rows(k), :], k) for k in range(2)]
    grad_swaps = [send(grad.at[rows(k), :], grad.at[rows(2 + k), :], 2 + k) for k in range(2)]
    for swap_down in down_swaps:
        swap_down.start()

    def fetches(t):
        slot, j = lax.rem(t, 2), lax.rem(t, steps)
        at = pl.ds(pl.multiple_of(j * block, block), block)
        here = pl.ds(pl.multiple_of(lax.div(t, steps) * half, half), half)
        return (
            pltpu.make_async_copy(full_down.at[at, :], down_w.at[slot], fetch_sem.at[0, slot]),
            pltpu.make_async_copy(gate_in.at[here, at], gate_v.at[slot], fetch_sem.at[1, slot]),
            pltpu.make_async_copy(up_in.at[here, at], up_v.at[slot], fetch_sem.at[2, slot]),
        )

    def strip_fetches(k):
        slot = lax.rem(k, 2)
        at = pl.ds(pl.multiple_of(k * strip, strip), strip)
        return (
            pltpu.make_async_copy(full_gate.at[at, :], gate_w.at[slot], strip_sem.at[0, slot]),
            pltpu.make_async_copy(full_up.at[at, :], up_w.at[slot], strip_sem.at[1, slot]),
        )

    for fetch in fetches(0) + strip_fetches(0):
        fetch.start()
    pack[...] = jnp.zeros_like(pack)
    ffn_codes[...] = jnp.zeros_like(ffn_codes)

    for k in range(2):
        down_swaps[k].wait_recv()
        at = rows(k)
        down = wide(part[at, :]) + wide(got[at, :])
        down_inverse = inverse_rms(down)
        after = combined[at, :] + down * down_inverse * gain_post[...]
        mixing = wide(per_layer[at, :])
        act, slope = gelu_parts(dot(low(after), lgate[...]))
        proj = dot(low(act * mixing), lproj[...])
        proj_inverse = inverse_rms(proj)
        output[at, :] = low(after + proj * proj_inverse * gain_layer[...])
        top = wide(cotangent[at, :])
        grad_proj = rms_back(proj, proj_inverse, top * gain_layer[...])
        grad_mix = dot_t(low(grad_proj), lproj[...]) * mixing * slope
        top = top + dot_t(low(grad_mix), lgate[...])
        grad_comb[at, :] = top
        grad[at, :] = low(rms_back(down, down_inverse, top * gain_post[...]))
        grad_swaps[k].start()
        back_codes[at, :] = low(dot_t(grad[at, :], down_out[...]))

    def level(t, carry):
        @pl.when(t + 1 < 2 * steps)
        def _():
            for fetch in fetches(t + 1):
                fetch.start()

        @pl.when(t == steps)
        def _():
            for k in range(2):
                grad_swaps[k].wait_recv()
            back_codes[half:, :] = low(dot_t(grad[half:, :], down_out[...]))

        slot, j = lax.rem(t, 2), lax.rem(t, steps)
        at = pl.ds(pl.multiple_of(j * block, block), block)
        here = pl.ds(pl.multiple_of(lax.div(t, steps) * half, half), half)
        for fetch in fetches(t):
            fetch.wait()
        back = back_codes[here, :]
        hidden_grad = dot_t(grad[here, :], down_w[slot]) + dot(back, down_in[:, at])
        up_now = wide(up_v[slot])
        act, slope = gelu_parts(wide(gate_v[slot]))
        grad_g = low(hidden_grad * up_now * slope)
        grad_u = low(hidden_grad * act)
        grad_gate[here, at] = grad_g
        grad_up[here, at] = grad_u
        ffn_codes[0, here, :] += dot_t(grad_g, gu_out[0, :, at])
        ffn_codes[1, here, :] += dot_t(grad_u, gu_out[1, :, at])
        codes = code_ffn[here, :]

        def put(i, term):
            pack[:, pl.ds(pl.multiple_of(i * hidden + j * block, block), block)] += term

        put(0, dot_o(codes[:, :rank], grad_g))
        put(1, dot_o(codes[:, rank:], grad_u))
        put(2, dot_o(back, low(act * up_now)))
        return carry

    lax.fori_loop(0, 2 * steps, level, 0)
    base = 3 * hidden
    pack[:, base : base + width] = dot_o(low(ffn_codes[0]), ffn[...])
    pack[:, base + width : base + 2 * width] = dot_o(low(ffn_codes[1]), ffn[...])
    pack[:, base + 2 * width : base + 3 * width] = dot_o(code_down[...], grad[...])
    pack[:, base + 3 * width :] = mark[...]
    start()

    def strip_send(k):
        return send(sent.at[k], came.at[k], 4 + k)

    def cross(k, carry):
        @pl.when(k + 1 < strips)
        def _():
            for fetch in strip_fetches(k + 1):
                fetch.start()

        slot = lax.rem(k, 2)
        at = pl.ds(pl.multiple_of(k * strip, strip), strip)
        for fetch in strip_fetches(k):
            fetch.wait()
        result = (
            dot_t(grad_gate[...], gate_w[slot])
            + dot_t(grad_up[...], up_w[slot])
            + dot(low(ffn_codes[0]), ffn_in[:rank, at])
            + dot(low(ffn_codes[1]), ffn_in[rank:, at])
        )
        sent[k] = low(result[half:])
        strip_send(k).start()
        mine[:, at] = result[:half]
        for when, act in (
            (1, turn), (2, settle), (4, cross_over), (7, lambda: hop(1)),
        ):
            pl.when(k == when)(act)
        return carry

    lax.fori_loop(0, strips, cross, 0)
    hop(2)

    def add(k, carry):
        at = pl.ds(pl.multiple_of(k * strip, strip), strip)
        strip_send(k).wait_recv()
        mine[:, at] += wide(came[k])
        return carry

    lax.fori_loop(0, strips, add, 0)
    hops(3)
    attn_swaps = []
    for k in range(2):
        at = rows(k)
        comb = combined[at, :]
        top = (grad_comb[at, :] + rms_back(comb, inverse_rms(comb), mine[at, :] * gain_pre[...])) * ROOT_HALF
        grad_comb[at, :] = top
        proj = attn_proj[at, :]
        there = pl.ds(pl.multiple_of(side * half + k * quarter, quarter), quarter)
        attn[there, :] = low(rms_back(proj, inverse_rms(proj), top * gain_attn[...]))
        attn_swaps.append(send(attn.at[there, :], attn.at[there, :], 4 + strips + k))
        attn_swaps[k].start()
        end = dot(laurel_mid[at, :], right[...])
        grad_end = low(rms_back(end, inverse_rms(end), top * gain_laurel[...]))
        grad_normed[at, :] = top + dot(low(dot_t(grad_end, right[...])), left[...])
    spread()
    for swap_attn in attn_swaps:
        swap_attn.wait()
    keep = pltpu.make_async_copy(attn, grad_attn_out, keep_sem)
    keep.start()
    for k in range(2):
        down_swaps[k].wait_send()
        grad_swaps[k].wait_send()

    def flush(k, carry):
        strip_send(k).wait_send()
        return carry

    lax.fori_loop(0, strips, flush, 0)
    finish()
    keep.wait()


def aft(weights, kept, arrays, shards):
    full_gate = weights[0]
    part, combined, per_layer = arrays[:3]
    count, width = part.shape
    hidden = full_gate.shape[1]
    half = count // 2
    rank = arrays[9].shape[0]
    block, strip = min(512, hidden), 256
    strips = width // strip
    columns = 3 * hidden + 3 * width + arrays[17].shape[1]
    bf16, f32 = jnp.bfloat16, jnp.float32
    shape = jax.ShapeDtypeStruct
    anywhere, vmem = pl.BlockSpec(memory_space=pl.ANY), pl.BlockSpec(memory_space=pltpu.VMEM)
    return pl.pallas_call(
        functools.partial(aft_kernel, shards, block, strip),
        out_shape=[
            shape((count, width), bf16),
            shape((2, shards, rank, columns), bf16),
            shape((half, width), bf16),
            shape((half, width), f32),
            shape((half, width), f32),
        ],
        in_specs=[anywhere] * 5 + [vmem] * len(arrays),
        out_specs=[anywhere] * 2 + [vmem] * 3,
        scratch_shapes=[
            pltpu.VMEM((rank, columns), f32),
            pltpu.VMEM((half, width), bf16),
            pltpu.VMEM((count, width), bf16),
            pltpu.VMEM((count, hidden), bf16),
            pltpu.VMEM((count, hidden), bf16),
            pltpu.VMEM((2, block, width), bf16),
            pltpu.VMEM((2, half, block), bf16),
            pltpu.VMEM((2, half, block), bf16),
            pltpu.VMEM((2, strip, hidden), bf16),
            pltpu.VMEM((2, strip, hidden), bf16),
            pltpu.VMEM((half, width), f32),
            pltpu.VMEM((strips, half, strip), bf16),
            pltpu.VMEM((strips, half, strip), bf16),
            pltpu.VMEM((count, width), bf16),
            pltpu.VMEM((count, rank), bf16),
            pltpu.VMEM((2, count, rank), f32),
            pltpu.SemaphoreType.DMA((3, 2)),
            pltpu.SemaphoreType.DMA((2, 2)),
            pltpu.SemaphoreType.DMA,
            pltpu.SemaphoreType.DMA((6 + strips,)),
            pltpu.SemaphoreType.DMA((6 + strips,)),
        ]
        + sharer_scratch(rank, columns, shards),
        compiler_params=pltpu.CompilerParams(
            collective_id=2, has_side_effects=True, vmem_limit_bytes=60 * 2**20
        ),
        cost_estimate=pl.CostEstimate(
            flops=6 * count * width * hidden, bytes_accessed=8 * width * hidden, transcendentals=count * hidden
        ),
    )(*weights, *kept, *arrays)


def mover(sources, fulls, semaphores, shards):
    z_recv, y_recv, near_recv, far_recv, z_send, y_send, near_send, far_send = semaphores
    z, c = lax.axis_index("shard"), lax.axis_index("context")
    across = lax.rem(c + 2, 4)
    beside = c + 1 - 2 * lax.rem(c, 2)

    def greet(also=(), row=False):
        barrier = pltpu.get_barrier_semaphore()

        def signal(place):
            pl.semaphore_signal(barrier, inc=1, device_id=place, device_id_type=MESH)

        signal({"context": across})
        signal({"context": beside})
        for place in also:
            signal(place)

        @pl.when(z > 0)
        def _():
            signal({"shard": z - 1})

        @pl.when(z < shards - 1)
        def _():
            signal({"shard": z + 1})

        peers = 2 + len(also) + lax.div(z + shards - 1, shards) + lax.div(2 * shards - 2 - z, shards)
        if row:

            @pl.when(c > 0)
            def _():
                signal({"context": c - 1})

            @pl.when(c < 3)
            def _():
                signal({"context": c + 1})

            peers = peers + lax.div(c + 3, 4) + lax.div(6 - c, 4)
        pl.semaphore_wait(barrier, peers)

    def region(piece, s, q):
        _, item, axis, row, rows, col, cols = piece
        rows_here, cols_here = sources[item].shape
        part = rows // 4
        if axis == 0:
            return fulls[item].at[
                pl.ds(pl.multiple_of(s * rows_here + row + q * part, 16), part),
                pl.ds(pl.multiple_of(col, 128), cols),
            ]
        return fulls[item].at[
            pl.ds(pl.multiple_of(row + q * part, 16), part),
            pl.ds(pl.multiple_of(s * cols_here + col, 128), cols),
        ]

    def own(piece):
        _, item, axis, row, rows, col, cols = piece
        part = rows // 4
        return sources[item].at[
            pl.ds(pl.multiple_of(row + c * part, 16), part), pl.ds(pl.multiple_of(col, 128), cols)
        ]

    def copy(source, target, send, recv, place):
        return pltpu.make_async_remote_copy(
            src_ref=source, dst_ref=target, send_sem=send, recv_sem=recv, device_id=place, device_id_type=MESH
        )

    def along(piece, s, source, sender, by):
        slot = piece[0]
        return copy(source, region(piece, s, c), z_send.at[slot, sender], z_recv.at[slot, s], {"shard": z + by})

    def passed(piece, s, by):
        return along(piece, s, region(piece, s, c), s, by)

    def y_copy(piece, s, q):
        at = region(piece, s, q)
        return copy(at, at, y_send.at[piece[0], s], y_recv.at[piece[0], s], {"context": across})

    def near_copy(piece, s, q):
        at = region(piece, s, q)
        return copy(at, at, near_send.at[piece[0], s], near_recv.at[piece[0], s], {"context": beside})

    def far_copy(piece, s, q):
        at = region(piece, s, q)
        return copy(at, at, far_send.at[piece[0], s], far_recv.at[piece[0], s], {"context": beside})

    def begin(pieces):
        @pl.when(z < shards - 1)
        def _():
            for piece in pieces:
                along(piece, z, own(piece), z, 1).start()

        @pl.when(z > 0)
        def _():
            for piece in pieces:
                along(piece, z, own(piece), shards, -1).start()

    def relay(pieces, first=1, last=None):
        def hop(d, carry):
            @pl.when(z >= d)
            def _():
                s = z - d
                for piece in pieces:
                    passed(piece, s, 1).wait_recv()

                    @pl.when(z < shards - 1)
                    def _(piece=piece):
                        passed(piece, s, 1).start()

                    y_copy(piece, s, c).start()
                    near_copy(piece, s, c).start()

            @pl.when(z + d <= shards - 1)
            def _():
                s = z + d
                for piece in pieces:
                    passed(piece, s, -1).wait_recv()

                    @pl.when(z > 0)
                    def _(piece=piece):
                        passed(piece, s, -1).start()

                    y_copy(piece, s, c).start()
                    near_copy(piece, s, c).start()

            return carry

        last = shards - 1 if last is None else last
        if first == last:
            hop(first, 0)
        else:
            lax.fori_loop(first, last + 1, hop, 0)

    def others(pieces, act):
        def one(d, carry):
            for piece in pieces:
                act(piece, lax.rem(z + d, shards))
            return carry

        lax.fori_loop(1, shards, one, 0)

    def spread(pieces):
        def act(piece, s):
            y_copy(piece, s, across).wait_recv()
            far_copy(piece, s, across).start()

        others(pieces, act)

    def finish(pieces):
        def act(piece, s):
            near_copy(piece, s, beside).wait_recv()
            far_copy(piece, s, lax.rem(beside + 2, 4)).wait_recv()

        others(pieces, act)

    def flush(pieces):
        @pl.when(z < shards - 1)
        def _():
            for piece in pieces:
                along(piece, z, own(piece), z, 1).wait_send()

        @pl.when(z > 0)
        def _():
            for piece in pieces:
                along(piece, z, own(piece), shards, -1).wait_send()

        def act(piece, s):
            y_copy(piece, s, c).wait_send()
            near_copy(piece, s, c).wait_send()
            far_copy(piece, s, across).wait_send()

            @pl.when((s < z) & (z < shards - 1))
            def _():
                passed(piece, s, 1).wait_send()

            @pl.when((s > z) & (z > 0))
            def _():
                passed(piece, s, -1).wait_send()

        others(pieces, act)

    def own_place(item, axis):
        rows_here, cols_here = sources[item].shape
        if axis == 0:
            return fulls[item].at[pl.ds(pl.multiple_of(z * rows_here, 16), rows_here), :]
        return fulls[item].at[:, pl.ds(pl.multiple_of(z * cols_here, 128), cols_here)]

    return greet, begin, relay, spread, finish, flush, own_place


def mover_semaphores(slots, shards):
    table = pltpu.SemaphoreType.DMA((slots, shards))
    return [table, table, table, table, pltpu.SemaphoreType.DMA((slots, shards + 1)), table, table, table]


def full_shapes(weights, axes, shards):
    shapes = []
    for w, axis in zip(weights, axes):
        shape = list(w.shape)
        shape[axis] *= shards
        shapes.append(jax.ShapeDtypeStruct(tuple(shape), w.dtype))
    return shapes


def pick_kernel(chosen, *refs):
    count = len(refs) // 2
    for source, target in zip(refs[:count], refs[count:]):
        if len(source.shape) > len(target.shape):
            target[...] = source[0]
        else:
            target[...] = source[...]


def pick_rows(chosen, side, tables, arrays):
    in_specs, out_specs, shapes = [], [], []
    for t in tables:
        rest = t.shape[1:]
        in_specs.append(pl.BlockSpec((1,) + rest, lambda i, at, n=len(rest): (at[0],) + (0,) * n))
        out_specs.append(pl.BlockSpec(rest, lambda i, at, n=len(rest): (0,) * n))
        shapes.append(jax.ShapeDtypeStruct(rest, t.dtype))
    for a in arrays:
        part = (a.shape[0] // 2, a.shape[1])
        in_specs.append(pl.BlockSpec(part, lambda i, at: (at[1], 0)))
        out_specs.append(pl.BlockSpec(part, lambda i, at: (0, 0)))
        shapes.append(jax.ShapeDtypeStruct(part, a.dtype))
    return pl.pallas_call(
        pick_kernel,
        grid_spec=pltpu.PrefetchScalarGridSpec(
            num_scalar_prefetch=1, grid=(1,), in_specs=in_specs, out_specs=out_specs
        ),
        out_shape=shapes,
        compiler_params=pltpu.CompilerParams(vmem_limit_bytes=61 * 2**20),
    )(jnp.stack([chosen, side]), *tables, *arrays)


FRONT_AXES = (0, 0, 0, 1, 1, 1, 0, 1)


def front_kernel(
    shards, *refs
):
    sources, rest = refs[:8], refs[8:]
    (tokens, attn_in, query_out, kv_out, cosine, sine, seg_rows, seg_cols, gain_in, gain_query, gain_key), rest = (
        rest[:11], rest[11:]
    )
    fulls, rest = rest[:8], rest[8:]
    (normed, code_attn, lin, lin_kv, query_rot, kv_rot, prior_out, attended, log_total), rest = rest[:9], rest[9:]
    held, rest = rest[:8], rest[8:]
    query_w, key_w, value_w, own, prior, bias, load_sem, store_sem, weight_sem, shift_sem, *semaphores = rest
    c = lax.axis_index("context")
    greet, begin, relay, spread, finish, flush, own_place = mover(sources, fulls, semaphores, shards)
    pieces = [(i, i, FRONT_AXES[i], 0, sources[i].shape[0], 0, sources[i].shape[1]) for i in range(8)]
    needed, further = pieces[:4], pieces[4:]
    greet(row=True)
    begin(needed)
    loads = [pltpu.make_async_copy(sources[i], held[i], load_sem.at[i]) for i in range(8)]
    stores = [pltpu.make_async_copy(held[i], own_place(i, FRONT_AXES[i]), store_sem.at[i]) for i in range(8)]
    for load in loads:
        load.start()
    for load, store in zip(loads, stores):
        load.wait()
        store.start()
    count = tokens.shape[0]
    rows = 64

    def norm(i, carry):
        at = pl.ds(pl.multiple_of(i * rows, rows), rows)
        token = wide(tokens[at, :])
        normed[at, :] = low(token * inverse_rms(token) * gain_in[...])
        return carry

    relay(needed, 1, 1)
    begin(further)
    lax.fori_loop(0, count // rows, norm, 0)
    code_attn[...] = low(dot_t(normed[...], attn_in[...]))
    relay(needed, 2)
    bias[...] = allowed_bias(seg_rows, seg_cols, 2 * count)

    @pl.when(c == 0)
    def _():
        prior[...] = jnp.zeros_like(prior)

    relay(further, 1, 1)
    spread(needed)
    finish(needed)
    for store in stores:
        store.wait()
    bring = [
        pltpu.make_async_copy(full, w, weight_sem.at[i])
        for i, (full, w) in enumerate(zip(fulls[:3], (query_w, key_w, value_w)))
    ]
    for copy in bring:
        copy.start()
    head = gain_query.shape[1]
    middle = head // 2
    rank = query_out.shape[0]
    queries, keys = query_w.shape[1], key_w.shape[1]

    def rotate(values, target, at):
        former, latter = values[:, :middle], values[:, middle:]
        target[:, at : at + middle] = low(former * cosine[...] - latter * sine[...])
        target[:, at + middle : at + head] = low(latter * cosine[...] + former * sine[...])

    bring[1].wait()
    bring[2].wait()
    values = dot(normed[...], key_w[...]) + dot(code_attn[:, rank : 2 * rank], kv_out[0])
    lin_kv[:, :keys] = values
    rotate(values * inverse_rms(values) * gain_key[...], own.at[0], 0)
    values = dot(normed[...], value_w[...]) + dot(code_attn[:, 2 * rank :], kv_out[1])
    lin_kv[:, keys:] = values
    own[1] = low(values * inverse_rms(values))
    shift = pltpu.make_async_remote_copy(
        src_ref=own, dst_ref=prior, send_sem=shift_sem.at[0], recv_sem=shift_sem.at[1],
        device_id={"context": c + 1}, device_id_type=MESH,
    )
    shifted_in = pltpu.make_async_remote_copy(
        src_ref=own, dst_ref=prior, send_sem=shift_sem.at[0], recv_sem=shift_sem.at[1],
        device_id={"context": c - 1}, device_id_type=MESH,
    )

    @pl.when(c < 3)
    def _():
        shift.start()

    kv_rot[...] = own[...]
    relay(further, 2, 2)
    bring[0].wait()
    heads = queries // head
    for h in range(heads):
        at = slice(h * head, (h + 1) * head)
        values = dot(normed[...], query_w[:, at]) + dot(code_attn[:, :rank], query_out[:, at])
        lin[:, at] = values
        rotate(values * inverse_rms(values) * gain_query[...], query_rot, h * head)
    relay(further, 3)

    @pl.when(c > 0)
    def _():
        shifted_in.wait_recv()

    prior_out[...] = prior[...]
    scale = 1.0 / math.sqrt(head)
    for h in range(heads):
        if h == 2:
            spread(further)
        at = slice(h * head, (h + 1) * head)
        early = dot_t(query_rot[:, at], prior[0]) * scale + bias[:, :count]
        later = dot_t(query_rot[:, at], own[0]) * scale + bias[:, count:]
        top = jnp.maximum(jnp.max(early, axis=-1, keepdims=True), jnp.max(later, axis=-1, keepdims=True))
        early, later = jnp.exp(early - top), jnp.exp(later - top)
        total = jnp.sum(early, axis=-1, keepdims=True) + jnp.sum(later, axis=-1, keepdims=True)
        log_total[h] = top + jnp.log(total)
        attended[:, at] = low(dot(low(early / total), prior[1]) + dot(low(later / total), own[1]))

    @pl.when(c < 3)
    def _():
        shift.wait_send()

    finish(further)
    flush(pieces)


def front(weights, arrays, shards):
    count, width = arrays[0].shape
    queries, keys = weights[0].shape[1], weights[1].shape[1]
    rank = arrays[2].shape[0]
    bf16, f32 = jnp.bfloat16, jnp.float32
    shape = jax.ShapeDtypeStruct
    anywhere, vmem = pl.BlockSpec(memory_space=pl.ANY), pl.BlockSpec(memory_space=pltpu.VMEM)
    return pl.pallas_call(
        functools.partial(front_kernel, shards),
        out_shape=full_shapes(weights, FRONT_AXES, shards)
        + [
            shape((count, width), bf16),
            shape((count, 3 * rank), bf16),
            shape((count, queries), f32),
            shape((count, 2 * keys), f32),
            shape((count, queries), bf16),
            shape((2, count, keys), bf16),
            shape((2, count, keys), bf16),
            shape((count, queries), bf16),
            shape((queries // keys, count, 1), f32),
        ],
        in_specs=[anywhere] * 8 + [vmem] * len(arrays),
        out_specs=[anywhere] * 8 + [vmem] * 9,
        scratch_shapes=[pltpu.VMEM(w.shape, w.dtype) for w in weights]
        + [pltpu.VMEM((width, n), bf16) for n in (queries, keys, keys)]
        + [pltpu.VMEM((2, count, keys), bf16), pltpu.VMEM((2, count, keys), bf16), pltpu.VMEM((count, 2 * count), f32)]
        + [pltpu.SemaphoreType.DMA((n,)) for n in (8, 8, 3, 2)]
        + mover_semaphores(8, shards),
        compiler_params=pltpu.CompilerParams(
            collective_id=0, has_side_effects=True, vmem_limit_bytes=60 * 2**20
        ),
    )(*weights, *arrays)


FORE_AXES = (0, 0, 1)


def fore_kernel(
    shards, block,
    w_gate, w_up, w_down,
    out_w, right_w, attended, tokens, left, out_in, out_out, ffn_in, gu_out, down_in, down_out,
    gain_in, gain_attn, gain_laurel, gain_pre,
    full_gate, full_up, full_down, gate_out, up_out, ffn_out,
    attn_proj, combined, laurel_mid, code_out, code_ffn, code_down, part,
    stage_a, stage_b, stage_c, gate_w, up_w, down_w, sent, got, ffn, total, codes, hidden,
    gate_keep, up_keep,
    load_sem, store_sem, weight_sem, keep_sem, ffn_sem, swap_send, swap_recv, *semaphores,
):
    sources = (w_gate, w_up, w_down)
    fulls = (full_gate, full_up, full_down)
    side = lax.axis_index("tensor")
    partner = {"tensor": 1 - side}
    greet, begin, relay, spread, finish, flush, own_place = mover(sources, fulls, semaphores, shards)
    rank = out_in.shape[0]
    count, width = ffn.shape
    half = count // 2
    quarter = half // 2
    groups = w_gate.shape[1] // block

    def group(g):
        base = 3 * g
        return [
            (base, 0, 0, 0, sources[0].shape[0], g * block, block),
            (base + 1, 1, 0, 0, sources[1].shape[0], g * block, block),
            (base + 2, 2, 1, g * block, block, 0, sources[2].shape[1]),
        ]

    greet([partner])
    begin(group(0))
    begin(group(1))
    stages = (stage_a, stage_b, stage_c)
    loads = [pltpu.make_async_copy(sources[i], stages[i], load_sem.at[i]) for i in range(3)]
    stores = [pltpu.make_async_copy(stages[i], own_place(i, FORE_AXES[i]), store_sem.at[i]) for i in range(3)]
    for load in loads:
        load.start()
    for load, store in zip(loads, stores):
        load.wait()
        store.start()
    code = low(dot_t(attended[...], out_in[...]))
    code_out[...] = code
    mine = pl.ds(pl.multiple_of(side * half, half), half)
    theirs = pl.ds(pl.multiple_of((1 - side) * half, half), half)
    sent[...] = low(dot(attended[theirs, :], out_w[...]) + dot(code_out[theirs, :], out_out[...]))
    swap_attn = pltpu.make_async_remote_copy(
        src_ref=sent, dst_ref=got, send_sem=swap_send.at[0], recv_sem=swap_recv.at[0],
        device_id=partner, device_id_type=MESH,
    )
    swap_attn.start()
    attn_proj[...] = dot(attended[mine, :], out_w[...]) + dot(code_out[mine, :], out_out[...])

    relay(group(0))
    for store in stores:
        store.wait()
    swap_attn.wait()
    rows = 64

    def combine(i, carry):
        at = pl.ds(pl.multiple_of(i * rows, rows), rows)
        proj = attn_proj[at, :] + wide(got[at, :])
        attn_proj[at, :] = proj
        token = wide(tokens[at, :])
        normed = token * inverse_rms(token) * gain_in[...]
        mid = low(dot_t(low(normed), left[...]))
        laurel_mid[at, :] = mid
        end = dot(mid, right_w[...])
        comb = (
            token + proj * inverse_rms(proj) * gain_attn[...] + normed + end * inverse_rms(end) * gain_laurel[...]
        ) * ROOT_HALF
        combined[at, :] = comb
        ffn[at, :] = low(comb * inverse_rms(comb) * gain_pre[...])
        return carry

    lax.fori_loop(0, half // rows, combine, 0)
    swaps = []
    for k in range(2):
        swaps.append(
            pltpu.make_async_remote_copy(
                src_ref=ffn.at[pl.ds(k * quarter, quarter), :], dst_ref=ffn.at[pl.ds(half + k * quarter, quarter), :],
                send_sem=swap_send.at[1 + k], recv_sem=swap_recv.at[1 + k],
                device_id=partner, device_id_type=MESH,
            )
        )
        swaps[k].start()
    total[...] = jnp.zeros_like(total)
    codes[...] = jnp.zeros_like(codes)

    def keeps(g, slot):
        at = pl.ds(pl.multiple_of(g * block, block), block)
        return (
            pltpu.make_async_copy(gate_keep.at[slot], gate_out.at[:, at], keep_sem.at[0, slot]),
            pltpu.make_async_copy(up_keep.at[slot], up_out.at[:, at], keep_sem.at[1, slot]),
        )

    def weights(g):
        at = pl.ds(pl.multiple_of(g * block, block), block)
        return (
            pltpu.make_async_copy(full_gate.at[:, at], gate_w, weight_sem.at[0]),
            pltpu.make_async_copy(full_up.at[:, at], up_w, weight_sem.at[1]),
            pltpu.make_async_copy(full_down.at[at, :], down_w, weight_sem.at[2]),
        )

    def climb(g):
        at = pl.ds(pl.multiple_of(g * block, block), block)
        slot = lax.rem(g, 2)

        @pl.when(g >= 2)
        def _():
            for keep in keeps(g - 2, slot):
                keep.wait()

        ready = weights(g)
        ready[0].wait()
        gate = dot(ffn[...], gate_w[...]) + dot(code_ffn[:, :rank], gu_out[0, :, at])
        gate_keep[slot] = low(gate)
        act = gelu_parts(gate)[0]
        ready[1].wait()
        up = dot(ffn[...], up_w[...]) + dot(code_ffn[:, rank:], gu_out[1, :, at])
        up_keep[slot] = low(up)
        hidden[...] = low(act * up)
        for keep in keeps(g, slot):
            keep.start()

    def descend(g):
        at = pl.ds(pl.multiple_of(g * block, block), block)
        weights(g)[2].wait()
        codes[...] += dot_t(hidden[...], down_in[:, at])
        total[...] += dot(hidden[...], down_w[...])

    def round_(g, carry):
        more = g + 1 < groups

        @pl.when(more)
        def _():
            relay(group(g + 1), 1, 1)

        @pl.when(g + 2 < groups)
        def _():
            begin(group(g + 2))

        spread(group(g))

        @pl.when(g >= 1)
        def _():
            descend(g - 1)

        @pl.when(more)
        def _():
            relay(group(g + 1), 2, 2)

        finish(group(g))
        for load in weights(g):
            load.start()

        @pl.when(more)
        def _():
            relay(group(g + 1), 3)

        @pl.when(g == 0)
        def _():
            for swap_ffn in swaps:
                swap_ffn.wait()
            pltpu.make_async_copy(ffn, ffn_out, ffn_sem).start()
            code_ffn[...] = low(dot_t(ffn[...], ffn_in[...]))

        climb(g)
        return carry

    lax.fori_loop(0, groups, round_, 0)
    descend(groups - 1)
    code_down[...] = low(codes[...])
    part[...] = low(total[...] + dot(code_down[...], down_out[...]))
    for g in (groups - 2, groups - 1):
        for keep in keeps(g, g % 2):
            keep.wait()
    pltpu.make_async_copy(ffn, ffn_out, ffn_sem).wait()

    def flush_group(g, carry):
        flush(group(g))
        return carry

    lax.fori_loop(0, groups, flush_group, 0)


def fore(
    weights, out_w, right_w, attended, tokens, left, out_in, out_out, ffn_in, gu_out, down_in, down_out, gains, shards
):
    count = attended.shape[0]
    width = tokens.shape[1]
    hidden = weights[0].shape[1]
    half = count // 2
    rank = out_in.shape[0]
    block = min(512, hidden)
    groups = hidden // block
    bf16, f32 = jnp.bfloat16, jnp.float32
    anywhere, vmem = pl.BlockSpec(memory_space=pl.ANY), pl.BlockSpec(memory_space=pltpu.VMEM)
    shape = jax.ShapeDtypeStruct
    return pl.pallas_call(
        functools.partial(fore_kernel, shards, block),
        out_shape=full_shapes(weights, FORE_AXES, shards)
        + [
            shape((count, hidden), bf16),
            shape((count, hidden), bf16),
            shape((count, width), bf16),
            shape((half, width), f32),
            shape((half, width), f32),
            shape((half, left.shape[0]), bf16),
            shape((count, rank), bf16),
            shape((count, 2 * rank), bf16),
            shape((count, rank), bf16),
            shape((count, width), bf16),
        ],
        in_specs=[anywhere] * 3 + [vmem] * 15,
        out_specs=[anywhere] * 6 + [vmem] * 7,
        scratch_shapes=[
            *[pltpu.VMEM(w.shape, bf16) for w in weights],
            pltpu.VMEM((width, block), bf16),
            pltpu.VMEM((width, block), bf16),
            pltpu.VMEM((block, width), bf16),
            pltpu.VMEM((half, width), bf16),
            pltpu.VMEM((half, width), bf16),
            pltpu.VMEM((count, width), bf16),
            pltpu.VMEM((count, width), f32),
            pltpu.VMEM((count, rank), f32),
            pltpu.VMEM((count, block), bf16),
            pltpu.VMEM((2, count, block), bf16),
            pltpu.VMEM((2, count, block), bf16),
            pltpu.SemaphoreType.DMA((3,)),
            pltpu.SemaphoreType.DMA((3,)),
            pltpu.SemaphoreType.DMA((3,)),
            pltpu.SemaphoreType.DMA((2, 2)),
            pltpu.SemaphoreType.DMA,
            pltpu.SemaphoreType.DMA((3,)),
            pltpu.SemaphoreType.DMA((3,)),
        ]
        + mover_semaphores(3 * groups, shards),
        compiler_params=pltpu.CompilerParams(
            collective_id=1, has_side_effects=True, vmem_limit_bytes=60 * 2**20
        ),
    )(*weights, out_w, right_w, attended, tokens, left, out_in, out_out, ffn_in, gu_out, down_in, down_out, *gains)


def body(
    tokens,
    layer_input,
    segments,
    adapter_ids,
    cotangent,
    w_query,
    w_key,
    w_value,
    w_output,
    w_gate,
    w_up,
    w_down,
    laurel_left,
    laurel_right,
    input_gate,
    input_proj,
    gain_in,
    gain_attn,
    gain_laurel,
    gain_pre,
    gain_post,
    gain_layer,
    gain_query,
    gain_key,
    adapt_attn_in,
    adapt_query_out,
    adapt_kv_out,
    adapt_out_in,
    adapt_out_out,
    adapt_ffn_in,
    adapt_gu_out,
    adapt_down_in,
    adapt_down_out,
):
    seq_count, count, width = tokens.shape
    assert seq_count == 1 and lax.axis_size("tensor") == 2 and lax.axis_size("context") == 4
    half = count // 2
    head_size = gain_query.shape[0]
    rank = adapt_query_out.shape[1]
    heads = adapt_query_out.shape[2] // head_size
    kv_heads = adapt_kv_out.shape[3] // head_size
    assert kv_heads == 1
    side = lax.axis_index("tensor")
    place = lax.axis_index("context")
    shards = lax.axis_size("shard")

    hidden_here = w_gate.shape[1]
    chosen = adapter_ids[0]

    def turned(table):
        return table.transpose(0, 2, 1)

    (
        pick_attn_in, pick_query_out, pick_kv_out, pick_out_in, pick_out_out, pick_ffn_in, pick_gu_out,
        pick_down_in, pick_down_out, tokens_own, per_layer_own, cotangent_own,
    ) = pick_rows(
        chosen, side,
        [
            turned(adapt_attn_in), adapt_query_out, adapt_kv_out, turned(adapt_out_in), adapt_out_out,
            turned(adapt_ffn_in), adapt_gu_out, turned(adapt_down_in), adapt_down_out,
        ],
        [tokens[0], layer_input[0], cotangent[0]],
    )

    start_pos = place * count
    seg_all = segments[0]
    seg_query = lax.dynamic_slice_in_dim(seg_all, start_pos, count, 0)
    before = jnp.sum((seg_all[None, :] < seg_query[:, None]).astype(jnp.int32), axis=1)
    own_pos = start_pos + jnp.arange(count, dtype=jnp.int32) - before
    cosine, sine_table = rope_tables(own_pos, head_size)
    seg_prior = lax.dynamic_slice_in_dim(seg_all, jnp.maximum(start_pos - count, 0), count, 0)
    seg_cols = jnp.concatenate([jnp.where(place > 0, seg_prior, -1), seg_query])[None, :]
    seg_rows = seg_query[:, None]
    score_scale = 1.0 / math.sqrt(head_size)
    (
        full_query, full_key, full_value, full_left, full_output, full_right, full_layer_gate, full_layer_proj, normed_b,
        code_attn, lin, lin_kv, query_rot, kv_own, kv_prior, attended_b, log_total,
    ) = front(
        (w_query, w_key, w_value, laurel_left.T, w_output, laurel_right, input_gate, input_proj),
        (
            tokens[0], pick_attn_in, pick_query_out, pick_kv_out, cosine, sine_table, seg_rows, seg_cols,
            gain_in[None], gain_query[None], gain_key[None],
        ),
        shards,
    )
    (
        full_gate, full_up, full_down,
        gate_b, up_b, ffn_b, attn_proj, combined, laurel_mid, code_out, code_ffn, code_down, down_part,
    ) = fore(
        (w_gate, w_up, w_down), full_output, full_right,
        attended_b, tokens_own, full_left,
        pick_out_in, pick_out_out, pick_ffn_in, pick_gu_out, pick_down_in, pick_down_out,
        (gain_in[None], gain_attn[None], gain_laurel[None], gain_pre[None]), shards,
    )
    mark = jnp.where(
        (lax.broadcasted_iota(jnp.int32, (rank, 512), 1) == chosen) & (place == 0), 1.0, 0.0
    )
    grad_attn_b, early, output_own, grad_inputs, grad_normed = aft(
        (full_gate, full_up, full_down), (gate_b, up_b),
        (
            down_part, combined, per_layer_own, cotangent_own, full_layer_gate, full_layer_proj,
            code_ffn, code_down, ffn_b, pick_down_in, pick_down_out, pick_gu_out, pick_ffn_in,
            attn_proj, laurel_mid, full_left, full_right, mark,
            gain_post[None], gain_layer[None], gain_pre[None], gain_attn[None], gain_laurel[None],
        ),
        shards,
    )
    output_other = swap(output_own)
    grad_query, sent_kv, own_kv, term_out_in, term_out_out = attend_back(
        grad_attn_b, full_output, pick_out_in, pick_out_out, code_out, attended_b, query_rot, kv_prior, kv_own,
        log_total, seg_rows, seg_cols, lin, cosine, sine_table, gain_query[None], score_scale,
    )
    input_grad, late = tail(
        (
            grad_query, full_query, full_key, full_value, code_attn, normed_b,
            pick_query_out, pick_kv_out, pick_attn_in, term_out_in, term_out_out,
            tokens_own, gain_in[None], grad_inputs, grad_normed,
            own_kv, shifted(sent_kv, "context", -1), lin_kv, cosine, sine_table, gain_key[None],
        ),
        shards,
    )
    (
        layer_output, table_attn_in, table_query_out, table_kv_out, table_out_in, table_out_out, table_ffn_in,
        table_gu_out, table_down_in, table_down_out,
    ) = tables(
        early, late, output_own, output_other, heads * head_size, kv_heads * head_size, adapt_attn_in.shape[0], hidden_here
    )
    return (
        layer_output[None], input_grad[None], turned(table_attn_in), table_query_out, table_kv_out,
        turned(table_out_in), table_out_out, turned(table_ffn_in), table_gu_out, turned(table_down_in), table_down_out,
    )


def solution(mesh):
    in_specs = (
        P("shard", "context", None),
        P("shard", "context", None),
        P("shard", None),
        P("shard"),
        P("shard", "context", None),
        P("shard", "tensor"),
        P("shard", "tensor"),
        P("shard", "tensor"),
        P("tensor", "shard"),
        P("shard", "tensor"),
        P("shard", "tensor"),
        P("tensor", "shard"),
        P("shard", None),
        P(None, "shard"),
        P("shard", None),
        P(None, "shard"),
        P(),
        P(),
        P(),
        P(),
        P(),
        P(),
        P(),
        P(),
        P(),
        P(None, None, "tensor"),
        P(None, None, None, "tensor"),
        P(None, "tensor", None),
        P(),
        P(),
        P(None, None, None, "tensor"),
        P(None, "tensor", None),
        P(),
    )
    out_specs = (
        P("shard", "context", None),
        P("shard", "context", None),
        P(),
        P(),
        P(),
        P(),
        P(),
        P(),
        P(),
        P(),
        P(),
    )
    return jax.shard_map(body, mesh=mesh, in_specs=in_specs, out_specs=out_specs, check_vma=False)
```

```python
import functools
import math

import jax
import jax.numpy as jnp
from jax import lax
from jax.experimental import pallas as pl
from jax.experimental.pallas import tpu as pltpu
from jax.sharding import PartitionSpec as P

WINDOW = 512
EPSILON = 1e-06
ROOT_HALF = 0.7071067811865476
GELU_SCALE = math.sqrt(2.0 / math.pi)
GELU_CUBE = 0.044715

MESH = pl.DeviceIdType.MESH


def shifted(array, axis, by):
    count = lax.axis_size(axis)
    pairs = [(i, i + by) for i in range(count) if 0 <= i + by < count]
    return lax.ppermute(array, axis, pairs)


def swap(array):
    return lax.ppermute(array, "tensor", [(0, 1), (1, 0)])


def rope_tables(positions, head_size):
    frequency = jnp.exp(
        jnp.arange(head_size // 2, dtype=jnp.float32) * (-2.0 * math.log(10000.0) / head_size)
    )
    angles = positions.astype(jnp.float32)[..., None] * frequency
    return (jnp.cos(angles), jnp.sin(angles))


def low(values):
    return values.astype(jnp.bfloat16)


def wide(values):
    return values.astype(jnp.float32)


def dot(left, right):
    return lax.dot_general(left, right, (((1,), (0,)), ((), ())), preferred_element_type=jnp.float32)


def dot_t(left, right):
    return lax.dot_general(left, right, (((1,), (1,)), ((), ())), preferred_element_type=jnp.float32)


def dot_o(left, right):
    return lax.dot_general(left, right, (((0,), (0,)), ((), ())), preferred_element_type=jnp.float32)


def row_mean(values):
    return jnp.mean(values, axis=-1, keepdims=True)


def inverse_rms(values):
    return lax.rsqrt(row_mean(values * values) + EPSILON)


def rms_back(values, inverse, scaled):
    return inverse * scaled - values * (inverse * inverse * inverse * row_mean(values * scaled))


def gelu_parts(values):
    squared = values * values
    bend = jnp.tanh(GELU_SCALE * values * (1.0 + GELU_CUBE * squared))
    rise = 0.5 * (1.0 + bend)
    slope = rise + 0.5 * values * (1.0 - bend * bend) * (GELU_SCALE * (1.0 + 3.0 * GELU_CUBE * squared))
    return values * rise, slope


def greet_all(shards, places, ends):
    z = lax.axis_index("shard")
    barrier = pltpu.get_barrier_semaphore()

    def signal(place):
        pl.semaphore_signal(barrier, inc=1, device_id=place, device_id_type=MESH)

    for place in places:
        signal(place)
    peers = len(places)
    if ends:

        @pl.when(z > 0)
        def _():
            signal({"shard": z - 1})

        @pl.when(z < shards - 1)
        def _():
            signal({"shard": z + 1})

        peers = peers + lax.div(z + shards - 1, shards) + lax.div(2 * shards - 2 - z, shards)
    pl.semaphore_wait(barrier, peers)


def context_partners():
    c = lax.axis_index("context")
    return lax.rem(c + 2, 4), c + 1 - 2 * lax.rem(c, 2)


def sharer(pack, whole, inbox, turn_in, turn_out, piece, semaphores, shards):
    (
        pre_send, pre_recv, z_send, z_recv, x_send, x_recv, y_send, y_recv, near_send, near_recv,
        far_send, far_recv, keep_sem,
    ) = semaphores
    z, c, side = (lax.axis_index(a) for a in ("shard", "context", "tensor"))
    across, beside = context_partners()
    opposite = lax.rem(beside + 2, 4)
    columns = piece.shape[1]

    def cols(q):
        return pl.ds(pl.multiple_of(q * columns, 128), columns)

    def region(t, s, q):
        return whole.at[t, s, :, cols(q)]

    def copy(source, target, send, recv, place):
        return pltpu.make_async_remote_copy(
            src_ref=source, dst_ref=target, send_sem=send, recv_sem=recv, device_id=place, device_id_type=MESH
        )

    def halves(k):
        q = beside if k == 0 else opposite
        return copy(pack.at[:, cols(q)], inbox.at[k], pre_send.at[k], pre_recv.at[k], {"context": beside})

    def turned():
        return copy(turn_out, turn_in, pre_send.at[2], pre_recv.at[2], {"context": across})

    def z_copy(t, s, source, sender, by):
        return copy(source, region(t, s, c), z_send.at[t, sender], z_recv.at[t, s], {"shard": z + by})

    def passed(t, s, by):
        return z_copy(t, s, region(t, s, c), s, by)

    def x_copy(source, t):
        return copy(source, region(t, z, c), x_send, x_recv, {"tensor": 1 - side})

    def y_copy(t, s, source, q):
        return copy(source, region(t, s, q), y_send.at[t, s], y_recv.at[t, s], {"context": across})

    def near_copy(t, s, source, q):
        return copy(source, region(t, s, q), near_send.at[t, s], near_recv.at[t, s], {"context": beside})

    def far_copy(t, s, q):
        at = region(t, s, q)
        return copy(at, at, far_send.at[t, s], far_recv.at[t, s], {"context": beside})

    def keep():
        return pltpu.make_async_copy(piece, region(side, z, c), keep_sem)

    def start():
        for k in range(2):
            halves(k).start()

    def turn():
        for k in range(2):
            halves(k).wait_recv()
        turn_out[...] = low(pack[:, cols(across)] + inbox[1])
        turned().start()

    def settle():
        turned().wait_recv()
        piece[...] = low(pack[:, cols(c)] + inbox[0] + wide(turn_in[...]))
        keep().start()
        x_copy(piece, side).start()
        set_out(side, piece)

    def set_out(t, source):
        @pl.when(z < shards - 1)
        def _():
            z_copy(t, z, source, z, 1).start()

        @pl.when(z > 0)
        def _():
            z_copy(t, z, source, shards, -1).start()

        y_copy(t, z, source, c).start()
        near_copy(t, z, source, c).start()

    def cross_over():
        at = region(1 - side, z, c)
        x_copy(at, 1 - side).wait_recv()
        set_out(1 - side, at)

    def hop(d):
        def one(t, s, by, last):
            passed(t, s, by).wait_recv()

            @pl.when(z != last)
            def _():
                passed(t, s, by).start()

            at = region(t, s, c)
            y_copy(t, s, at, c).start()
            near_copy(t, s, at, c).start()

        @pl.when(z >= d)
        def _():
            for t in (side, 1 - side):
                one(t, z - d, 1, shards - 1)

        @pl.when(z + d <= shards - 1)
        def _():
            for t in (side, 1 - side):
                one(t, z + d, -1, 0)

    def hops(first):
        lax.fori_loop(first, shards, lambda d, carry: (hop(d), carry)[1], 0)

    def every(act):
        def one(s, carry):
            for t in range(2):
                act(t, s)
            return carry

        lax.fori_loop(0, shards, one, 0)

    def spread():
        def act(t, s):
            y_copy(t, s, region(t, s, across), across).wait_recv()
            far_copy(t, s, across).start()

        every(act)

    def finish():
        def act(t, s):
            near_copy(t, s, region(t, s, beside), beside).wait_recv()
            far_copy(t, s, opposite).wait_recv()
            y_copy(t, s, region(t, s, c), c).wait_send()
            near_copy(t, s, region(t, s, c), c).wait_send()
            far_copy(t, s, across).wait_send()

        every(act)

        def sent(t, s):
            @pl.when((s <= z) & (z < shards - 1))
            def _():
                passed(t, s, 1).wait_send()

            @pl.when((s > z) & (z > 0))
            def _():
                passed(t, s, -1).wait_send()

        every(sent)

        @pl.when(z > 0)
        def _():
            for t in range(2):
                z_copy(t, z, piece, shards, -1).wait_send()

        x_copy(piece, side).wait_send()

        for k in range(2):
            halves(k).wait_send()
        turned().wait_send()
        keep().wait()

    return start, turn, settle, hop, hops, cross_over, spread, finish


def sharer_scratch(rows, columns, shards):
    part = columns // 4
    dma = pltpu.SemaphoreType.DMA
    return [
        pltpu.VMEM((2, rows, part), jnp.float32),
        pltpu.VMEM((rows, part), jnp.bfloat16),
        pltpu.VMEM((rows, part), jnp.bfloat16),
        pltpu.VMEM((rows, part), jnp.bfloat16),
        dma((3,)), dma((3,)), dma((2, shards + 1)), dma((2, shards)), dma, dma,
        dma((2, shards)), dma((2, shards)), dma((2, shards)), dma((2, shards)), dma((2, shards)), dma((2, shards)),
        dma,
    ]


def tail_kernel(
    shards,
    grad_query, w_query, w_key, w_value, code_attn, normed, query_out, kv_out, attn_in,
    out_in_term, out_out_term, tokens, gain_in, grad_comb, grad_normed,
    own_kv, came_kv, lin_kv, cosine, sine, gain_key,
    input_grad_out, whole,
    pack, mine, sent, got, result, grad_key, grad_value, send_sem, recv_sem, keep_sem, *shared,
):
    side = lax.axis_index("tensor")
    partner = {"tensor": 1 - side}
    across, beside = context_partners()
    count, width = normed.shape
    half = count // 2
    quarter = half // 2
    rank = query_out.shape[0]
    start, turn, settle, hop, hops, cross_over, spread, finish = sharer(
        pack, whole, shared[0], shared[1], shared[2], shared[3], shared[4:], shards
    )
    greet_all(shards, [partner, {"context": across}, {"context": beside}], True)
    keys = grad_key.shape[1]
    values = lin_kv[:, :keys]
    turned = unrotate(own_kv[0] + wide(came_kv[0]), cosine[...], sine[...]) * gain_key[...]
    grad_key[...] = low(rms_back(values, inverse_rms(values), turned))
    values = lin_kv[:, keys:]
    grad_value[...] = low(rms_back(values, inverse_rms(values), own_kv[1] + wide(came_kv[1])))
    parts = ((grad_query, w_query, query_out[...]), (grad_key, w_key, kv_out[0]), (grad_value, w_value, kv_out[1]))
    at = 0

    def put(term):
        nonlocal at
        pack[:, at : at + term.shape[1]] = term
        at += term.shape[1]

    put(out_in_term[...])
    put(out_out_term[...])
    backs = []
    for i, (grad, _, table) in enumerate(parts):
        put(dot_o(code_attn[:, i * rank : (i + 1) * rank], grad[...]))
        backs.append(low(dot_t(grad[...], table)))
    for back in backs:
        put(dot_o(back, normed[...]))
    start()

    def product(here):
        total = dot_t(grad_query[here, :], w_query[...])
        total += dot_t(grad_key[here, :], w_key[...]) + dot_t(grad_value[here, :], w_value[...])
        for i, (grad, _, table) in enumerate(parts):
            back = low(dot_t(grad[here, :], table))
            total += dot(back, attn_in[i * rank : (i + 1) * rank, :])
        return total

    def send(source, target, k):
        return pltpu.make_async_remote_copy(
            src_ref=source, dst_ref=target, send_sem=send_sem.at[k], recv_sem=recv_sem.at[k],
            device_id=partner, device_id_type=MESH,
        )

    def rows(k):
        return pl.ds(k * quarter, quarter)

    def rows_of(owner, k):
        return pl.ds(pl.multiple_of(owner * half + k * quarter, quarter), quarter)

    swaps = []
    for k in range(2):
        sent[rows(k), :] = low(product(rows_of(1 - side, k)))
        swaps.append(send(sent.at[rows(k), :], got.at[rows(k), :], k))
        swaps[k].start()
    turn()
    for k in range(2):
        mine[rows(k), :] = product(rows_of(side, k))
        if k == 0:
            settle()
    cross_over()
    ends = []
    for k in range(2):
        swaps[k].wait_recv()
        here = rows(k)
        grad = (grad_normed[here, :] + mine[here, :] + wide(got[here, :])) * gain_in[...]
        token = wide(tokens[here, :])
        there = rows_of(side, k)
        result[there, :] = low(grad_comb[here, :] + rms_back(token, inverse_rms(token), grad))
        ends.append(send(result.at[there, :], result.at[there, :], 2 + k))
        ends[k].start()
        if k == 0:
            hop(1)
    hops(2)
    spread()
    for end in ends:
        end.wait()
    keep = pltpu.make_async_copy(result, input_grad_out, keep_sem)
    keep.start()
    for swap_part in swaps:
        swap_part.wait_send()
    finish()
    keep.wait()


def tail(arrays, shards):
    count, width = arrays[5].shape
    rank = arrays[6].shape[0]
    half = count // 2
    queries, keys = arrays[0].shape[1], arrays[2].shape[1]
    columns = 2 * queries + 2 * keys + 4 * width
    bf16, f32 = jnp.bfloat16, jnp.float32
    anywhere, vmem = pl.BlockSpec(memory_space=pl.ANY), pl.BlockSpec(memory_space=pltpu.VMEM)
    return pl.pallas_call(
        functools.partial(tail_kernel, shards),
        out_shape=[
            jax.ShapeDtypeStruct((count, width), bf16),
            jax.ShapeDtypeStruct((2, shards, rank, columns), bf16),
        ],
        in_specs=[vmem] * len(arrays),
        out_specs=[anywhere] * 2,
        scratch_shapes=[
            pltpu.VMEM((rank, columns), f32),
            pltpu.VMEM((half, width), f32),
            pltpu.VMEM((half, width), bf16),
            pltpu.VMEM((half, width), bf16),
            pltpu.VMEM((count, width), bf16),
            pltpu.VMEM((count, keys), bf16),
            pltpu.VMEM((count, keys), bf16),
            pltpu.SemaphoreType.DMA((4,)),
            pltpu.SemaphoreType.DMA((4,)),
            pltpu.SemaphoreType.DMA,
        ]
        + sharer_scratch(rank, columns, shards),
        compiler_params=pltpu.CompilerParams(
            collective_id=3, has_side_effects=True, vmem_limit_bytes=60 * 2**20
        ),
    )(*arrays)


def allowed_bias(seg_rows, seg_cols, keys):
    count = seg_rows.shape[0]
    shape = (count, keys)
    distance = lax.broadcasted_iota(jnp.int32, shape, 0) + (keys - count) - lax.broadcasted_iota(jnp.int32, shape, 1)
    seen = (seg_rows[...] == seg_cols[...]) & (distance >= 0) & (distance < WINDOW)
    return jnp.where(seen, 0.0, -1e30)


def unrotate(grad, cosine, sine):
    middle = grad.shape[1] // 2
    former, latter = grad[:, :middle], grad[:, middle:]
    return jnp.concatenate([former * cosine + latter * sine, latter * cosine - former * sine], axis=1)


def attend_back_kernel(
    scale, grad, w_out, out_in, out_out, code_out, attended, query, prior, own, log_total, seg_rows, seg_cols, lin,
    cosine, sine, gain_query,
    grad_query, sent_kv, own_kv, term_in, term_out, bias, back, grad_k, grad_v,
):
    count = query.shape[0]
    head = pl.program_id(0)

    @pl.when(head == 0)
    def _():
        bias[...] = allowed_bias(seg_rows, seg_cols, 2 * count)
        back[...] = low(dot_t(grad[...], out_out[...]))
        term_out[...] = dot_o(code_out[...], grad[...])
        grad_k[...] = jnp.zeros_like(grad_k)
        grad_v[...] = jnp.zeros_like(grad_v)

    top = low(dot_t(grad[...], w_out[...]) + dot(back[...], out_in[...]))
    term_in[...] = dot_o(back[...], attended[...])
    probs, slopes, mean = [], [], 0.0
    for i, kv in enumerate((prior, own)):
        score = dot_t(query[...], kv[0]) * scale + bias[:, i * count : (i + 1) * count]
        probs.append(jnp.exp(score - log_total[...]))
        slopes.append(dot_t(top, kv[1]))
        mean += jnp.sum(probs[i] * slopes[i], axis=-1, keepdims=True)
    turned = 0.0
    for i, kv in enumerate((prior, own)):
        grad_score = low(probs[i] * (slopes[i] - mean))
        turned += dot(grad_score, kv[0])
        grad_k[i] += dot_o(grad_score, query[...]) * scale
        grad_v[i] += dot_o(low(probs[i]), top)
    values = lin[...]
    turned = unrotate(turned * scale, cosine[...], sine[...]) * gain_query[...]
    grad_query[...] = low(rms_back(values, inverse_rms(values), turned))

    @pl.when(head == pl.num_programs(0) - 1)
    def _():
        sent_kv[0] = low(grad_k[0])
        sent_kv[1] = low(grad_v[0])
        own_kv[0] = grad_k[1]
        own_kv[1] = grad_v[1]


def attend_back(
    grad, w_out, out_in, out_out, code_out, attended, query, prior, own, log_total, seg_rows, seg_cols, lin,
    cosine, sine, gain_query, scale,
):
    count, inner = query.shape
    width = grad.shape[1]
    head = gain_query.shape[1]
    rank = out_in.shape[0]
    bf16, f32 = jnp.bfloat16, jnp.float32
    whole = lambda *shape: pl.BlockSpec(shape, lambda h: (0,) * len(shape))
    column = lambda rows: pl.BlockSpec((rows, head), lambda h: (0, h))
    return pl.pallas_call(
        functools.partial(attend_back_kernel, scale),
        grid=(inner // head,),
        in_specs=[
            whole(count, width),
            pl.BlockSpec((head, width), lambda h: (h, 0)),
            column(rank),
            whole(rank, width),
            whole(count, rank),
            column(count),
            column(count),
            whole(2, count, head),
            whole(2, count, head),
            pl.BlockSpec((None, count, 1), lambda h: (h, 0, 0)),
            whole(count, 1),
            whole(1, 2 * count),
            column(count),
            whole(count, head // 2),
            whole(count, head // 2),
            whole(1, head),
        ],
        out_specs=[column(count), whole(2, count, head), whole(2, count, head), column(rank), whole(rank, width)],
        out_shape=[
            jax.ShapeDtypeStruct((count, inner), bf16),
            jax.ShapeDtypeStruct((2, count, head), bf16),
            jax.ShapeDtypeStruct((2, count, head), f32),
            jax.ShapeDtypeStruct((rank, inner), f32),
            jax.ShapeDtypeStruct((rank, width), f32),
        ],
        scratch_shapes=[
            pltpu.VMEM((count, 2 * count), f32),
            pltpu.VMEM((count, rank), bf16),
            pltpu.VMEM((2, count, head), f32),
            pltpu.VMEM((2, count, head), f32),
        ],
        compiler_params=pltpu.CompilerParams(vmem_limit_bytes=56 * 2**20),
    )(
        grad, w_out, out_in, out_out, code_out, attended, query, prior, own, log_total, seg_rows, seg_cols, lin,
        cosine, sine, gain_query,
    )


def tables_kernel(
    queries, keys, early, late, output_own, output_other,
    output, out_attn, out_query, out_kv, out_out_in, out_out_out, out_ffn, out_gu, out_down_in, out_down_out,
    marks, drawn, laid, spots, placing, mark_sem, drawn_sem, laid_sem, output_sem,
):
    side = lax.axis_index("tensor")
    shards, rank = early.shape[1], early.shape[2]
    half, width = output_own.shape
    puts = []
    for i, (rows, owner) in enumerate(((output_own, side), (output_other, 1 - side))):
        there = output.at[pl.ds(pl.multiple_of(owner * half, half), half), :]
        puts.append(pltpu.make_async_copy(rows, there, output_sem.at[i]))
        puts[i].start()
    adapters, hidden = out_gu.shape[0], out_gu.shape[3] // 2
    wide_at = early.shape[3] - 512
    get_marks = pltpu.make_async_copy(early.at[0, :, :, pl.ds(wide_at, 128)], marks, mark_sem)
    get_marks.start()
    span = drawn.shape[4]
    def both(source, at, columns, table, inner):
        found = []
        for first in range(0, columns, span):
            size = min(span, columns - first)
            found.append(
                (source, at + first, size, [table(t * inner + first, size) for t in range(2)])
            )
        return found

    def gu_table(i):
        return lambda at, size: out_gu.at[:, i, :, pl.ds(at, size)]

    def kv_table(i):
        return lambda at, size: out_kv.at[:, i, :, pl.ds(at, size)]

    def plain(out, row=0):
        return lambda at, size: out.at[:, pl.ds(row, rank), pl.ds(at, size)]

    def single(source, at, out, row=0):
        return [
            (source, at + first, span, [plain(out, row)(first, span)]) for first in range(0, width, span)
        ]

    early_units = both(early, 0, hidden, gu_table(0), hidden) + both(early, hidden, hidden, gu_table(1), hidden)
    early_units += both(early, 2 * hidden, hidden, plain(out_down_in), hidden)
    early_units += single(early, 3 * hidden, out_ffn) + single(early, 3 * hidden + width, out_ffn, rank)
    early_units += single(early, 3 * hidden + 2 * width, out_down_out)
    late_units = both(late, 0, queries, plain(out_out_in), queries) + single(late, queries, out_out_out)
    late_units += both(late, queries + width, queries, plain(out_query), queries)
    late_units += both(late, 2 * queries + width, keys, kv_table(0), keys)
    late_units += both(late, 2 * queries + width + keys, keys, kv_table(1), keys)
    for i in range(3):
        late_units += single(late, 2 * queries + (1 + i) * width + 2 * keys, out_attn, i * rank)
    units = early_units + late_units

    def draw(u):
        source, at, size, _ = units[u]
        return pltpu.make_async_copy(
            source.at[:, :, :, pl.ds(at, size)], drawn.at[u % 2, :, :, :, pl.ds(0, size)], drawn_sem.at[u % 2]
        )

    def lays(u):
        _, _, size, targets = units[u]
        return [
            pltpu.make_async_copy(laid.at[u % 2, t, :, :, pl.ds(0, size)], target, laid_sem.at[u % 2, t])
            for t, target in enumerate(targets)
        ]

    def lay_out(u, last):
        if u + 1 < last:
            draw(u + 1).start()
        draw(u).wait()
        if u >= 2:
            for lay in lays(u - 2):
                lay.wait()
        _, _, size, targets = units[u]
        slot = u % 2
        for t in range(len(targets)):
            terms = drawn[slot, t, :, :, :size].reshape(shards * rank, size)
            total = dot(placing[...], terms)
            if len(targets) == 1:
                total += dot(placing[...], drawn[slot, 1, :, :, :size].reshape(shards * rank, size))
            laid[slot, t, :, :, :size] = total.reshape(adapters, rank, size)
        for lay in lays(u):
            lay.start()

    draw(0).start()
    get_marks.wait()
    same = lax.broadcasted_iota(jnp.int32, (rank, rank), 0) == lax.broadcasted_iota(jnp.int32, (rank, rank), 1)
    same = same.astype(jnp.float32)
    for q in range(shards):
        mark = wide(marks[q])
        for k in range(adapters):
            spots[k * rank : (k + 1) * rank, q * rank : (q + 1) * rank] = same * mark[:, k : k + 1]
    placing[...] = low(spots[...])
    for u in range(len(units)):
        lay_out(u, len(units))
    for u in (len(units) - 2, len(units) - 1):
        for lay in lays(u):
            lay.wait()
    for put in puts:
        put.wait()


def tables(early, late, output_own, output_other, queries, keys, adapters, hidden):
    half, width = output_own.shape
    shards, rank = early.shape[1], early.shape[2]
    span = 2048
    bf16, f32 = jnp.bfloat16, jnp.float32
    anywhere, vmem = pl.BlockSpec(memory_space=pl.ANY), pl.BlockSpec(memory_space=pltpu.VMEM)
    return pl.pallas_call(
        functools.partial(tables_kernel, queries, keys),
        out_shape=[jax.ShapeDtypeStruct((2 * half, width), bf16)]
        + [
            jax.ShapeDtypeStruct((adapters,) + rest, f32)
            for rest in (
                (3 * rank, width), (rank, 2 * queries), (2, rank, 2 * keys), (rank, 2 * queries), (rank, width),
                (2 * rank, width), (2, rank, 2 * hidden), (rank, 2 * hidden), (rank, width),
            )
        ],
        in_specs=[anywhere] * 2 + [vmem] * 2,
        out_specs=[anywhere] * 10,
        scratch_shapes=[
            pltpu.VMEM((shards, rank, 128), bf16),
            pltpu.VMEM((2, 2, shards, rank, span), bf16),
            pltpu.VMEM((2, 2, adapters, rank, span), f32),
            pltpu.VMEM((adapters * rank, shards * rank), f32),
            pltpu.VMEM((adapters * rank, shards * rank), bf16),
            pltpu.SemaphoreType.DMA,
            pltpu.SemaphoreType.DMA((2,)),
            pltpu.SemaphoreType.DMA((2, 2)),
            pltpu.SemaphoreType.DMA((2,)),
        ],
        compiler_params=pltpu.CompilerParams(vmem_limit_bytes=60 * 2**20),
    )(early, late, output_own, output_other)


def aft_kernel(
    shards, block, strip,
    full_gate, full_up, full_down, gate_in, up_in,
    part, combined, per_layer, cotangent, lgate, lproj, code_ffn, code_down, ffn, down_in, down_out, gu_out, ffn_in,
    attn_proj, laurel_mid, left, right, mark, gain_post, gain_layer, gain_pre, gain_attn, gain_laurel,
    grad_attn_out, whole, output, grad_comb, grad_normed, pack,
    got, grad, grad_gate, grad_up, down_w, gate_v, up_v, gate_w, up_w, mine, sent, came, attn, back_codes, ffn_codes,
    fetch_sem, strip_sem, keep_sem, send_sem, recv_sem, *shared,
):
    side = lax.axis_index("tensor")
    partner = {"tensor": 1 - side}
    across, beside = context_partners()
    greet_all(shards, [partner, {"context": across}, {"context": beside}], True)
    start, turn, settle, hop, hops, cross_over, spread, finish = sharer(
        pack, whole, shared[0], shared[1], shared[2], shared[3], shared[4:], shards
    )
    count, width = grad.shape
    half = count // 2
    quarter = half // 2
    rank = down_in.shape[0]
    hidden = grad_gate.shape[1]
    steps = hidden // block
    strips = width // strip

    def send(source, target, k):
        return pltpu.make_async_remote_copy(
            src_ref=source, dst_ref=target, send_sem=send_sem.at[k], recv_sem=recv_sem.at[k],
            device_id=partner, device_id_type=MESH,
        )

    def rows(k):
        return pl.ds(k * quarter, quarter)

    down_swaps = [send(part.at[rows(2 + k), :], got.at[rows(k), :], k) for k in range(2)]
    grad_swaps = [send(grad.at[rows(k), :], grad.at[rows(2 + k), :], 2 + k) for k in range(2)]
    for swap_down in down_swaps:
        swap_down.start()

    def fetches(t):
        slot, j = lax.rem(t, 2), lax.rem(t, steps)
        at = pl.ds(pl.multiple_of(j * block, block), block)
        here = pl.ds(pl.multiple_of(lax.div(t, steps) * half, half), half)
        return (
            pltpu.make_async_copy(full_down.at[at, :], down_w.at[slot], fetch_sem.at[0, slot]),
            pltpu.make_async_copy(gate_in.at[here, at], gate_v.at[slot], fetch_sem.at[1, slot]),
            pltpu.make_async_copy(up_in.at[here, at], up_v.at[slot], fetch_sem.at[2, slot]),
        )

    def strip_fetches(k):
        slot = lax.rem(k, 2)
        at = pl.ds(pl.multiple_of(k * strip, strip), strip)
        return (
            pltpu.make_async_copy(full_gate.at[at, :], gate_w.at[slot], strip_sem.at[0, slot]),
            pltpu.make_async_copy(full_up.at[at, :], up_w.at[slot], strip_sem.at[1, slot]),
        )

    for fetch in fetches(0) + strip_fetches(0):
        fetch.start()
    pack[...] = jnp.zeros_like(pack)
    ffn_codes[...] = jnp.zeros_like(ffn_codes)

    for k in range(2):
        down_swaps[k].wait_recv()
        at = rows(k)
        down = wide(part[at, :]) + wide(got[at, :])
        down_inverse = inverse_rms(down)
        after = combined[at, :] + down * down_inverse * gain_post[...]
        mixing = wide(per_layer[at, :])
        act, slope = gelu_parts(dot(low(after), lgate[...]))
        proj = dot(low(act * mixing), lproj[...])
        proj_inverse = inverse_rms(proj)
        output[at, :] = low(after + proj * proj_inverse * gain_layer[...])
        top = wide(cotangent[at, :])
        grad_proj = rms_back(proj, proj_inverse, top * gain_layer[...])
        grad_mix = dot_t(low(grad_proj), lproj[...]) * mixing * slope
        top = top + dot_t(low(grad_mix), lgate[...])
        grad_comb[at, :] = top
        grad[at, :] = low(rms_back(down, down_inverse, top * gain_post[...]))
        grad_swaps[k].start()
        back_codes[at, :] = low(dot_t(grad[at, :], down_out[...]))

    def level(t, carry):
        @pl.when(t + 1 < 2 * steps)
        def _():
            for fetch in fetches(t + 1):
                fetch.start()

        @pl.when(t == steps)
        def _():
            for k in range(2):
                grad_swaps[k].wait_recv()
            back_codes[half:, :] = low(dot_t(grad[half:, :], down_out[...]))

        slot, j = lax.rem(t, 2), lax.rem(t, steps)
        at = pl.ds(pl.multiple_of(j * block, block), block)
        here = pl.ds(pl.multiple_of(lax.div(t, steps) * half, half), half)
        for fetch in fetches(t):
            fetch.wait()
        back = back_codes[here, :]
        hidden_grad = dot_t(grad[here, :], down_w[slot]) + dot(back, down_in[:, at])
        up_now = wide(up_v[slot])
        act, slope = gelu_parts(wide(gate_v[slot]))
        grad_g = low(hidden_grad * up_now * slope)
        grad_u = low(hidden_grad * act)
        grad_gate[here, at] = grad_g
        grad_up[here, at] = grad_u
        ffn_codes[0, here, :] += dot_t(grad_g, gu_out[0, :, at])
        ffn_codes[1, here, :] += dot_t(grad_u, gu_out[1, :, at])
        codes = code_ffn[here, :]

        def put(i, term):
            pack[:, pl.ds(pl.multiple_of(i * hidden + j * block, block), block)] += term

        put(0, dot_o(codes[:, :rank], grad_g))
        put(1, dot_o(codes[:, rank:], grad_u))
        put(2, dot_o(back, low(act * up_now)))
        return carry

    lax.fori_loop(0, 2 * steps, level, 0)
    base = 3 * hidden
    pack[:, base : base + width] = dot_o(low(ffn_codes[0]), ffn[...])
    pack[:, base + width : base + 2 * width] = dot_o(low(ffn_codes[1]), ffn[...])
    pack[:, base + 2 * width : base + 3 * width] = dot_o(code_down[...], grad[...])
    pack[:, base + 3 * width :] = mark[...]
    start()

    def strip_send(k):
        return send(sent.at[k], came.at[k], 4 + k)

    def cross(k, carry):
        @pl.when(k + 1 < strips)
        def _():
            for fetch in strip_fetches(k + 1):
                fetch.start()

        slot = lax.rem(k, 2)
        at = pl.ds(pl.multiple_of(k * strip, strip), strip)
        for fetch in strip_fetches(k):
            fetch.wait()
        result = (
            dot_t(grad_gate[...], gate_w[slot])
            + dot_t(grad_up[...], up_w[slot])
            + dot(low(ffn_codes[0]), ffn_in[:rank, at])
            + dot(low(ffn_codes[1]), ffn_in[rank:, at])
        )
        sent[k] = low(result[half:])
        strip_send(k).start()
        mine[:, at] = result[:half]
        for when, act in (
            (1, turn), (2, settle), (4, cross_over), (7, lambda: hop(1)),
        ):
            pl.when(k == when)(act)
        return carry

    lax.fori_loop(0, strips, cross, 0)
    def add(k, carry):
        at = pl.ds(pl.multiple_of(k * strip, strip), strip)
        strip_send(k).wait_recv()
        mine[:, at] += wide(came[k])
        return carry

    lax.fori_loop(0, strips, add, 0)
    attn_swaps = []
    for k in range(2):
        at = rows(k)
        comb = combined[at, :]
        top = (grad_comb[at, :] + rms_back(comb, inverse_rms(comb), mine[at, :] * gain_pre[...])) * ROOT_HALF
        grad_comb[at, :] = top
        proj = attn_proj[at, :]
        there = pl.ds(pl.multiple_of(side * half + k * quarter, quarter), quarter)
        attn[there, :] = low(rms_back(proj, inverse_rms(proj), top * gain_attn[...]))
        attn_swaps.append(send(attn.at[there, :], attn.at[there, :], 4 + strips + k))
        attn_swaps[k].start()
        if k == 0:
            hop(2)
        else:
            hops(3)
        end = dot(laurel_mid[at, :], right[...])
        grad_end = low(rms_back(end, inverse_rms(end), top * gain_laurel[...]))
        grad_normed[at, :] = top + dot(low(dot_t(grad_end, right[...])), left[...])
    spread()
    for swap_attn in attn_swaps:
        swap_attn.wait()
    keep = pltpu.make_async_copy(attn, grad_attn_out, keep_sem)
    keep.start()
    for k in range(2):
        down_swaps[k].wait_send()
        grad_swaps[k].wait_send()

    def flush(k, carry):
        strip_send(k).wait_send()
        return carry

    lax.fori_loop(0, strips, flush, 0)
    finish()
    keep.wait()


def aft(weights, kept, arrays, shards):
    full_gate = weights[0]
    part, combined, per_layer = arrays[:3]
    count, width = part.shape
    hidden = full_gate.shape[1]
    half = count // 2
    rank = arrays[9].shape[0]
    block, strip = min(512, hidden), 256
    strips = width // strip
    columns = 3 * hidden + 3 * width + arrays[17].shape[1]
    bf16, f32 = jnp.bfloat16, jnp.float32
    shape = jax.ShapeDtypeStruct
    anywhere, vmem = pl.BlockSpec(memory_space=pl.ANY), pl.BlockSpec(memory_space=pltpu.VMEM)
    return pl.pallas_call(
        functools.partial(aft_kernel, shards, block, strip),
        out_shape=[
            shape((count, width), bf16),
            shape((2, shards, rank, columns), bf16),
            shape((half, width), bf16),
            shape((half, width), f32),
            shape((half, width), f32),
        ],
        in_specs=[anywhere] * 5 + [vmem] * len(arrays),
        out_specs=[anywhere] * 2 + [vmem] * 3,
        scratch_shapes=[
            pltpu.VMEM((rank, columns), f32),
            pltpu.VMEM((half, width), bf16),
            pltpu.VMEM((count, width), bf16),
            pltpu.VMEM((count, hidden), bf16),
            pltpu.VMEM((count, hidden), bf16),
            pltpu.VMEM((2, block, width), bf16),
            pltpu.VMEM((2, half, block), bf16),
            pltpu.VMEM((2, half, block), bf16),
            pltpu.VMEM((2, strip, hidden), bf16),
            pltpu.VMEM((2, strip, hidden), bf16),
            pltpu.VMEM((half, width), f32),
            pltpu.VMEM((strips, half, strip), bf16),
            pltpu.VMEM((strips, half, strip), bf16),
            pltpu.VMEM((count, width), bf16),
            pltpu.VMEM((count, rank), bf16),
            pltpu.VMEM((2, count, rank), f32),
            pltpu.SemaphoreType.DMA((3, 2)),
            pltpu.SemaphoreType.DMA((2, 2)),
            pltpu.SemaphoreType.DMA,
            pltpu.SemaphoreType.DMA((6 + strips,)),
            pltpu.SemaphoreType.DMA((6 + strips,)),
        ]
        + sharer_scratch(rank, columns, shards),
        compiler_params=pltpu.CompilerParams(
            collective_id=2, has_side_effects=True, vmem_limit_bytes=60 * 2**20
        ),
        cost_estimate=pl.CostEstimate(
            flops=6 * count * width * hidden, bytes_accessed=8 * width * hidden, transcendentals=count * hidden
        ),
    )(*weights, *kept, *arrays)


def mover(sources, fulls, semaphores, shards):
    z_recv, y_recv, near_recv, far_recv, z_send, y_send, near_send, far_send = semaphores
    z, c = lax.axis_index("shard"), lax.axis_index("context")
    across = lax.rem(c + 2, 4)
    beside = c + 1 - 2 * lax.rem(c, 2)

    def greet(also=(), row=False):
        barrier = pltpu.get_barrier_semaphore()

        def signal(place):
            pl.semaphore_signal(barrier, inc=1, device_id=place, device_id_type=MESH)

        signal({"context": across})
        signal({"context": beside})
        for place in also:
            signal(place)

        @pl.when(z > 0)
        def _():
            signal({"shard": z - 1})

        @pl.when(z < shards - 1)
        def _():
            signal({"shard": z + 1})

        peers = 2 + len(also) + lax.div(z + shards - 1, shards) + lax.div(2 * shards - 2 - z, shards)
        if row:

            @pl.when(c > 0)
            def _():
                signal({"context": c - 1})

            @pl.when(c < 3)
            def _():
                signal({"context": c + 1})

            peers = peers + lax.div(c + 3, 4) + lax.div(6 - c, 4)
        pl.semaphore_wait(barrier, peers)

    def region(piece, s, q):
        _, item, axis, row, rows, col, cols = piece
        rows_here, cols_here = sources[item].shape
        part = rows // 4
        if axis == 0:
            return fulls[item].at[
                pl.ds(pl.multiple_of(s * rows_here + row + q * part, 16), part),
                pl.ds(pl.multiple_of(col, 128), cols),
            ]
        return fulls[item].at[
            pl.ds(pl.multiple_of(row + q * part, 16), part),
            pl.ds(pl.multiple_of(s * cols_here + col, 128), cols),
        ]

    def own(piece):
        _, item, axis, row, rows, col, cols = piece
        part = rows // 4
        return sources[item].at[
            pl.ds(pl.multiple_of(row + c * part, 16), part), pl.ds(pl.multiple_of(col, 128), cols)
        ]

    def copy(source, target, send, recv, place):
        return pltpu.make_async_remote_copy(
            src_ref=source, dst_ref=target, send_sem=send, recv_sem=recv, device_id=place, device_id_type=MESH
        )

    def along(piece, s, source, sender, by):
        slot = piece[0]
        return copy(source, region(piece, s, c), z_send.at[slot, sender], z_recv.at[slot, s], {"shard": z + by})

    def passed(piece, s, by):
        return along(piece, s, region(piece, s, c), s, by)

    def y_copy(piece, s, q):
        at = region(piece, s, q)
        return copy(at, at, y_send.at[piece[0], s], y_recv.at[piece[0], s], {"context": across})

    def near_copy(piece, s, q):
        at = region(piece, s, q)
        return copy(at, at, near_send.at[piece[0], s], near_recv.at[piece[0], s], {"context": beside})

    def far_copy(piece, s, q):
        at = region(piece, s, q)
        return copy(at, at, far_send.at[piece[0], s], far_recv.at[piece[0], s], {"context": beside})

    def begin(pieces):
        @pl.when(z < shards - 1)
        def _():
            for piece in pieces:
                along(piece, z, own(piece), z, 1).start()

        @pl.when(z > 0)
        def _():
            for piece in pieces:
                along(piece, z, own(piece), shards, -1).start()

    def relay(pieces, first=1, last=None):
        def hop(d, carry):
            @pl.when(z >= d)
            def _():
                s = z - d
                for piece in pieces:
                    passed(piece, s, 1).wait_recv()

                    @pl.when(z < shards - 1)
                    def _(piece=piece):
                        passed(piece, s, 1).start()

                    y_copy(piece, s, c).start()
                    near_copy(piece, s, c).start()

            @pl.when(z + d <= shards - 1)
            def _():
                s = z + d
                for piece in pieces:
                    passed(piece, s, -1).wait_recv()

                    @pl.when(z > 0)
                    def _(piece=piece):
                        passed(piece, s, -1).start()

                    y_copy(piece, s, c).start()
                    near_copy(piece, s, c).start()

            return carry

        last = shards - 1 if last is None else last
        if first == last:
            hop(first, 0)
        else:
            lax.fori_loop(first, last + 1, hop, 0)

    def others(pieces, act):
        def one(d, carry):
            for piece in pieces:
                act(piece, lax.rem(z + d, shards))
            return carry

        lax.fori_loop(1, shards, one, 0)

    def spread(pieces):
        def act(piece, s):
            y_copy(piece, s, across).wait_recv()
            far_copy(piece, s, across).start()

        others(pieces, act)

    def finish(pieces):
        def act(piece, s):
            near_copy(piece, s, beside).wait_recv()
            far_copy(piece, s, lax.rem(beside + 2, 4)).wait_recv()

        others(pieces, act)

    def flush(pieces):
        @pl.when(z < shards - 1)
        def _():
            for piece in pieces:
                along(piece, z, own(piece), z, 1).wait_send()

        @pl.when(z > 0)
        def _():
            for piece in pieces:
                along(piece, z, own(piece), shards, -1).wait_send()

        def act(piece, s):
            y_copy(piece, s, c).wait_send()
            near_copy(piece, s, c).wait_send()
            far_copy(piece, s, across).wait_send()

            @pl.when((s < z) & (z < shards - 1))
            def _():
                passed(piece, s, 1).wait_send()

            @pl.when((s > z) & (z > 0))
            def _():
                passed(piece, s, -1).wait_send()

        others(pieces, act)

    def own_place(item, axis):
        rows_here, cols_here = sources[item].shape
        if axis == 0:
            return fulls[item].at[pl.ds(pl.multiple_of(z * rows_here, 16), rows_here), :]
        return fulls[item].at[:, pl.ds(pl.multiple_of(z * cols_here, 128), cols_here)]

    return greet, begin, relay, spread, finish, flush, own_place


def mover_semaphores(slots, shards):
    table = pltpu.SemaphoreType.DMA((slots, shards))
    return [table, table, table, table, pltpu.SemaphoreType.DMA((slots, shards + 1)), table, table, table]


def full_shapes(weights, axes, shards):
    shapes = []
    for w, axis in zip(weights, axes):
        shape = list(w.shape)
        shape[axis] *= shards
        shapes.append(jax.ShapeDtypeStruct(tuple(shape), w.dtype))
    return shapes


def pick_kernel(chosen, *refs):
    count = len(refs) // 2
    for source, target in zip(refs[:count], refs[count:]):
        if len(source.shape) > len(target.shape):
            target[...] = source[0]
        else:
            target[...] = source[...]


def pick_rows(chosen, side, tables, arrays):
    in_specs, out_specs, shapes = [], [], []
    for t in tables:
        rest = t.shape[1:]
        in_specs.append(pl.BlockSpec((1,) + rest, lambda i, at, n=len(rest): (at[0],) + (0,) * n))
        out_specs.append(pl.BlockSpec(rest, lambda i, at, n=len(rest): (0,) * n))
        shapes.append(jax.ShapeDtypeStruct(rest, t.dtype))
    for a in arrays:
        part = (a.shape[0] // 2, a.shape[1])
        in_specs.append(pl.BlockSpec(part, lambda i, at: (at[1], 0)))
        out_specs.append(pl.BlockSpec(part, lambda i, at: (0, 0)))
        shapes.append(jax.ShapeDtypeStruct(part, a.dtype))
    return pl.pallas_call(
        pick_kernel,
        grid_spec=pltpu.PrefetchScalarGridSpec(
            num_scalar_prefetch=1, grid=(1,), in_specs=in_specs, out_specs=out_specs
        ),
        out_shape=shapes,
        compiler_params=pltpu.CompilerParams(vmem_limit_bytes=61 * 2**20),
    )(jnp.stack([chosen, side]), *tables, *arrays)


FRONT_AXES = (0, 0, 0, 1, 1, 1, 0, 1)


def front_kernel(
    shards, *refs
):
    sources, rest = refs[:8], refs[8:]
    (tokens, attn_in, query_out, kv_out, cosine, sine, seg_rows, seg_cols, gain_in, gain_query, gain_key), rest = (
        rest[:11], rest[11:]
    )
    fulls, rest = rest[:8], rest[8:]
    (normed, code_attn, lin, lin_kv, query_rot, kv_rot, prior_out, attended, log_total), rest = rest[:9], rest[9:]
    held, rest = rest[:8], rest[8:]
    query_w, key_w, value_w, own, prior, bias, load_sem, store_sem, weight_sem, shift_sem, *semaphores = rest
    c = lax.axis_index("context")
    greet, begin, relay, spread, finish, flush, own_place = mover(sources, fulls, semaphores, shards)
    pieces = [(i, i, FRONT_AXES[i], 0, sources[i].shape[0], 0, sources[i].shape[1]) for i in range(8)]
    needed, further = pieces[:4], pieces[4:]
    greet(row=True)
    begin(needed)
    loads = [pltpu.make_async_copy(sources[i], held[i], load_sem.at[i]) for i in range(8)]
    stores = [pltpu.make_async_copy(held[i], own_place(i, FRONT_AXES[i]), store_sem.at[i]) for i in range(8)]
    for load in loads:
        load.start()
    for load, store in zip(loads, stores):
        load.wait()
        store.start()
    count = tokens.shape[0]
    rows = 64

    def norm(i, carry):
        at = pl.ds(pl.multiple_of(i * rows, rows), rows)
        token = wide(tokens[at, :])
        normed[at, :] = low(token * inverse_rms(token) * gain_in[...])
        return carry

    relay(needed, 1, 1)
    begin(further)
    lax.fori_loop(0, count // rows, norm, 0)
    code_attn[...] = low(dot_t(normed[...], attn_in[...]))
    relay(needed, 2)
    bias[...] = allowed_bias(seg_rows, seg_cols, 2 * count)

    @pl.when(c == 0)
    def _():
        prior[...] = jnp.zeros_like(prior)

    relay(further, 1, 1)
    spread(needed)
    finish(needed)
    for store in stores:
        store.wait()
    bring = [
        pltpu.make_async_copy(full, w, weight_sem.at[i])
        for i, (full, w) in enumerate(zip(fulls[:3], (query_w, key_w, value_w)))
    ]
    for copy in bring:
        copy.start()
    head = gain_query.shape[1]
    middle = head // 2
    rank = query_out.shape[0]
    queries, keys = query_w.shape[1], key_w.shape[1]

    def rotate(values, target, at):
        former, latter = values[:, :middle], values[:, middle:]
        target[:, at : at + middle] = low(former * cosine[...] - latter * sine[...])
        target[:, at + middle : at + head] = low(latter * cosine[...] + former * sine[...])

    bring[1].wait()
    bring[2].wait()
    values = dot(normed[...], key_w[...]) + dot(code_attn[:, rank : 2 * rank], kv_out[0])
    lin_kv[:, :keys] = values
    rotate(values * inverse_rms(values) * gain_key[...], own.at[0], 0)
    values = dot(normed[...], value_w[...]) + dot(code_attn[:, 2 * rank :], kv_out[1])
    lin_kv[:, keys:] = values
    own[1] = low(values * inverse_rms(values))
    shift = pltpu.make_async_remote_copy(
        src_ref=own, dst_ref=prior, send_sem=shift_sem.at[0], recv_sem=shift_sem.at[1],
        device_id={"context": c + 1}, device_id_type=MESH,
    )
    shifted_in = pltpu.make_async_remote_copy(
        src_ref=own, dst_ref=prior, send_sem=shift_sem.at[0], recv_sem=shift_sem.at[1],
        device_id={"context": c - 1}, device_id_type=MESH,
    )

    @pl.when(c < 3)
    def _():
        shift.start()

    kv_rot[...] = own[...]
    relay(further, 2, 2)
    bring[0].wait()
    heads = queries // head
    for h in range(heads):
        at = slice(h * head, (h + 1) * head)
        values = dot(normed[...], query_w[:, at]) + dot(code_attn[:, :rank], query_out[:, at])
        lin[:, at] = values
        rotate(values * inverse_rms(values) * gain_query[...], query_rot, h * head)
    relay(further, 3)

    @pl.when(c > 0)
    def _():
        shifted_in.wait_recv()

    prior_out[...] = prior[...]
    scale = 1.0 / math.sqrt(head)
    for h in range(heads):
        if h == 2:
            spread(further)
        at = slice(h * head, (h + 1) * head)
        early = dot_t(query_rot[:, at], prior[0]) * scale + bias[:, :count]
        later = dot_t(query_rot[:, at], own[0]) * scale + bias[:, count:]
        top = jnp.maximum(jnp.max(early, axis=-1, keepdims=True), jnp.max(later, axis=-1, keepdims=True))
        early, later = jnp.exp(early - top), jnp.exp(later - top)
        total = jnp.sum(early, axis=-1, keepdims=True) + jnp.sum(later, axis=-1, keepdims=True)
        log_total[h] = top + jnp.log(total)
        attended[:, at] = low(dot(low(early / total), prior[1]) + dot(low(later / total), own[1]))

    @pl.when(c < 3)
    def _():
        shift.wait_send()

    finish(further)
    flush(pieces)


def front(weights, arrays, shards):
    count, width = arrays[0].shape
    queries, keys = weights[0].shape[1], weights[1].shape[1]
    rank = arrays[2].shape[0]
    bf16, f32 = jnp.bfloat16, jnp.float32
    shape = jax.ShapeDtypeStruct
    anywhere, vmem = pl.BlockSpec(memory_space=pl.ANY), pl.BlockSpec(memory_space=pltpu.VMEM)
    return pl.pallas_call(
        functools.partial(front_kernel, shards),
        out_shape=full_shapes(weights, FRONT_AXES, shards)
        + [
            shape((count, width), bf16),
            shape((count, 3 * rank), bf16),
            shape((count, queries), f32),
            shape((count, 2 * keys), f32),
            shape((count, queries), bf16),
            shape((2, count, keys), bf16),
            shape((2, count, keys), bf16),
            shape((count, queries), bf16),
            shape((queries // keys, count, 1), f32),
        ],
        in_specs=[anywhere] * 8 + [vmem] * len(arrays),
        out_specs=[anywhere] * 8 + [vmem] * 9,
        scratch_shapes=[pltpu.VMEM(w.shape, w.dtype) for w in weights]
        + [pltpu.VMEM((width, n), bf16) for n in (queries, keys, keys)]
        + [pltpu.VMEM((2, count, keys), bf16), pltpu.VMEM((2, count, keys), bf16), pltpu.VMEM((count, 2 * count), f32)]
        + [pltpu.SemaphoreType.DMA((n,)) for n in (8, 8, 3, 2)]
        + mover_semaphores(8, shards),
        compiler_params=pltpu.CompilerParams(
            collective_id=0, has_side_effects=True, vmem_limit_bytes=60 * 2**20
        ),
    )(*weights, *arrays)


FORE_AXES = (0, 0, 1)


def fore_kernel(
    shards, block,
    w_gate, w_up, w_down,
    out_w, right_w, attended, tokens, left, out_in, out_out, ffn_in, gu_out, down_in, down_out,
    gain_in, gain_attn, gain_laurel, gain_pre,
    full_gate, full_up, full_down, gate_out, up_out, ffn_out,
    attn_proj, combined, laurel_mid, code_out, code_ffn, code_down, part,
    stage_a, stage_b, stage_c, gate_w, up_w, down_w, sent, got, ffn, total, codes, hidden,
    gate_keep, up_keep,
    load_sem, store_sem, weight_sem, keep_sem, ffn_sem, swap_send, swap_recv, *semaphores,
):
    sources = (w_gate, w_up, w_down)
    fulls = (full_gate, full_up, full_down)
    side = lax.axis_index("tensor")
    partner = {"tensor": 1 - side}
    greet, begin, relay, spread, finish, flush, own_place = mover(sources, fulls, semaphores, shards)
    rank = out_in.shape[0]
    count, width = ffn.shape
    half = count // 2
    quarter = half // 2
    groups = w_gate.shape[1] // block

    def group(g):
        base = 3 * g
        return [
            (base, 0, 0, 0, sources[0].shape[0], g * block, block),
            (base + 1, 1, 0, 0, sources[1].shape[0], g * block, block),
            (base + 2, 2, 1, g * block, block, 0, sources[2].shape[1]),
        ]

    greet([partner])
    begin(group(0))
    begin(group(1))
    stages = (stage_a, stage_b, stage_c)
    loads = [pltpu.make_async_copy(sources[i], stages[i], load_sem.at[i]) for i in range(3)]
    stores = [pltpu.make_async_copy(stages[i], own_place(i, FORE_AXES[i]), store_sem.at[i]) for i in range(3)]
    for load in loads:
        load.start()
    for load, store in zip(loads, stores):
        load.wait()
        store.start()
    code = low(dot_t(attended[...], out_in[...]))
    code_out[...] = code
    mine = pl.ds(pl.multiple_of(side * half, half), half)
    theirs = pl.ds(pl.multiple_of((1 - side) * half, half), half)
    sent[...] = low(dot(attended[theirs, :], out_w[...]) + dot(code_out[theirs, :], out_out[...]))
    swap_attn = pltpu.make_async_remote_copy(
        src_ref=sent, dst_ref=got, send_sem=swap_send.at[0], recv_sem=swap_recv.at[0],
        device_id=partner, device_id_type=MESH,
    )
    swap_attn.start()
    attn_proj[...] = dot(attended[mine, :], out_w[...]) + dot(code_out[mine, :], out_out[...])

    relay(group(0))
    for store in stores:
        store.wait()
    swap_attn.wait()
    rows = 64

    def combine(i, carry):
        at = pl.ds(pl.multiple_of(i * rows, rows), rows)
        proj = attn_proj[at, :] + wide(got[at, :])
        attn_proj[at, :] = proj
        token = wide(tokens[at, :])
        normed = token * inverse_rms(token) * gain_in[...]
        mid = low(dot_t(low(normed), left[...]))
        laurel_mid[at, :] = mid
        end = dot(mid, right_w[...])
        comb = (
            token + proj * inverse_rms(proj) * gain_attn[...] + normed + end * inverse_rms(end) * gain_laurel[...]
        ) * ROOT_HALF
        combined[at, :] = comb
        ffn[at, :] = low(comb * inverse_rms(comb) * gain_pre[...])
        return carry

    lax.fori_loop(0, half // rows, combine, 0)
    swaps = []
    for k in range(2):
        swaps.append(
            pltpu.make_async_remote_copy(
                src_ref=ffn.at[pl.ds(k * quarter, quarter), :], dst_ref=ffn.at[pl.ds(half + k * quarter, quarter), :],
                send_sem=swap_send.at[1 + k], recv_sem=swap_recv.at[1 + k],
                device_id=partner, device_id_type=MESH,
            )
        )
        swaps[k].start()
    total[...] = jnp.zeros_like(total)
    codes[...] = jnp.zeros_like(codes)

    def keeps(g, slot):
        at = pl.ds(pl.multiple_of(g * block, block), block)
        return (
            pltpu.make_async_copy(gate_keep.at[slot], gate_out.at[:, at], keep_sem.at[0, slot]),
            pltpu.make_async_copy(up_keep.at[slot], up_out.at[:, at], keep_sem.at[1, slot]),
        )

    def weights(g):
        at = pl.ds(pl.multiple_of(g * block, block), block)
        return (
            pltpu.make_async_copy(full_gate.at[:, at], gate_w, weight_sem.at[0]),
            pltpu.make_async_copy(full_up.at[:, at], up_w, weight_sem.at[1]),
            pltpu.make_async_copy(full_down.at[at, :], down_w, weight_sem.at[2]),
        )

    def climb(g):
        at = pl.ds(pl.multiple_of(g * block, block), block)
        slot = lax.rem(g, 2)

        @pl.when(g >= 2)
        def _():
            for keep in keeps(g - 2, slot):
                keep.wait()

        ready = weights(g)
        ready[0].wait()
        gate = dot(ffn[...], gate_w[...]) + dot(code_ffn[:, :rank], gu_out[0, :, at])
        gate_keep[slot] = low(gate)
        act = gelu_parts(gate)[0]
        ready[1].wait()
        up = dot(ffn[...], up_w[...]) + dot(code_ffn[:, rank:], gu_out[1, :, at])
        up_keep[slot] = low(up)
        hidden[...] = low(act * up)
        for keep in keeps(g, slot):
            keep.start()

    def descend(g):
        at = pl.ds(pl.multiple_of(g * block, block), block)
        weights(g)[2].wait()
        codes[...] += dot_t(hidden[...], down_in[:, at])
        total[...] += dot(hidden[...], down_w[...])

    def round_(g, carry):
        more = g + 1 < groups

        @pl.when(more)
        def _():
            relay(group(g + 1), 1, 1)

        @pl.when(g + 2 < groups)
        def _():
            begin(group(g + 2))

        spread(group(g))

        @pl.when(g >= 1)
        def _():
            descend(g - 1)

        @pl.when(more)
        def _():
            relay(group(g + 1), 2, 2)

        finish(group(g))
        for load in weights(g):
            load.start()

        @pl.when(more)
        def _():
            relay(group(g + 1), 3)

        @pl.when(g == 0)
        def _():
            for swap_ffn in swaps:
                swap_ffn.wait()
            pltpu.make_async_copy(ffn, ffn_out, ffn_sem).start()
            code_ffn[...] = low(dot_t(ffn[...], ffn_in[...]))

        climb(g)
        return carry

    lax.fori_loop(0, groups, round_, 0)
    descend(groups - 1)
    code_down[...] = low(codes[...])
    part[...] = low(total[...] + dot(code_down[...], down_out[...]))
    for g in (groups - 2, groups - 1):
        for keep in keeps(g, g % 2):
            keep.wait()
    pltpu.make_async_copy(ffn, ffn_out, ffn_sem).wait()

    def flush_group(g, carry):
        flush(group(g))
        return carry

    lax.fori_loop(0, groups, flush_group, 0)


def fore(
    weights, out_w, right_w, attended, tokens, left, out_in, out_out, ffn_in, gu_out, down_in, down_out, gains, shards
):
    count = attended.shape[0]
    width = tokens.shape[1]
    hidden = weights[0].shape[1]
    half = count // 2
    rank = out_in.shape[0]
    block = min(512, hidden)
    groups = hidden // block
    bf16, f32 = jnp.bfloat16, jnp.float32
    anywhere, vmem = pl.BlockSpec(memory_space=pl.ANY), pl.BlockSpec(memory_space=pltpu.VMEM)
    shape = jax.ShapeDtypeStruct
    return pl.pallas_call(
        functools.partial(fore_kernel, shards, block),
        out_shape=full_shapes(weights, FORE_AXES, shards)
        + [
            shape((count, hidden), bf16),
            shape((count, hidden), bf16),
            shape((count, width), bf16),
            shape((half, width), f32),
            shape((half, width), f32),
            shape((half, left.shape[0]), bf16),
            shape((count, rank), bf16),
            shape((count, 2 * rank), bf16),
            shape((count, rank), bf16),
            shape((count, width), bf16),
        ],
        in_specs=[anywhere] * 3 + [vmem] * 15,
        out_specs=[anywhere] * 6 + [vmem] * 7,
        scratch_shapes=[
            *[pltpu.VMEM(w.shape, bf16) for w in weights],
            pltpu.VMEM((width, block), bf16),
            pltpu.VMEM((width, block), bf16),
            pltpu.VMEM((block, width), bf16),
            pltpu.VMEM((half, width), bf16),
            pltpu.VMEM((half, width), bf16),
            pltpu.VMEM((count, width), bf16),
            pltpu.VMEM((count, width), f32),
            pltpu.VMEM((count, rank), f32),
            pltpu.VMEM((count, block), bf16),
            pltpu.VMEM((2, count, block), bf16),
            pltpu.VMEM((2, count, block), bf16),
            pltpu.SemaphoreType.DMA((3,)),
            pltpu.SemaphoreType.DMA((3,)),
            pltpu.SemaphoreType.DMA((3,)),
            pltpu.SemaphoreType.DMA((2, 2)),
            pltpu.SemaphoreType.DMA,
            pltpu.SemaphoreType.DMA((3,)),
            pltpu.SemaphoreType.DMA((3,)),
        ]
        + mover_semaphores(3 * groups, shards),
        compiler_params=pltpu.CompilerParams(
            collective_id=1, has_side_effects=True, vmem_limit_bytes=60 * 2**20
        ),
    )(*weights, out_w, right_w, attended, tokens, left, out_in, out_out, ffn_in, gu_out, down_in, down_out, *gains)


def body(
    tokens,
    layer_input,
    segments,
    adapter_ids,
    cotangent,
    w_query,
    w_key,
    w_value,
    w_output,
    w_gate,
    w_up,
    w_down,
    laurel_left,
    laurel_right,
    input_gate,
    input_proj,
    gain_in,
    gain_attn,
    gain_laurel,
    gain_pre,
    gain_post,
    gain_layer,
    gain_query,
    gain_key,
    adapt_attn_in,
    adapt_query_out,
    adapt_kv_out,
    adapt_out_in,
    adapt_out_out,
    adapt_ffn_in,
    adapt_gu_out,
    adapt_down_in,
    adapt_down_out,
):
    seq_count, count, width = tokens.shape
    assert seq_count == 1 and lax.axis_size("tensor") == 2 and lax.axis_size("context") == 4
    half = count // 2
    head_size = gain_query.shape[0]
    rank = adapt_query_out.shape[1]
    heads = adapt_query_out.shape[2] // head_size
    kv_heads = adapt_kv_out.shape[3] // head_size
    assert kv_heads == 1
    side = lax.axis_index("tensor")
    place = lax.axis_index("context")
    shards = lax.axis_size("shard")

    hidden_here = w_gate.shape[1]
    chosen = adapter_ids[0]

    def turned(table):
        return table.transpose(0, 2, 1)

    (
        pick_attn_in, pick_query_out, pick_kv_out, pick_out_in, pick_out_out, pick_ffn_in, pick_gu_out,
        pick_down_in, pick_down_out, tokens_own, per_layer_own, cotangent_own,
    ) = pick_rows(
        chosen, side,
        [
            turned(adapt_attn_in), adapt_query_out, adapt_kv_out, turned(adapt_out_in), adapt_out_out,
            turned(adapt_ffn_in), adapt_gu_out, turned(adapt_down_in), adapt_down_out,
        ],
        [tokens[0], layer_input[0], cotangent[0]],
    )

    start_pos = place * count
    seg_all = segments[0]
    seg_query = lax.dynamic_slice_in_dim(seg_all, start_pos, count, 0)
    before = jnp.sum((seg_all[None, :] < seg_query[:, None]).astype(jnp.int32), axis=1)
    own_pos = start_pos + jnp.arange(count, dtype=jnp.int32) - before
    cosine, sine_table = rope_tables(own_pos, head_size)
    seg_prior = lax.dynamic_slice_in_dim(seg_all, jnp.maximum(start_pos - count, 0), count, 0)
    seg_cols = jnp.concatenate([jnp.where(place > 0, seg_prior, -1), seg_query])[None, :]
    seg_rows = seg_query[:, None]
    score_scale = 1.0 / math.sqrt(head_size)
    (
        full_query, full_key, full_value, full_left, full_output, full_right, full_layer_gate, full_layer_proj, normed_b,
        code_attn, lin, lin_kv, query_rot, kv_own, kv_prior, attended_b, log_total,
    ) = front(
        (w_query, w_key, w_value, laurel_left.T, w_output, laurel_right, input_gate, input_proj),
        (
            tokens[0], pick_attn_in, pick_query_out, pick_kv_out, cosine, sine_table, seg_rows, seg_cols,
            gain_in[None], gain_query[None], gain_key[None],
        ),
        shards,
    )
    (
        full_gate, full_up, full_down,
        gate_b, up_b, ffn_b, attn_proj, combined, laurel_mid, code_out, code_ffn, code_down, down_part,
    ) = fore(
        (w_gate, w_up, w_down), full_output, full_right,
        attended_b, tokens_own, full_left,
        pick_out_in, pick_out_out, pick_ffn_in, pick_gu_out, pick_down_in, pick_down_out,
        (gain_in[None], gain_attn[None], gain_laurel[None], gain_pre[None]), shards,
    )
    mark = jnp.where(
        (lax.broadcasted_iota(jnp.int32, (rank, 512), 1) == chosen) & (place == 0), 1.0, 0.0
    )
    grad_attn_b, early, output_own, grad_inputs, grad_normed = aft(
        (full_gate, full_up, full_down), (gate_b, up_b),
        (
            down_part, combined, per_layer_own, cotangent_own, full_layer_gate, full_layer_proj,
            code_ffn, code_down, ffn_b, pick_down_in, pick_down_out, pick_gu_out, pick_ffn_in,
            attn_proj, laurel_mid, full_left, full_right, mark,
            gain_post[None], gain_layer[None], gain_pre[None], gain_attn[None], gain_laurel[None],
        ),
        shards,
    )
    output_other = swap(output_own)
    grad_query, sent_kv, own_kv, term_out_in, term_out_out = attend_back(
        grad_attn_b, full_output, pick_out_in, pick_out_out, code_out, attended_b, query_rot, kv_prior, kv_own,
        log_total, seg_rows, seg_cols, lin, cosine, sine_table, gain_query[None], score_scale,
    )
    input_grad, late = tail(
        (
            grad_query, full_query, full_key, full_value, code_attn, normed_b,
            pick_query_out, pick_kv_out, pick_attn_in, term_out_in, term_out_out,
            tokens_own, gain_in[None], grad_inputs, grad_normed,
            own_kv, shifted(sent_kv, "context", -1), lin_kv, cosine, sine_table, gain_key[None],
        ),
        shards,
    )
    (
        layer_output, table_attn_in, table_query_out, table_kv_out, table_out_in, table_out_out, table_ffn_in,
        table_gu_out, table_down_in, table_down_out,
    ) = tables(
        early, late, output_own, output_other, heads * head_size, kv_heads * head_size, adapt_attn_in.shape[0], hidden_here
    )
    return (
        layer_output[None], input_grad[None], turned(table_attn_in), table_query_out, table_kv_out,
        turned(table_out_in), table_out_out, turned(table_ffn_in), table_gu_out, turned(table_down_in), table_down_out,
    )


def solution(mesh):
    in_specs = (
        P("shard", "context", None),
        P("shard", "context", None),
        P("shard", None),
        P("shard"),
        P("shard", "context", None),
        P("shard", "tensor"),
        P("shard", "tensor"),
        P("shard", "tensor"),
        P("tensor", "shard"),
        P("shard", "tensor"),
        P("shard", "tensor"),
        P("tensor", "shard"),
        P("shard", None),
        P(None, "shard"),
        P("shard", None),
        P(None, "shard"),
        P(),
        P(),
        P(),
        P(),
        P(),
        P(),
        P(),
        P(),
        P(),
        P(None, None, "tensor"),
        P(None, None, None, "tensor"),
        P(None, "tensor", None),
        P(),
        P(),
        P(None, None, None, "tensor"),
        P(None, "tensor", None),
        P(),
    )
    out_specs = (
        P("shard", "context", None),
        P("shard", "context", None),
        P(),
        P(),
        P(),
        P(),
        P(),
        P(),
        P(),
        P(),
        P(),
    )
    return jax.shard_map(body, mesh=mesh, in_specs=in_specs, out_specs=out_specs, check_vma=False)
```
